32 devices in a mesh: grp: 2 (over core), row: 16 (over z, y, x).
Axes of the slice: x: 2, y: 2, z: 4, core: 2. Of those that a mesh axis runs over, the one named last changes fastest.
Arguments:
- pair_in: bfloat16 [2, 2, 384, 384, 128], P('grp', None, 'row'), may hold values from -6 to 6
- crop_lengths: int32 [2], replicated, may hold values from 192 to 384, as said below
- in_gain: float32 [2, 128], P('grp'), may hold values from 0.5 to 1.5
- in_bias: float32 [2, 128], P('grp'), may hold values from -3 to 3
- w_proj: bfloat16 [2, 128, 512], P('grp'), may hold values from -0.5 to 0.5
- w_gate: bfloat16 [2, 128, 128], P('grp'), may hold values from -0.5 to 0.5
- w_out: bfloat16 [2, 128, 128], P('grp'), may hold values from -0.5 to 0.5
- out_gain: float32 [2, 128], P('grp'), may hold values from 0.5 to 1.5
- out_bias: float32 [2, 128], P('grp'), may hold values from -3 to 3
- trans_gain: float32 [2, 128], P('grp'), may hold values from 0.5 to 1.5
- trans_bias: float32 [2, 128], P('grp'), may hold values from -3 to 3
- w_up: bfloat16 [2, 128, 512], P('grp'), may hold values from -0.5 to 0.5
- w_down: bfloat16 [2, 512, 128], P('grp'), may hold values from -0.5 to 0.5
- pair_cot: bfloat16 [2, 2, 384, 384, 128], P('grp', None, 'row'), may hold values from -6 to 6
Outputs:
- pair_out: bfloat16 [2, 2, 384, 384, 128], P('grp', None, 'row')
- pair_grad: float32 [2, 2, 384, 384, 128], P('grp', None, 'row')
- in_gain_grad: float32 [2, 128], P('grp')
- in_bias_grad: float32 [2, 128], P('grp')
- proj_grad: float32 [2, 128, 512], P('grp')
- gate_grad: float32 [2, 128, 128], P('grp')
- out_weight_grad: float32 [2, 128, 128], P('grp')
- out_gain_grad: float32 [2, 128], P('grp')
- out_bias_grad: float32 [2, 128], P('grp')
- trans_gain_grad: float32 [2, 128], P('grp')
- trans_bias_grad: float32 [2, 128], P('grp')
- up_grad: float32 [2, 128, 512], P('grp')
- down_grad: float32 [2, 512, 128], P('grp')
The draws below stay inside these ranges and needn't reach their ends.
Inputs may be any that keep to these rules, and one draw needn't show every extreme that they name: `crop_lengths`: one crop, drawn from the seed, has all 384 residues; positions from a crop's length on are padding.
All inputs are finite; a program needn't handle non-finite values.
Results may differ from the reference program's by a relative error of at most 0.013.
Values may be sent and summed in bfloat16 or wider, within the bound.
No kernel may reach another device: no remote copies, remote signals or barrier semaphores. Data moves between devices by JAX's collectives and lax.ppermute only.
A program may use at most 768 MiB of HBM per device.

```python
import jax
import jax.numpy as jnp
from jax import lax

C = 128
CT = 128
L = 384
CROPS = 2


def draw_crop_lengths(key, part):
    key = jax.random.fold_in(key, 11)
    lengths = jax.random.randint(jax.random.fold_in(key, 1), (CROPS,), L // 2, L + 1)
    longest = jax.random.randint(jax.random.fold_in(key, 2), (), 0, CROPS)
    return jnp.where(jnp.arange(CROPS) == longest, L, lengths).astype(jnp.int32)


def levels(key, dims, cuts, smallest, top_value):
    factor_of, own = 1.0, jax.random.fold_in(key, 6)
    for dim, shards_of in cuts:
        steps = jnp.exp(jax.random.uniform(jax.random.fold_in(own, dim), (shards_of,), jnp.float32, smallest / len(cuts), top_value / len(cuts)))
        factor_of = factor_of * jnp.repeat(steps, dims[dim] // shards_of).reshape([-1 if axis == dim else 1 for axis in range(len(dims))])
    return factor_of


def scatter_about(rng, dims, scale, most, split=(), kind=jnp.bfloat16):
    loudness = levels(rng, dims, split, -0.22, 0.18) if split else 1.0
    array = jax.random.normal(rng, dims, jnp.float32) * scale * loudness
    return jnp.minimum(jnp.maximum(array, -most), most).astype(kind)


def setup_inputs(seed: int = 0) -> dict:
    seeds = jax.random.split(jax.random.key(seed), 15)
    pair_in = scatter_about(seeds[0], (2, CROPS, L, L, C), 1.0, 6.0, ((0, 2), (2, 16)))
    crop_lengths = draw_crop_lengths(jax.random.fold_in(seeds[14], 71), 0)
    in_gain = jnp.clip(1.0 + 0.1 * jax.random.normal(seeds[2], (2, C), jnp.float32), 0.5, 1.5)
    in_bias = scatter_about(seeds[3], (2, C), 0.5, 3.0, ((0, 2),), jnp.float32)
    w_proj = scatter_about(seeds[4], (2, C, 4 * CT), C ** -0.5, 0.5, ((0, 2),))
    w_gate = scatter_about(seeds[5], (2, C, C), C ** -0.5, 0.5, ((0, 2),))
    w_out = scatter_about(seeds[6], (2, CT, C), CT ** -0.5, 0.5, ((0, 2),))
    out_gain = jnp.clip(1.0 + 0.1 * jax.random.normal(seeds[7], (2, CT), jnp.float32), 0.5, 1.5)
    out_bias = scatter_about(seeds[8], (2, CT), 0.5, 3.0, ((0, 2),), jnp.float32)
    trans_gain = jnp.clip(1.0 + 0.1 * jax.random.normal(seeds[9], (2, C), jnp.float32), 0.5, 1.5)
    trans_bias = scatter_about(seeds[10], (2, C), 0.5, 3.0, ((0, 2),), jnp.float32)
    w_up = scatter_about(seeds[11], (2, C, 4 * C), C ** -0.5, 0.5, ((0, 2),))
    w_down = scatter_about(seeds[12], (2, 4 * C, C), C ** -0.5, 0.5, ((0, 2),))
    pair_cot = scatter_about(seeds[13], (2, CROPS, L, L, C), 1.0, 6.0, ((0, 2), (2, 16)))
    return dict(pair_in=pair_in, crop_lengths=crop_lengths, in_gain=in_gain, in_bias=in_bias, w_proj=w_proj, w_gate=w_gate, w_out=w_out, out_gain=out_gain, out_bias=out_bias, trans_gain=trans_gain, trans_bias=trans_bias, w_up=w_up, w_down=w_down, pair_cot=pair_cot)


@jax.custom_vjp
def low(v):
    return lax.optimization_barrier(v.astype(jnp.bfloat16)).astype(jnp.float32)

@jax.custom_vjp
def low_back(v):
    return v

def low_keep(v):
    return (low(v), None)

def low_pass(kept, grad):
    return (grad,)

def back_keep(v):
    return (v, None)

def back_low(kept, grad):
    return (low(grad),)
low.defvjp(low_keep, low_pass)
low_back.defvjp(back_keep, back_low)
EPSILON = 1e-05

def layer_norm(values, gain, offset):
    mean_value = lax.optimization_barrier(jnp.mean(values, axis=-1, keepdims=True))
    centred = values - mean_value
    variance = lax.optimization_barrier(jnp.mean(centred * centred, axis=-1, keepdims=True))
    return centred * lax.rsqrt(variance + EPSILON) * gain + offset

def triangle_block(pair_state, residues, gain_in, bias_in, proj_weight, gate_weight, out_weight, gain_out, bias_out, gain_trans, bias_trans, up_weight, down_weight):
    hidden_width = out_weight.shape[0]
    normed = low(layer_norm(pair_state, gain_in, bias_in))
    projected = low_back(jnp.dot(normed, proj_weight, precision=lax.Precision.HIGHEST))
    gate_logit = low_back(jnp.dot(normed, gate_weight, precision=lax.Precision.HIGHEST))
    pair_mask = (residues[:, None] * residues[None, :])[:, :, None]
    left_value = projected[..., :hidden_width]
    left_logit = projected[..., hidden_width:2 * hidden_width]
    right_value = projected[..., 2 * hidden_width:3 * hidden_width]
    right_logit = projected[..., 3 * hidden_width:]
    left_factor = low_back(low(jax.nn.sigmoid(left_logit) * left_value * pair_mask))
    right_factor = low_back(low(jax.nn.sigmoid(right_logit) * right_value * pair_mask))
    mixed_sum = low_back(jnp.einsum('ikc,jkc->ijc', left_factor, right_factor, precision=lax.Precision.HIGHEST))
    mixed_norm = low(layer_norm(mixed_sum, gain_out, bias_out))
    update = low_back(jnp.dot(mixed_norm, out_weight, precision=lax.Precision.HIGHEST))
    first_state = pair_state + jax.nn.sigmoid(gate_logit) * update
    trans_normed = low(layer_norm(first_state, gain_trans, bias_trans))
    hidden = low_back(jnp.dot(trans_normed, up_weight, precision=lax.Precision.HIGHEST))
    activated = low(jax.nn.silu(hidden))
    trans_out = low_back(jnp.dot(activated, down_weight, precision=lax.Precision.HIGHEST))
    return first_state + trans_out

def forward(pair_value, gain_in, bias_in, proj_weight, gate_weight, out_weight, gain_out, bias_out, gain_trans, bias_trans, up_weight, down_weight, residues):
    branch_list = []
    main_list = []
    for crop_index in range(CROPS):
        branch_out = triangle_block(pair_value[0, crop_index], residues[crop_index], gain_in[0], bias_in[0], proj_weight[0], gate_weight[0], out_weight[0], gain_out[0], bias_out[0], gain_trans[0], bias_trans[0], up_weight[0], down_weight[0])
        passed = low_back(low(branch_out))
        main_out = triangle_block(passed + pair_value[1, crop_index], residues[crop_index], gain_in[1], bias_in[1], proj_weight[1], gate_weight[1], out_weight[1], gain_out[1], bias_out[1], gain_trans[1], bias_trans[1], up_weight[1], down_weight[1])
        branch_list.append(branch_out)
        main_list.append(main_out)
    return jnp.stack([jnp.stack(branch_list), jnp.stack(main_list)])

def reference(pair_in, crop_lengths, in_gain, in_bias, w_proj, w_gate, w_out, out_gain, out_bias, trans_gain, trans_bias, w_up, w_down, pair_cot):
    residues = (jnp.arange(L)[None, :] < crop_lengths[:, None]).astype(jnp.float32)

    def closed(pair_value, gain_in, bias_in, proj_weight, gate_weight, out_weight, gain_out, bias_out, gain_trans, bias_trans, up_weight, down_weight):
        return forward(pair_value, gain_in, bias_in, proj_weight, gate_weight, out_weight, gain_out, bias_out, gain_trans, bias_trans, up_weight, down_weight, residues)
    pair_out, pullback = jax.vjp(closed, pair_in.astype(jnp.float32), in_gain.astype(jnp.float32), in_bias.astype(jnp.float32), w_proj.astype(jnp.float32), w_gate.astype(jnp.float32), w_out.astype(jnp.float32), out_gain.astype(jnp.float32), out_bias.astype(jnp.float32), trans_gain.astype(jnp.float32), trans_bias.astype(jnp.float32), w_up.astype(jnp.float32), w_down.astype(jnp.float32))
    gradients = pullback(pair_cot.astype(jnp.float32))
    return (pair_out.astype(jnp.bfloat16), gradients[0], gradients[1], gradients[2], gradients[3], gradients[4], gradients[5], gradients[6], gradients[7], gradients[8], gradients[9], gradients[10], gradients[11])
```

```python
import jax
import jax.numpy as jnp
from jax import lax
from jax.sharding import PartitionSpec as P

EPSILON = 1e-05
F32 = jnp.float32
BF16 = jnp.bfloat16


def norm_stats(values):
    mean_value = jnp.mean(values, axis=-1, keepdims=True)
    centred = values - mean_value
    inv_scale = lax.rsqrt(jnp.mean(centred * centred, axis=-1, keepdims=True) + EPSILON)
    return (centred * inv_scale, inv_scale)


def norm_back(grad_scaled, scaled, inv_scale):
    mean_grad = jnp.mean(grad_scaled, axis=-1, keepdims=True)
    mean_cross = jnp.mean(grad_scaled * scaled, axis=-1, keepdims=True)
    return inv_scale * (grad_scaled - mean_grad - scaled * mean_cross)


def dot(a, b):
    return jnp.dot(a, b, preferred_element_type=F32)


def dot_t(a, b):
    return jnp.einsum("ijf,cf->ijc", a, b, preferred_element_type=F32)


def outer(a, b):
    return jnp.einsum("ijc,ijf->cf", a, b, preferred_element_type=F32)


def to_channels(value, n):
    rows, cols, channels = value.shape
    return jnp.transpose(value, (2, 0, 1)).reshape(n, channels // n, rows, cols)


def from_channels(value):
    n, held, rows, cols = value.shape
    return jnp.transpose(value.reshape(n * held, rows, cols), (1, 2, 0))


def swap_rows(value):
    return lax.all_to_all(value, "row", 0, 0)


def pre(state, mask, w):
    scaled, _ = norm_stats(state)
    normed = (scaled * w["gain_in"] + w["bias_in"]).astype(BF16)
    projected = dot(normed, w["proj"])
    width = projected.shape[-1] // 4
    lv, lg, rv, rg = (projected[..., i * width : (i + 1) * width] for i in range(4))
    left = (jax.nn.sigmoid(lg) * lv * mask).astype(BF16)
    right = (jax.nn.sigmoid(rg) * rv * mask).astype(BF16)
    return normed, left, right


def post(state, normed, mixed, w):
    gate_logit = dot(normed, w["gate"])
    scaled_mid, inv_mid = norm_stats(mixed)
    mixed_norm = (scaled_mid * w["gain_out"] + w["bias_out"]).astype(BF16)
    update = dot(mixed_norm, w["out"])
    gate_sigma = jax.nn.sigmoid(gate_logit)
    first_state = state + gate_sigma * update
    scaled_tr, inv_tr = norm_stats(first_state)
    trans_normed = (scaled_tr * w["gain_tr"] + w["bias_tr"]).astype(BF16)
    hidden = dot(trans_normed, w["up"])
    activated = jax.nn.silu(hidden).astype(BF16)
    result = (first_state + dot(activated, w["down"])).astype(BF16)
    saved = (gate_sigma, scaled_mid, inv_mid, mixed_norm, update, scaled_tr, inv_tr, trans_normed, hidden, activated)
    return result, saved


def back_upper(grad_final, saved, w):
    gate_sigma, scaled_mid, inv_mid, mixed_norm, update, scaled_tr, inv_tr, trans_normed, hidden, activated = saved
    grads = {}
    grad_trans = grad_final.astype(BF16)
    grads["down"] = outer(activated, grad_trans)
    grad_act = dot_t(grad_trans, w["down"])
    sigma = jax.nn.sigmoid(hidden)
    grad_hidden = (grad_act * sigma * (1.0 + hidden * (1.0 - sigma))).astype(BF16)
    grads["up"] = outer(trans_normed, grad_hidden)
    grad_tnorm = dot_t(grad_hidden, w["up"])
    grads["gain_tr"] = jnp.sum(grad_tnorm * scaled_tr, axis=(0, 1))
    grads["bias_tr"] = jnp.sum(grad_tnorm, axis=(0, 1))
    grad_result = grad_final + norm_back(grad_tnorm * w["gain_tr"], scaled_tr, inv_tr)
    grad_update = (grad_result * gate_sigma).astype(BF16)
    grad_gate = (grad_result * update * gate_sigma * (1.0 - gate_sigma)).astype(BF16)
    grads["out"] = outer(mixed_norm, grad_update)
    grad_norm_mid = dot_t(grad_update, w["out"])
    grads["gain_out"] = jnp.sum(grad_norm_mid * scaled_mid, axis=(0, 1))
    grads["bias_out"] = jnp.sum(grad_norm_mid, axis=(0, 1))
    grad_mixed = norm_back(grad_norm_mid * w["gain_out"], scaled_mid, inv_mid).astype(BF16)
    return grad_result, grad_gate, grad_mixed, grads


def back_lower(state, normed, mask, grad_result, grad_gate, grad_left, grad_right, w):
    scaled_in, inv_in = norm_stats(state)
    projected = dot(normed, w["proj"])
    width = projected.shape[-1] // 4
    lv, lg, rv, rg = (projected[..., i * width : (i + 1) * width] for i in range(4))
    ls = jax.nn.sigmoid(lg)
    rs = jax.nn.sigmoid(rg)
    gl = grad_left.astype(F32) * mask
    gr = grad_right.astype(F32) * mask
    grad_proj = jnp.concatenate(
        [gl * ls, gl * lv * ls * (1.0 - ls), gr * rs, gr * rv * rs * (1.0 - rs)], axis=-1
    ).astype(BF16)
    grads = {"proj": outer(normed, grad_proj), "gate": outer(normed, grad_gate)}
    grad_normed = dot_t(grad_proj, w["proj"]) + dot_t(grad_gate, w["gate"])
    grads["gain_in"] = jnp.sum(grad_normed * scaled_in, axis=(0, 1))
    grads["bias_in"] = jnp.sum(grad_normed, axis=(0, 1))
    return grad_result + norm_back(grad_normed * w["gain_in"], scaled_in, inv_in), grads


def product(left, right):
    n, held, rows, cols = left.shape
    mixed = jnp.einsum("atik,btjk->taibj", left, right, preferred_element_type=F32)
    return jnp.transpose(mixed.reshape(held, n, rows, n * rows), (1, 0, 2, 3)).astype(BF16)


def product_back(grad_mixed, left, right):
    n, held, rows, cols = left.shape
    split = grad_mixed.reshape(n, held, rows, n, rows)
    grad_left = jnp.einsum("atibj,btjk->atik", split, right, preferred_element_type=F32)
    grad_right = jnp.einsum("atibj,atik->btjk", split, left, preferred_element_type=F32)
    return grad_left.astype(BF16), grad_right.astype(BF16)


ORDER = ("gain_in", "bias_in", "proj", "gate", "out", "gain_out", "bias_out", "gain_tr", "bias_tr", "up", "down")


def per_device(pair_in, crop_lengths, gain_in, bias_in, proj, gate, out, gain_out, bias_out, gain_tr, bias_tr, up, down, pair_cot):
    own_weights = dict(
        gain_in=gain_in[0], bias_in=bias_in[0], proj=proj[0], gate=gate[0], out=out[0], gain_out=gain_out[0],
        bias_out=bias_out[0], gain_tr=gain_tr[0], bias_tr=bias_tr[0], up=up[0], down=down[0],
    )
    n = lax.axis_size("row")
    rows, cols = pair_in.shape[2], pair_in.shape[3]
    group = lax.axis_index("grp")
    first = group == 0
    swap = lambda v: lax.ppermute(v, "grp", [(0, 1), (1, 0)])
    pick = lambda v, i: lax.dynamic_index_in_dim(v, i, 0, keepdims=False)
    other_weights = {k: swap(v) for k, v in own_weights.items()}
    weights = [
        {k: jnp.where(first, own_weights[k], other_weights[k]) for k in ORDER},
        {k: jnp.where(first, other_weights[k], own_weights[k]) for k in ORDER},
    ]

    def both(value):
        own, got = pick(value, group), swap(pick(value, 1 - group))
        return jnp.where(first, own, got), jnp.where(first, got, own)

    def home(value_0, value_1):
        own, got = jnp.where(first, value_0, value_1), swap(jnp.where(first, value_1, value_0))
        return jnp.stack([jnp.where(first, own, got), jnp.where(first, got, own)])[None]

    pair_0, pair_1 = both(pair_in[0])
    cot_0, cot_1 = both(pair_cot[0])
    crop_length = pick(crop_lengths, group)
    own_rows = lax.axis_index("row") * rows + jnp.arange(rows)
    mask = (own_rows < crop_length).astype(F32)[:, None, None] * (jnp.arange(cols) < crop_length).astype(F32)[None, :, None]

    def send(*values):
        return swap_rows(jnp.stack([to_channels(v, n) for v in values], axis=1))

    w0, w1 = weights
    state_0 = pair_0.astype(F32)
    normed_0, left, right = pre(state_0, mask, w0)
    lr_0 = send(left, right)
    mixed_0 = from_channels(swap_rows(product(lr_0[:, 0], lr_0[:, 1]))).astype(F32)
    out_0, saved_0 = post(state_0, normed_0, mixed_0, w0)
    state_1 = out_0.astype(F32) + pair_1.astype(F32)
    normed_1, left, right = pre(state_1, mask, w1)
    lr_1 = send(left, right)
    mixed_1 = from_channels(swap_rows(product(lr_1[:, 0], lr_1[:, 1]))).astype(F32)
    out_1, saved_1 = post(state_1, normed_1, mixed_1, w1)
    pair_out = home(out_0, out_1)
    grad_result, grad_gate, grad_mixed, upper_1 = back_upper(cot_1.astype(F32), saved_1, w1)
    gm = send(grad_mixed)
    glr = swap_rows(jnp.stack(product_back(gm[:, 0], lr_1[:, 0], lr_1[:, 1]), axis=1))
    grad_1, lower_1 = back_lower(
        state_1, normed_1, mask, grad_result, grad_gate, from_channels(glr[:, 0]), from_channels(glr[:, 1]), w1
    )
    grad_final = cot_0.astype(F32) + grad_1.astype(BF16).astype(F32)
    grad_result, grad_gate, grad_mixed, upper_0 = back_upper(grad_final, saved_0, w0)
    gm = send(grad_mixed)
    glr = swap_rows(jnp.stack(product_back(gm[:, 0], lr_0[:, 0], lr_0[:, 1]), axis=1))
    grad_0, lower_0 = back_lower(
        state_0, normed_0, mask, grad_result, grad_gate, from_channels(glr[:, 0]), from_channels(glr[:, 1]), w0
    )
    pair_grad = home(grad_0, grad_1)
    grads_0, grads_1 = {**upper_0, **lower_0}, {**upper_1, **lower_1}
    mine = {k: jnp.where(first, grads_0[k], grads_1[k]) + swap(jnp.where(first, grads_1[k], grads_0[k])) for k in ORDER}
    summed = lax.psum(mine, "row")
    return (pair_out, pair_grad) + tuple(summed[k][None] for k in ORDER)


def solution(mesh):
    pair = P("grp", None, "row", None, None)
    vector, matrix = P("grp", None), P("grp", None, None)
    weights = (vector, vector, matrix, matrix, matrix, vector, vector, vector, vector, matrix, matrix)
    return jax.shard_map(
        per_device,
        mesh=mesh,
        in_specs=(pair, P()) + weights + (pair,),
        out_specs=(pair, pair) + weights,
        check_vma=False,
    )
```

```python
import functools

import jax
import jax.numpy as jnp
from jax import lax
from jax.experimental import pallas as pl
from jax.experimental.pallas import tpu as pltpu
from jax.sharding import PartitionSpec as P

EPSILON = 1e-05
F32 = jnp.float32
BF16 = jnp.bfloat16


def norm_stats(values):
    mean_value = jnp.mean(values, axis=-1, keepdims=True)
    centred = values - mean_value
    inv_scale = lax.rsqrt(jnp.mean(centred * centred, axis=-1, keepdims=True) + EPSILON)
    return (centred * inv_scale, inv_scale)


def norm_back(grad_scaled, scaled, inv_scale):
    mean_grad = jnp.mean(grad_scaled, axis=-1, keepdims=True)
    mean_cross = jnp.mean(grad_scaled * scaled, axis=-1, keepdims=True)
    return inv_scale * (grad_scaled - mean_grad - scaled * mean_cross)


def dot(a, b):
    return jnp.dot(a, b, preferred_element_type=F32)


def dot_t(a, b):
    return jnp.einsum("ijf,cf->ijc", a, b, preferred_element_type=F32)


def outer(a, b):
    return jnp.einsum("ijc,ijf->cf", a, b, preferred_element_type=F32)


def to_channels(value, n):
    rows, cols, channels = value.shape
    return jnp.transpose(value, (2, 0, 1)).reshape(n, channels // n, rows, cols)


def from_channels(value):
    n, held, rows, cols = value.shape
    return jnp.transpose(value.reshape(n * held, rows, cols), (1, 2, 0))


def swap_rows(value):
    return lax.all_to_all(value, "row", 0, 0)


def pre(state, mask, w):
    scaled, _ = norm_stats(state)
    normed = (scaled * w["gain_in"] + w["bias_in"]).astype(BF16)
    projected = dot(normed, w["proj"])
    width = projected.shape[-1] // 4
    lv, lg, rv, rg = (projected[..., i * width : (i + 1) * width] for i in range(4))
    left = (jax.nn.sigmoid(lg) * lv * mask).astype(BF16)
    right = (jax.nn.sigmoid(rg) * rv * mask).astype(BF16)
    return normed, left, right


def post(state, normed, mixed, w):
    gate_logit = dot(normed, w["gate"])
    scaled_mid, inv_mid = norm_stats(mixed)
    mixed_norm = (scaled_mid * w["gain_out"] + w["bias_out"]).astype(BF16)
    update = dot(mixed_norm, w["out"])
    gate_sigma = jax.nn.sigmoid(gate_logit)
    first_state = state + gate_sigma * update
    scaled_tr, inv_tr = norm_stats(first_state)
    trans_normed = (scaled_tr * w["gain_tr"] + w["bias_tr"]).astype(BF16)
    hidden = dot(trans_normed, w["up"])
    activated = jax.nn.silu(hidden).astype(BF16)
    result = (first_state + dot(activated, w["down"])).astype(BF16)
    saved = (gate_sigma, scaled_mid, inv_mid, mixed_norm, update, scaled_tr, inv_tr, trans_normed, hidden, activated)
    return result, saved


def back_upper(grad_final, saved, w):
    gate_sigma, scaled_mid, inv_mid, mixed_norm, update, scaled_tr, inv_tr, trans_normed, hidden, activated = saved
    grads = {}
    grad_trans = grad_final.astype(BF16)
    grads["down"] = outer(activated, grad_trans)
    grad_act = dot_t(grad_trans, w["down"])
    sigma = jax.nn.sigmoid(hidden)
    grad_hidden = (grad_act * sigma * (1.0 + hidden * (1.0 - sigma))).astype(BF16)
    grads["up"] = outer(trans_normed, grad_hidden)
    grad_tnorm = dot_t(grad_hidden, w["up"])
    grads["gain_tr"] = jnp.sum(grad_tnorm * scaled_tr, axis=(0, 1))
    grads["bias_tr"] = jnp.sum(grad_tnorm, axis=(0, 1))
    grad_result = grad_final + norm_back(grad_tnorm * w["gain_tr"], scaled_tr, inv_tr)
    grad_update = (grad_result * gate_sigma).astype(BF16)
    grad_gate = (grad_result * update * gate_sigma * (1.0 - gate_sigma)).astype(BF16)
    grads["out"] = outer(mixed_norm, grad_update)
    grad_norm_mid = dot_t(grad_update, w["out"])
    grads["gain_out"] = jnp.sum(grad_norm_mid * scaled_mid, axis=(0, 1))
    grads["bias_out"] = jnp.sum(grad_norm_mid, axis=(0, 1))
    grad_mixed = norm_back(grad_norm_mid * w["gain_out"], scaled_mid, inv_mid).astype(BF16)
    return grad_result, grad_gate, grad_mixed, grads


def back_lower(state, normed, mask, grad_result, grad_gate, grad_left, grad_right, w):
    scaled_in, inv_in = norm_stats(state)
    projected = dot(normed, w["proj"])
    width = projected.shape[-1] // 4
    lv, lg, rv, rg = (projected[..., i * width : (i + 1) * width] for i in range(4))
    ls = jax.nn.sigmoid(lg)
    rs = jax.nn.sigmoid(rg)
    gl = grad_left.astype(F32) * mask
    gr = grad_right.astype(F32) * mask
    grad_proj = jnp.concatenate(
        [gl * ls, gl * lv * ls * (1.0 - ls), gr * rs, gr * rv * rs * (1.0 - rs)], axis=-1
    ).astype(BF16)
    grads = {"proj": outer(normed, grad_proj), "gate": outer(normed, grad_gate)}
    grad_normed = dot_t(grad_proj, w["proj"]) + dot_t(grad_gate, w["gate"])
    grads["gain_in"] = jnp.sum(grad_normed * scaled_in, axis=(0, 1))
    grads["bias_in"] = jnp.sum(grad_normed, axis=(0, 1))
    return grad_result + norm_back(grad_normed * w["gain_in"], scaled_in, inv_in), grads


def product(left, right):
    n, held, rows, cols = left.shape
    mixed = jnp.einsum("atik,btjk->taibj", left, right, preferred_element_type=F32)
    return jnp.transpose(mixed.reshape(held, n, rows, n * rows), (1, 0, 2, 3)).astype(BF16)


def product_back(grad_mixed, left, right):
    n, held, rows, cols = left.shape
    split = grad_mixed.reshape(n, held, rows, n, rows)
    grad_left = jnp.einsum("atibj,btjk->atik", split, right, preferred_element_type=F32)
    grad_right = jnp.einsum("atibj,atik->btjk", split, left, preferred_element_type=F32)
    return grad_left.astype(BF16), grad_right.astype(BF16)


BLOCK_ROWS = 4
LANES = 128
VMEM = 56 << 20


def sig(x):
    return 0.5 * jnp.tanh(0.5 * x) + 0.5


def mm(a, b, ca=1, cb=0):
    return lax.dot_general(a, b, (((ca,), (cb,)), ((), ())), preferred_element_type=F32)


def col_stats(values):
    centred = values - jnp.mean(values, axis=0, keepdims=True)
    inv_scale = lax.rsqrt(jnp.mean(centred * centred, axis=0, keepdims=True) + EPSILON)
    return centred * inv_scale, inv_scale


def col_back(grad_scaled, scaled, inv_scale):
    mean_grad = jnp.mean(grad_scaled, axis=0, keepdims=True)
    mean_cross = jnp.mean(grad_scaled * scaled, axis=0, keepdims=True)
    return inv_scale * (grad_scaled - mean_grad - scaled * mean_cross)


def fold(values):
    return jnp.sum(values.reshape(values.shape[0] // 8, 8, values.shape[1]), axis=0)


class Step:
    def __init__(self, place, n, rows, held, block_rows, crop):
        self.n, self.rows, self.held, self.block = n, rows, held, block_rows
        self.row = pl.program_id(1) * block_rows
        self.length, self.base, self.group = place[crop], place[2], place[3]
        column = pl.program_id(0) * LANES + lax.broadcasted_iota(jnp.int32, (1, LANES), 1)
        self.columns = (column < self.length).astype(F32)

    def mask(self, r):
        return self.columns * jnp.where(self.base + self.row + r < self.length, 1.0, 0.0)

    def flat(self, ref):
        return ref[...].reshape(self.block * LANES, ref.shape[-1])

    def pick(self, pair, section):
        own, got = (self.flat(ref).astype(F32) for ref in pair)
        return jnp.where(jnp.full(own.shape, self.group) == section, own, got)

    def put(self, ref, value):
        ref[...] = value.reshape(self.block, LANES, value.shape[-1]).astype(ref.dtype)

    def lanes(self, r):
        return slice(r * LANES, (r + 1) * LANES)

    def spans(self, r):
        return [pl.ds((self.row + r) * self.held + t, self.n, stride=self.rows * self.held) for t in range(self.held)]

    def load(self, scratch, r):
        return jnp.concatenate([scratch[span, :] for span in self.spans(r)], axis=0)

    def store(self, scratch, r, value):
        for t, span in enumerate(self.spans(r)):
            scratch[span, :] = value[t * self.n : (t + 1) * self.n, :]


def unpack(ref, scratch, first=0):
    n, size = ref.shape[0], scratch.shape[0] // ref.shape[0]

    def body(d, carry):
        scratch[pl.ds(pl.multiple_of(d * size, 8), size), :] = ref[d, first : first + size, :].astype(F32)
        return carry

    lax.fori_loop(0, n, body, 0)


def pack(scratch, ref, first=0):
    n, size = ref.shape[0], scratch.shape[0] // ref.shape[0]

    def body(d, carry):
        ref[d, first : first + size, :] = scratch[pl.ds(pl.multiple_of(d * size, 8), size), :].astype(ref.dtype)
        return carry

    lax.fori_loop(0, n, body, 0)


def at_first(action):
    pl.when(pl.program_id(1) == 0)(action)


def at_last(action):
    pl.when(pl.program_id(1) == pl.num_programs(1) - 1)(action)


def clear(accs, olds, cols=()):
    @pl.when((pl.program_id(0) == 0) & (pl.program_id(1) == 0))
    def _():
        for k, ref in enumerate(accs):
            ref[...] = olds[k][...] if olds else jnp.zeros(ref.shape, ref.dtype)
        for ref in cols:
            ref[...] = jnp.zeros(ref.shape, ref.dtype)


def add_blocks(ref, first, value):
    for q in range(value.shape[1] // LANES):
        ref[first + q * LANES : first + (q + 1) * LANES, :] += value[:, q * LANES : (q + 1) * LANES]


def close_cols(ref, cols):
    @pl.when((pl.program_id(0) == pl.num_programs(0) - 1) & (pl.program_id(1) == pl.num_programs(1) - 1))
    def _():
        for k in range(2):
            row = UP_VEC + 16 + 8 * k
            ref[row : row + 1, :] += jnp.sum(jnp.transpose(cols[k]), axis=0, keepdims=True)


def pre_part(st, state, w, normed_ref, left_scr, right_scr):
    scaled, _ = norm_stats(state)
    normed = (scaled * w.vec[0:1, :] + w.vec[1:2, :]).astype(BF16)
    st.put(normed_ref, normed)
    projected = mm(w.proj_t[...], normed, 1, 1)
    for r in range(st.block):
        lv, lg, rv, rg = (projected[q * LANES : (q + 1) * LANES, st.lanes(r)] for q in range(4))
        mask = st.mask(r)
        st.store(left_scr, r, sig(lg) * lv * mask)
        st.store(right_scr, r, sig(rg) * rv * mask)


def post_part(st, state, normed, mixed_scr, w):
    mids = [col_stats(st.load(mixed_scr, r)) for r in range(st.block)]
    gain, bias = w.col[0], w.col[1]
    mixed_norm = jnp.concatenate([(scaled * gain + bias).astype(BF16) for scaled, _ in mids], axis=1)
    update = mm(mixed_norm, w.out[...], 0, 0)
    gate = sig(mm(normed, w.gate[...]))
    first_state = state + gate * update
    scaled_tr, inv_tr = norm_stats(first_state)
    trans = (scaled_tr * w.vec[2:3, :] + w.vec[3:4, :]).astype(BF16)
    hidden = mm(trans, w.up[...])
    sigma = sig(hidden)
    activated = (hidden * sigma).astype(BF16)
    return mids, mixed_norm, update, gate, first_state, scaled_tr, inv_tr, trans, hidden, sigma, activated


def upper_part(st, grad_final, kept, w, acc, cols, grad_ref, gate_ref, mixed_scr):
    mids, mixed_norm, update, gate, first_state, scaled_tr, inv_tr, trans, hidden, sigma, activated = kept
    low = grad_final.astype(BF16)
    add_blocks(acc, 0, mm(low, activated, 0, 0))
    grad_hidden = (mm(low, w.down[...], 1, 1) * (sigma * (1.0 + hidden * (1.0 - sigma)))).astype(BF16)
    add_blocks(acc, 4 * LANES, mm(trans, grad_hidden, 0, 0))
    grad_tnorm = mm(grad_hidden, w.up[...], 1, 1)
    acc[UP_VEC : UP_VEC + 8, :] += fold(grad_tnorm * scaled_tr)
    acc[UP_VEC + 8 : UP_VEC + 16, :] += fold(grad_tnorm)
    grad_result = grad_final + norm_back(grad_tnorm * w.vec[2:3, :], scaled_tr, inv_tr)
    st.put(grad_ref, grad_result)
    scaled_grad = grad_result * gate
    grad_update = scaled_grad.astype(BF16)
    st.put(gate_ref, scaled_grad * update * (1.0 - gate))
    add_blocks(acc, 8 * LANES, mm(mixed_norm, grad_update))
    grad_norm = mm(w.out[...], grad_update, 1, 1)
    for r, (scaled, inv_scale) in enumerate(mids):
        grad = grad_norm[:, st.lanes(r)]
        cols[0] += grad * scaled
        cols[1] += grad
        st.store(mixed_scr, r, col_back(grad * w.col[0], scaled, inv_scale) * st.mask(r))


def lower_part(st, state, normed, grad_result, grad_gate, left_scr, right_scr, w, acc):
    projected = mm(w.proj_t[...], normed, 1, 1)
    parts = []
    for r in range(st.block):
        lv, lg, rv, rg = (projected[q * LANES : (q + 1) * LANES, st.lanes(r)] for q in range(4))
        ls, rs = sig(lg), sig(rg)
        a, b = st.load(left_scr, r) * ls, st.load(right_scr, r) * rs
        parts.append(jnp.concatenate([v.astype(BF16) for v in (a, a * lv * (1.0 - ls), b, b * rv * (1.0 - rs))], axis=0))
    grad_proj = jnp.concatenate(parts, axis=1)
    acc[: 4 * LANES, :] += mm(grad_proj, normed)
    add_blocks(acc, 4 * LANES, mm(normed, grad_gate, 0, 0))
    grad_normed = jnp.transpose(mm(w.proj[...], grad_proj)) + mm(grad_gate, w.gate[...], 1, 1)
    scaled_in, inv_in = norm_stats(state)
    acc[LOW_VEC : LOW_VEC + 8, :] += fold(grad_normed * scaled_in)
    acc[LOW_VEC + 8 : LOW_VEC + 16, :] += fold(grad_normed)
    return grad_result + norm_back(grad_normed * w.vec[0:1, :], scaled_in, inv_in)


class Named:
    def __init__(self, names, refs):
        for name, ref in zip(names, refs):
            setattr(self, name, ref)


PRE = ("vec", "proj_t")
POST = ("vec", "col", "out", "gate", "up", "down")
LOWER = ("vec", "proj_t", "proj", "gate")
UP_VEC = 9 * LANES
UP_ROWS = UP_VEC + 32
LOW_VEC = 5 * LANES
LOW_ROWS = LOW_VEC + 16


def k_pre(cfg, place, own, got, *refs):
    st = Step(place, *cfg)
    w = Named(PRE, refs[:2])
    normed, both, left, right = refs[2:]
    pre_part(st, st.pick((own, got), 0), w, normed, left, right)

    @at_last
    def _():
        pack(left, both)
        pack(right, both, both.shape[1] // 2)


def k_post_pre(cfg, place, own_0, got_0, own_1, got_1, normed_in, mixed_in, *refs):
    st = Step(place, *cfg)
    w0, w1 = Named(POST, refs[:6]), Named(PRE, refs[6:8])
    out, normed, both, mixed, left, right = refs[8:]
    at_first(lambda: unpack(mixed_in, mixed))
    kept = post_part(st, st.pick((own_0, got_0), 0), st.flat(normed_in), mixed, w0)
    result = (kept[4] + mm(kept[-1], w0.down[...])).astype(BF16)
    st.put(out, result)
    pre_part(st, result.astype(F32) + st.pick((own_1, got_1), 1), w1, normed, left, right)

    @at_last
    def _():
        pack(left, both)
        pack(right, both, both.shape[1] // 2)


def k_post_upper(cfg, place, own, got, own_cot, got_cot, before, normed_in, mixed_in, *refs):
    st = Step(place, *cfg)
    w = Named(POST, refs[:6])
    *olds, out, grad, gate, grad_mixed, sums, mixed, cols = refs[6:]
    clear([sums], olds, [cols])
    at_first(lambda: unpack(mixed_in, mixed))
    state = st.flat(before).astype(F32) + st.pick((own, got), 1)
    kept = post_part(st, state, st.flat(normed_in), mixed, w)
    st.put(out, kept[4] + mm(kept[-1], w.down[...]))
    upper_part(st, st.pick((own_cot, got_cot), 1), kept, w, sums, cols, grad, gate, mixed)
    close_cols(sums, cols)
    at_last(lambda: pack(mixed, grad_mixed))


def k_lower_upper(
    cfg, place, own_1, got_1, own_0, got_0, own_cot, got_cot, before, normed_1, grad_1, gate_1, normed_0, both, mixed_in, *refs
):
    st = Step(place, *cfg)
    w1, w0 = Named(LOWER, refs[:4]), Named(POST, refs[4:10])
    *olds, pair_grad, grad, gate, grad_mixed, low_sums, up_sums, left, right, mixed, cols = refs[10:]
    clear([low_sums, up_sums], olds, [cols])

    @at_first
    def _():
        unpack(both, left)
        unpack(both, right, both.shape[1] // 2)
        unpack(mixed_in, mixed)

    state = st.flat(before).astype(F32) + st.pick((own_1, got_1), 1)
    grad_state = lower_part(
        st, state, st.flat(normed_1), st.flat(grad_1), st.flat(gate_1), left, right, w1, low_sums
    )
    st.put(pair_grad, grad_state)
    kept = post_part(st, st.pick((own_0, got_0), 0), st.flat(normed_0), mixed, w0)
    grad_final = st.pick((own_cot, got_cot), 0) + grad_state.astype(BF16).astype(F32)
    upper_part(st, grad_final, kept, w0, up_sums, cols, grad, gate, mixed)
    close_cols(up_sums, cols)
    at_last(lambda: pack(mixed, grad_mixed))


def k_lower(cfg, place, own, got, normed, grad, gate, both, *refs):
    st = Step(place, *cfg)
    w = Named(LOWER, refs[:4])
    *olds, pair_grad, sums, left, right = refs[4:]
    clear([sums], olds)

    @at_first
    def _():
        unpack(both, left)
        unpack(both, right, both.shape[1] // 2)

    state = st.pick((own, got), 0)
    grad_state = lower_part(
        st, state, st.flat(normed), st.flat(grad), st.flat(gate), left, right, w, sums
    )
    st.put(pair_grad, grad_state)


def spread(ref, scratch, first=0):
    n, size = ref.shape[0], scratch.shape[1] // ref.shape[0]

    def body(d, carry):
        for c in range(scratch.shape[0]):
            value = ref[d, first : first + size, c * LANES : (c + 1) * LANES]
            scratch[c, pl.ds(pl.multiple_of(d * size, 8), size), :] = value.astype(F32)
        return carry

    lax.fori_loop(0, n, body, 0)


def gather(scratch, ref, first=0):
    n, size = ref.shape[0], scratch.shape[1] // ref.shape[0]

    def body(d, carry):
        for c in range(scratch.shape[0]):
            value = scratch[c, pl.ds(pl.multiple_of(d * size, 8), size), :]
            ref[d, first : first + size, c * LANES : (c + 1) * LANES] = value.astype(ref.dtype)
        return carry

    lax.fori_loop(0, n, body, 0)


def channel(scratch, t, held):
    chunks, size, _ = scratch.shape
    span = pl.ds(t, size // held, stride=held)
    return jnp.concatenate([scratch[c, span, :].astype(BF16) for c in range(chunks)], axis=1)


def put_channel(scratch, t, held, value):
    chunks, size, _ = scratch.shape
    span = pl.ds(t, size // held, stride=held)
    for c in range(chunks):
        scratch[c, span, :] = value[:, c * LANES : (c + 1) * LANES]


def k_product(held, both, out, left, right):
    spread(both, left)
    spread(both, right, both.shape[1] // 2)

    def body(t, carry):
        put_channel(left, t, held, mm(channel(left, t, held), channel(right, t, held), 1, 1))
        return carry

    lax.fori_loop(0, held, body, 0)
    gather(left, out)


def k_product_back(held, grad_in, both, out, grad, left, right):
    spread(grad_in, grad)
    spread(both, left)
    spread(both, right, both.shape[1] // 2)

    def body(t, carry):
        low, lv, rv = channel(grad, t, held), channel(left, t, held), channel(right, t, held)
        put_channel(left, t, held, mm(low, rv))
        put_channel(right, t, held, mm(low, lv, 0, 0))
        return carry

    lax.fori_loop(0, held, body, 0)
    gather(left, out)
    gather(right, out, both.shape[1] // 2)


STEPS = """\
1A SA0 1B SB0 TA0 MA0 TB0 MB0 2A SA1 2B SB1 TA1 MA1 TB1 MB1 3A GA1 3B GB1 tA1 sA1 tB1 sB1 4A GA0 4B EB0 GB0 tA0 sA0 tB0 sB0 5A 5B
"""


class Kernels:
    def __init__(self, place, n, rows, cols, channels, block_rows):
        self.place = place
        self.n, self.rows, self.cols, self.channels, self.block = n, rows, cols, channels, block_rows
        self.held = channels // n
        self.size = rows * self.held
        self.chunks = cols // LANES

    def row_call(self, body, crop, ins, outs, scratch, micros, cols=0):
        rows, block = self.rows, self.block

        def spec(kind, shape):
            if kind == "own":
                return pl.BlockSpec(
                    (pl.squeezed, block, LANES, shape[-1]), lambda c, i, s: (crop, s[3] * (rows // block) + i, c, 0)
                )
            if kind == "rows":
                return pl.BlockSpec((block, LANES, shape[-1]), lambda c, i, s: (i, c, 0))
            if kind == "moved":
                return pl.BlockSpec(shape[:-1] + (LANES,), lambda c, i, s: (0, 0, c))
            zeros = (0,) * len(shape)
            return pl.BlockSpec(shape, lambda c, i, s: zeros)

        return pl.pallas_call(
            functools.partial(body, (self.n, rows, self.held, block, crop)),
            out_shape=tuple(v for _, v in outs),
            grid_spec=pltpu.PrefetchScalarGridSpec(
                num_scalar_prefetch=1,
                grid=(self.chunks, rows // block),
                in_specs=[spec(k, v.shape) for k, v in ins],
                out_specs=tuple(spec(k, v.shape) for k, v in outs),
                scratch_shapes=[pltpu.VMEM((self.channels * rows, LANES), F32)] * scratch
                + [pltpu.VMEM((2, self.channels, LANES), F32)] * cols,
            ),
            compiler_params=pltpu.CompilerParams(vmem_limit_bytes=VMEM),
            cost_estimate=cost(micros),
        )(self.place, *[v for _, v in ins])

    def pairs(self, dtype):
        return ("rows", jax.ShapeDtypeStruct((self.rows, self.cols, self.channels), dtype))

    def moved(self, count=1):
        return ("moved", jax.ShapeDtypeStruct((self.n, count * self.size, self.cols), BF16))

    def sums(self, rows):
        return ("all", jax.ShapeDtypeStruct((rows, self.channels), F32))

    def channel_call(self, body, ins, out, scratch, micros):
        spec = pl.BlockSpec(memory_space=pltpu.VMEM)
        return pl.pallas_call(
            functools.partial(body, self.held),
            out_shape=out[1],
            in_specs=[spec] * len(ins),
            out_specs=spec,
            scratch_shapes=[pltpu.VMEM((self.chunks, self.n * self.size, LANES), F32)] * scratch,
            compiler_params=pltpu.CompilerParams(vmem_limit_bytes=VMEM),
            cost_estimate=cost(micros),
        )(*ins)


SCALE = 1.0


def cost(micros):
    micros = micros * SCALE
    return pl.CostEstimate(flops=int(micros * 1.15e9), bytes_accessed=int(micros * 1e6), transcendentals=0)


def weight_sets(w):
    wide = lambda v: jnp.broadcast_to(v[:, None], v.shape + (LANES,))
    vec = jnp.stack([w["gain_in"], w["bias_in"], w["gain_tr"], w["bias_tr"]] + [jnp.zeros_like(w["gain_in"])] * 4)
    col = jnp.stack([wide(w["gain_out"]), wide(w["bias_out"])])
    sets = {**w, "vec": vec, "col": col, "proj_t": jnp.transpose(w["proj"])}
    return lambda names: [("all", sets[name]) for name in names]


def steps(kernels, crops, pair, cot, weights, early):
    w0, w1 = weight_sets(weights[0]), weight_sets(weights[1])
    call, pairs, moved = kernels.row_call, kernels.pairs, kernels.moved
    up_sums, low_sums = kernels.sums(UP_ROWS), kernels.sums(LOW_ROWS)
    earlier = lambda *names: [("all", state[0][name]) for name in names if name in state[0]]
    mine = lambda v, crop: [("own", v[0]), ("rows", v[1][crop])]
    part = lambda *vs: [("rows", v) for v in vs]
    far = lambda *vs: [("moved", v) for v in vs]
    swap = lambda v: lax.all_to_all(v, ("row", "grp"), 0, 0)
    state = [dict() for _ in range(crops)]
    last = {}

    def ordered(kind, op, value):
        if kind in last:
            value, _ = lax.optimization_barrier((value, last[kind]))
        result = op(value)
        last[kind] = result[0] if isinstance(result, (tuple, list)) else result
        return result

    def row_kernel(body, crop, ins, *rest):
        return ordered("kernel", lambda v: call(body, crop, [(ins[0][0], v)] + ins[1:], *rest), ins[0][1])

    def channel_kernel(body, ins, *rest):
        return ordered("kernel", lambda v: kernels.channel_call(body, (v,) + tuple(ins[1:]), *rest), ins[0])

    def pre(crop, s):
        s["normed_0"], s["both_0"] = row_kernel(k_pre, crop, mine(pair, crop) + w0(PRE), [pairs(BF16), moved(2)], 2, 11)

    def post_pre(crop, s):
        s["out_0"], s["normed_1"], s["both_1"] = row_kernel(
            k_post_pre, crop, mine(pair, crop) + mine(pair, crop) + part(s["normed_0"]) + far(s["mixed_0"]) + w0(POST) + w1(PRE),
            [pairs(BF16), pairs(BF16), moved(2)], 3, 20,
        )

    def post_upper(crop, s):
        s["out_1"], s["grad_1"], s["gate_1"], s["grad_mixed_1"], s["up_1"] = row_kernel(
            k_post_upper, crop, mine(pair, crop) + mine(cot, crop) + part(s["out_0"], s["normed_1"]) + far(s["mixed_1"]) + w1(POST) + earlier("up_1"),
            [pairs(BF16), pairs(F32), pairs(BF16), moved(), up_sums], 1, 26, 1,
        )

    def lower_upper(crop, s):
        s["pair_grad_1"], s["grad_0"], s["gate_0"], s["grad_mixed_0"], s["low_1"], s["up_0"] = row_kernel(
            k_lower_upper, crop,
            mine(pair, crop) + mine(pair, crop) + mine(cot, crop) + part(s["out_0"], s["normed_1"], s["grad_1"], s["gate_1"], s["normed_0"])
            + far(s["back_1"], s["mixed_0"]) + w1(LOWER) + w0(POST) + earlier("low_1", "up_0"),
            [pairs(F32), pairs(F32), pairs(BF16), moved(), low_sums, up_sums], 3, 34, 1,
        )

    def lower(crop, s):
        s["pair_grad_0"], s["low_0"] = row_kernel(
            k_lower, crop, mine(pair, crop) + part(s["normed_0"], s["grad_0"], s["gate_0"])
            + far(s["back_0"]) + w0(LOWER) + earlier("low_0"),
            [pairs(F32), low_sums], 2, 14,
        )

    def product(s, k):
        s[f"product_{k}"] = channel_kernel(k_product, (s[f"factors_{k}"],), moved(), 2, 6)

    def product_back(s, k):
        s[f"grads_{k}"] = channel_kernel(k_product_back, (s[f"g_{k}"], s[f"factors_{k}"]), moved(2), 3, 12)

    transfers = dict(S=("factors", "both"), M=("mixed", "product"), G=("g", "grad_mixed"), s=("back", "grads"))
    rows_of = {"1": pre, "2": post_pre, "3": post_upper, "4": lower_upper, "5": lower}
    channels_of = {"T": product, "t": product_back}
    for step in STEPS.split():
        what, crop, k = step[0], "AB".index(step[1]), step[2:]
        s = state[crop]
        if what == "E":
            last["kernel"] = early(s)
            s["early"] = last["kernel"]
        elif what in rows_of:
            rows_of[what](crop, s)
        elif what in channels_of:
            channels_of[what](s, k)
        else:
            new, old = transfers[what]
            s[f"{new}_{k}"] = ordered("swap", swap, s[f"{old}_{k}"])

    return state


def early_sums(first, swap, sums):
    early_0 = jnp.concatenate([sums["up_0"], jnp.zeros((LOW_ROWS, LANES), F32)])
    early_1 = jnp.concatenate([sums["up_1"], sums["low_1"]])
    return jnp.where(first, early_0, early_1) + swap(jnp.where(first, early_1, early_0))


def whole_sums(early, late):
    n = lax.axis_size("row")
    rows = -(-(UP_ROWS + LOW_ROWS) // (16 * n)) * 16
    low = early[UP_ROWS:] + late
    rest = jnp.zeros((n * rows - UP_ROWS - LOW_ROWS, LANES), F32)
    parts = jnp.concatenate([early[:UP_ROWS], low, rest]).astype(BF16).reshape(n, rows, LANES)
    move = lambda v: lax.all_to_all(v, "row", 0, 0)
    share = jnp.sum(move(parts).astype(F32), axis=0).astype(BF16)
    total = move(jnp.broadcast_to(share[None], (n,) + share.shape)).reshape(n * rows, LANES).astype(F32)
    up, low = total[:UP_ROWS], total[UP_ROWS : UP_ROWS + LOW_ROWS]
    wide = lambda rows: jnp.transpose(rows.reshape(4, LANES, LANES), (1, 0, 2)).reshape(LANES, 4 * LANES)
    vec = lambda rows: jnp.sum(rows.reshape(-1, 8, LANES), axis=1)
    gain_tr, bias_tr, gain_out, bias_out = vec(up[UP_VEC:])
    gain_in, bias_in = vec(low[LOW_VEC:])
    return dict(
        down=wide(up[: 4 * LANES]).T, up=wide(up[4 * LANES : 8 * LANES]), out=up[8 * LANES : UP_VEC], gain_tr=gain_tr,
        bias_tr=bias_tr, gain_out=gain_out, bias_out=bias_out, proj=low[: 4 * LANES].T, gate=low[4 * LANES : LOW_VEC],
        gain_in=gain_in, bias_in=bias_in,
    )


def plain_steps(n, base, crop_length, pair_0, pair_1, cot_0, cot_1, weights):
    rows, cols = pair_0.shape[:2]
    own_rows = base + jnp.arange(rows)
    mask = (own_rows < crop_length).astype(F32)[:, None, None] * (jnp.arange(cols) < crop_length).astype(F32)[None, :, None]

    def send(*values):
        return swap_rows(jnp.stack([to_channels(v, n) for v in values], axis=1))

    w0, w1 = weights
    state_0 = pair_0.astype(F32)
    normed_0, left, right = pre(state_0, mask, w0)
    lr_0 = send(left, right)
    mixed_0 = from_channels(swap_rows(product(lr_0[:, 0], lr_0[:, 1]))).astype(F32)
    out_0, saved_0 = post(state_0, normed_0, mixed_0, w0)
    state_1 = out_0.astype(F32) + pair_1.astype(F32)
    normed_1, left, right = pre(state_1, mask, w1)
    lr_1 = send(left, right)
    mixed_1 = from_channels(swap_rows(product(lr_1[:, 0], lr_1[:, 1]))).astype(F32)
    out_1, saved_1 = post(state_1, normed_1, mixed_1, w1)
    grad_result, grad_gate, grad_mixed, upper_1 = back_upper(cot_1.astype(F32), saved_1, w1)
    gm = send(grad_mixed)
    glr = swap_rows(jnp.stack(product_back(gm[:, 0], lr_1[:, 0], lr_1[:, 1]), axis=1))
    grad_1, lower_1 = back_lower(
        state_1, normed_1, mask, grad_result, grad_gate, from_channels(glr[:, 0]), from_channels(glr[:, 1]), w1
    )
    grad_final = cot_0.astype(F32) + grad_1.astype(BF16).astype(F32)
    grad_result, grad_gate, grad_mixed, upper_0 = back_upper(grad_final, saved_0, w0)
    gm = send(grad_mixed)
    glr = swap_rows(jnp.stack(product_back(gm[:, 0], lr_0[:, 0], lr_0[:, 1]), axis=1))
    grad_0, lower_0 = back_lower(
        state_0, normed_0, mask, grad_result, grad_gate, from_channels(glr[:, 0]), from_channels(glr[:, 1]), w0
    )
    return out_0, out_1, grad_0, grad_1, {**upper_0, **lower_0}, {**upper_1, **lower_1}


ORDER = ("gain_in", "bias_in", "proj", "gate", "out", "gain_out", "bias_out", "gain_tr", "bias_tr", "up", "down")


def per_device(pair_in, crop_lengths, gain_in, bias_in, proj, gate, out, gain_out, bias_out, gain_tr, bias_tr, up, down, pair_cot):
    own_weights = dict(
        gain_in=gain_in[0], bias_in=bias_in[0], proj=proj[0], gate=gate[0], out=out[0], gain_out=gain_out[0],
        bias_out=bias_out[0], gain_tr=gain_tr[0], bias_tr=bias_tr[0], up=up[0], down=down[0],
    )
    groups, count = lax.axis_size("grp"), lax.axis_size("row")
    crops, rows, cols, channels = pair_in.shape[1:]
    group = lax.axis_index("grp")
    first = group == 0
    base = lax.axis_index("row") * rows
    swap = lambda v: lax.ppermute(v, "grp", [(0, 1), (1, 0)])
    pick = lambda v, i: lax.dynamic_index_in_dim(v, i, 0, keepdims=False)
    other_weights = {k: swap(v) for k, v in own_weights.items()}
    weights = [
        {k: jnp.where(first, own_weights[k], other_weights[k]) for k in ORDER},
        {k: jnp.where(first, other_weights[k], own_weights[k]) for k in ORDER},
    ]
    n = groups * count
    my_rows = rows // 2
    sizes = channels == LANES and out.shape[1] == LANES and up.shape[2] == 4 * LANES and crops == 2 and groups == 2
    if sizes and rows % 2 == 0 and my_rows % BLOCK_ROWS == 0 and cols % LANES == 0 and channels % n == 0 and n % 8 == 0 and (my_rows * (channels // n)) % 16 == 0:
        place = jnp.stack([crop_lengths[0], crop_lengths[1], base + group * my_rows, group]).astype(jnp.int32)
        kernels = Kernels(place, n, my_rows, cols, channels, BLOCK_ROWS)

        def shared(value):
            other = lambda v: lax.dynamic_slice_in_dim(v, (1 - group) * my_rows, my_rows, 0)
            return value, [swap(other(value[crop])) for crop in range(crops)]

        state = steps(
            kernels, crops, shared(pair_in[0]), shared(pair_cot[0]), weights, functools.partial(early_sums, first, swap)
        )

        def home(name):
            results = []
            for s in state:
                own = jnp.where(first, s[name + "_0"], s[name + "_1"])
                got = swap(jnp.where(first, s[name + "_1"], s[name + "_0"]))
                results.append(jnp.concatenate([jnp.where(first, own, got), jnp.where(first, got, own)], axis=0))
            return jnp.stack(results)[None]

        pair_out, pair_grad = home("out"), home("pair_grad")
        late = jnp.where(first, state[-1]["low_0"], 0.0) + lax.ppermute(state[-1]["low_0"], "grp", [(1, 0)])
        summed = whole_sums(state[-1]["early"], late)
    else:

        def both(value):
            own, got = pick(value, group), swap(pick(value, 1 - group))
            return jnp.where(first, own, got), jnp.where(first, got, own)

        def home(value_0, value_1):
            own, got = jnp.where(first, value_0, value_1), swap(jnp.where(first, value_1, value_0))
            return jnp.stack([jnp.where(first, own, got), jnp.where(first, got, own)])[None]

        out_0, out_1, grad_0, grad_1, grads_0, grads_1 = plain_steps(
            count, base, pick(crop_lengths, group), *both(pair_in[0]), *both(pair_cot[0]), weights
        )
        pair_out, pair_grad = home(out_0, out_1), home(grad_0, grad_1)
        mine = {k: jnp.where(first, grads_0[k], grads_1[k]) + swap(jnp.where(first, grads_1[k], grads_0[k])) for k in ORDER}
        summed = lax.psum(mine, "row")
    return (pair_out, pair_grad) + tuple(summed[k][None] for k in ORDER)


def solution(mesh):
    pair = P("grp", None, "row", None, None)
    vector, matrix = P("grp", None), P("grp", None, None)
    weights = (vector, vector, matrix, matrix, matrix, vector, vector, vector, vector, matrix, matrix)
    return jax.shard_map(
        per_device,
        mesh=mesh,
        in_specs=(pair, P()) + weights + (pair,),
        out_specs=(pair, pair) + weights,
        check_vma=False,
    )
```

```python
import functools

import jax
import jax.numpy as jnp
from jax import lax
from jax.experimental import pallas as pl
from jax.experimental.pallas import tpu as pltpu
from jax.sharding import PartitionSpec as P

EPSILON = 1e-05
F32 = jnp.float32
BF16 = jnp.bfloat16


def norm_stats(values):
    mean_value = jnp.mean(values, axis=-1, keepdims=True)
    centred = values - mean_value
    inv_scale = lax.rsqrt(jnp.mean(centred * centred, axis=-1, keepdims=True) + EPSILON)
    return (centred * inv_scale, inv_scale)


def norm_back(grad_scaled, scaled, inv_scale):
    mean_grad = jnp.mean(grad_scaled, axis=-1, keepdims=True)
    mean_cross = jnp.mean(grad_scaled * scaled, axis=-1, keepdims=True)
    return inv_scale * (grad_scaled - mean_grad - scaled * mean_cross)


def dot(a, b):
    return jnp.dot(a, b, preferred_element_type=F32)


def dot_t(a, b):
    return jnp.einsum("ijf,cf->ijc", a, b, preferred_element_type=F32)


def outer(a, b):
    return jnp.einsum("ijc,ijf->cf", a, b, preferred_element_type=F32)


def to_channels(value, n):
    rows, cols, channels = value.shape
    return jnp.transpose(value, (2, 0, 1)).reshape(n, channels // n, rows, cols)


def from_channels(value):
    n, held, rows, cols = value.shape
    return jnp.transpose(value.reshape(n * held, rows, cols), (1, 2, 0))


def swap_rows(value):
    return lax.all_to_all(value, "row", 0, 0)


def pre(state, mask, w):
    scaled, _ = norm_stats(state)
    normed = (scaled * w["gain_in"] + w["bias_in"]).astype(BF16)
    projected = dot(normed, w["proj"])
    width = projected.shape[-1] // 4
    lv, lg, rv, rg = (projected[..., i * width : (i + 1) * width] for i in range(4))
    left = (jax.nn.sigmoid(lg) * lv * mask).astype(BF16)
    right = (jax.nn.sigmoid(rg) * rv * mask).astype(BF16)
    return normed, left, right


def post(state, normed, mixed, w):
    gate_logit = dot(normed, w["gate"])
    scaled_mid, inv_mid = norm_stats(mixed)
    mixed_norm = (scaled_mid * w["gain_out"] + w["bias_out"]).astype(BF16)
    update = dot(mixed_norm, w["out"])
    gate_sigma = jax.nn.sigmoid(gate_logit)
    first_state = state + gate_sigma * update
    scaled_tr, inv_tr = norm_stats(first_state)
    trans_normed = (scaled_tr * w["gain_tr"] + w["bias_tr"]).astype(BF16)
    hidden = dot(trans_normed, w["up"])
    activated = jax.nn.silu(hidden).astype(BF16)
    result = (first_state + dot(activated, w["down"])).astype(BF16)
    saved = (gate_sigma, scaled_mid, inv_mid, mixed_norm, update, scaled_tr, inv_tr, trans_normed, hidden, activated)
    return result, saved


def back_upper(grad_final, saved, w):
    gate_sigma, scaled_mid, inv_mid, mixed_norm, update, scaled_tr, inv_tr, trans_normed, hidden, activated = saved
    grads = {}
    grad_trans = grad_final.astype(BF16)
    grads["down"] = outer(activated, grad_trans)
    grad_act = dot_t(grad_trans, w["down"])
    sigma = jax.nn.sigmoid(hidden)
    grad_hidden = (grad_act * sigma * (1.0 + hidden * (1.0 - sigma))).astype(BF16)
    grads["up"] = outer(trans_normed, grad_hidden)
    grad_tnorm = dot_t(grad_hidden, w["up"])
    grads["gain_tr"] = jnp.sum(grad_tnorm * scaled_tr, axis=(0, 1))
    grads["bias_tr"] = jnp.sum(grad_tnorm, axis=(0, 1))
    grad_result = grad_final + norm_back(grad_tnorm * w["gain_tr"], scaled_tr, inv_tr)
    grad_update = (grad_result * gate_sigma).astype(BF16)
    grad_gate = (grad_result * update * gate_sigma * (1.0 - gate_sigma)).astype(BF16)
    grads["out"] = outer(mixed_norm, grad_update)
    grad_norm_mid = dot_t(grad_update, w["out"])
    grads["gain_out"] = jnp.sum(grad_norm_mid * scaled_mid, axis=(0, 1))
    grads["bias_out"] = jnp.sum(grad_norm_mid, axis=(0, 1))
    grad_mixed = norm_back(grad_norm_mid * w["gain_out"], scaled_mid, inv_mid).astype(BF16)
    return grad_result, grad_gate, grad_mixed, grads


def back_lower(state, normed, mask, grad_result, grad_gate, grad_left, grad_right, w):
    scaled_in, inv_in = norm_stats(state)
    projected = dot(normed, w["proj"])
    width = projected.shape[-1] // 4
    lv, lg, rv, rg = (projected[..., i * width : (i + 1) * width] for i in range(4))
    ls = jax.nn.sigmoid(lg)
    rs = jax.nn.sigmoid(rg)
    gl = grad_left.astype(F32) * mask
    gr = grad_right.astype(F32) * mask
    grad_proj = jnp.concatenate(
        [gl * ls, gl * lv * ls * (1.0 - ls), gr * rs, gr * rv * rs * (1.0 - rs)], axis=-1
    ).astype(BF16)
    grads = {"proj": outer(normed, grad_proj), "gate": outer(normed, grad_gate)}
    grad_normed = dot_t(grad_proj, w["proj"]) + dot_t(grad_gate, w["gate"])
    grads["gain_in"] = jnp.sum(grad_normed * scaled_in, axis=(0, 1))
    grads["bias_in"] = jnp.sum(grad_normed, axis=(0, 1))
    return grad_result + norm_back(grad_normed * w["gain_in"], scaled_in, inv_in), grads


def product(left, right):
    n, held, rows, cols = left.shape
    mixed = jnp.einsum("atik,btjk->taibj", left, right, preferred_element_type=F32)
    return jnp.transpose(mixed.reshape(held, n, rows, n * rows), (1, 0, 2, 3)).astype(BF16)


def product_back(grad_mixed, left, right):
    n, held, rows, cols = left.shape
    split = grad_mixed.reshape(n, held, rows, n, rows)
    grad_left = jnp.einsum("atibj,btjk->atik", split, right, preferred_element_type=F32)
    grad_right = jnp.einsum("atibj,atik->btjk", split, left, preferred_element_type=F32)
    return grad_left.astype(BF16), grad_right.astype(BF16)


BLOCK_ROWS = 12
LANES = 128
VMEM = 62 << 20


def sig(x):
    return 0.5 * jnp.tanh(0.5 * x) + 0.5


def mm(a, b, ca=1, cb=0):
    return lax.dot_general(a, b, (((ca,), (cb,)), ((), ())), preferred_element_type=F32)


def col_stats(values):
    centred = values - jnp.mean(values, axis=0, keepdims=True)
    inv_scale = lax.rsqrt(jnp.mean(centred * centred, axis=0, keepdims=True) + EPSILON)
    return centred * inv_scale, inv_scale


def col_back(grad_scaled, scaled, inv_scale):
    mean_grad = jnp.mean(grad_scaled, axis=0, keepdims=True)
    mean_cross = jnp.mean(grad_scaled * scaled, axis=0, keepdims=True)
    return inv_scale * (grad_scaled - mean_grad - scaled * mean_cross)


def fold(values):
    return jnp.sum(values.reshape(values.shape[0] // 8, 8, values.shape[1]), axis=0)


class Step:
    def __init__(self, place, n, rows, held, block_rows, crop, last):
        self.last = last
        self.n, self.rows, self.held, self.block = n, rows, held, block_rows
        self.row = pl.program_id(1) * block_rows
        self.length, self.base, self.group = place[crop], place[2], place[3]
        column = pl.program_id(0) * LANES + lax.broadcasted_iota(jnp.int32, (1, LANES), 1)
        self.columns = (column < self.length).astype(F32)

    def mask(self, r):
        return self.columns * jnp.where(self.base + self.row + r < self.length, 1.0, 0.0)

    def flat(self, ref):
        return ref[...].reshape(self.block * LANES, ref.shape[-1])

    def pick(self, pair, section):
        own, got = (self.flat(ref).astype(F32) for ref in pair)
        return jnp.where(jnp.full(own.shape, self.group) == section, own, got)

    def put(self, ref, value):
        ref[...] = value.reshape(self.block, LANES, value.shape[-1]).astype(ref.dtype)

    def lanes(self, r):
        return slice(r * LANES, (r + 1) * LANES)

    def spans(self, r):
        return [pl.ds((self.row + r) * self.held + t, self.n, stride=self.rows * self.held) for t in range(self.held)]

    def load(self, scratch, r):
        return jnp.concatenate([scratch[span, :] for span in self.spans(r)], axis=0)

    def store(self, scratch, r, value):
        for t, span in enumerate(self.spans(r)):
            scratch[span, :] = value[t * self.n : (t + 1) * self.n, :]


def unpack(ref, scratch, first=0):
    n, size = ref.shape[0], scratch.shape[0] // ref.shape[0]

    def body(d, carry):
        scratch[pl.ds(pl.multiple_of(d * size, 8), size), :] = ref[d, first : first + size, :].astype(F32)
        return carry

    lax.fori_loop(0, n, body, 0)


def pack(scratch, ref, first=0):
    n, size = ref.shape[0], scratch.shape[0] // ref.shape[0]

    def body(d, carry):
        ref[d, first : first + size, :] = scratch[pl.ds(pl.multiple_of(d * size, 8), size), :].astype(ref.dtype)
        return carry

    lax.fori_loop(0, n, body, 0)


def at_first(action):
    pl.when(pl.program_id(1) == 0)(action)


def at_last(action):
    pl.when(pl.program_id(1) == pl.num_programs(1) - 1)(action)


def clear(accs, olds, cols=()):
    @pl.when((pl.program_id(0) == 0) & (pl.program_id(1) == 0))
    def _():
        for k, ref in enumerate(accs):
            ref[...] = olds[k][...] if olds else jnp.zeros(ref.shape, ref.dtype)
        for ref in cols:
            ref[...] = jnp.zeros(ref.shape, ref.dtype)


def add_blocks(ref, first, value):
    for q in range(value.shape[1] // LANES):
        ref[first + q * LANES : first + (q + 1) * LANES, :] += value[:, q * LANES : (q + 1) * LANES]


def close(st, ref, cols=None):
    @pl.when((pl.program_id(0) == pl.num_programs(0) - 1) & (pl.program_id(1) == pl.num_programs(1) - 1))
    def _():
        for k in range(2 if cols is not None else 0):
            row = UP_VEC + 16 + 8 * k
            ref[row : row + 1, :] += jnp.sum(jnp.transpose(cols[k]), axis=0, keepdims=True)
        for q in range(4 if st.last else 0):
            block = slice(q * LANES, (q + 1) * LANES)
            ref[block, :] = jnp.transpose(ref[block, :])


def pre_part(st, state, w, normed_ref, left_scr, right_scr):
    scaled, _ = norm_stats(state)
    normed = (scaled * w.vec[0:1, :] + w.vec[1:2, :]).astype(BF16)
    st.put(normed_ref, normed)
    projected = mm(w.proj_t[...], normed, 1, 1)
    for r in range(st.block):
        lv, lg, rv, rg = (projected[q * LANES : (q + 1) * LANES, st.lanes(r)] for q in range(4))
        mask = st.mask(r)
        st.store(left_scr, r, sig(lg) * lv * mask)
        st.store(right_scr, r, sig(rg) * rv * mask)


def post_part(st, state, normed, mixed_scr, w):
    mids = [col_stats(st.load(mixed_scr, r)) for r in range(st.block)]
    gain, bias = w.col[0], w.col[1]
    mixed_norm = jnp.concatenate([(scaled * gain + bias).astype(BF16) for scaled, _ in mids], axis=1)
    update = mm(mixed_norm, w.out[...], 0, 0)
    gate = sig(mm(normed, w.gate[...]))
    first_state = state + gate * update
    scaled_tr, inv_tr = norm_stats(first_state)
    trans = (scaled_tr * w.vec[2:3, :] + w.vec[3:4, :]).astype(BF16)
    hidden = mm(trans, w.up[...])
    sigma = sig(hidden)
    activated = (hidden * sigma).astype(BF16)
    return mids, mixed_norm, update, gate, first_state, scaled_tr, inv_tr, trans, hidden, sigma, activated


def upper_part(st, grad_final, kept, w, acc, cols, grad_ref, gate_ref, mixed_scr):
    mids, mixed_norm, update, gate, first_state, scaled_tr, inv_tr, trans, hidden, sigma, activated = kept
    low = grad_final.astype(BF16)
    add_blocks(acc, 0, mm(low, activated, 0, 0))
    grad_hidden = (mm(low, w.down[...], 1, 1) * (sigma * (1.0 + hidden * (1.0 - sigma)))).astype(BF16)
    add_blocks(acc, 4 * LANES, mm(trans, grad_hidden, 0, 0))
    grad_tnorm = mm(grad_hidden, w.up[...], 1, 1)
    acc[UP_VEC : UP_VEC + 8, :] += fold(grad_tnorm * scaled_tr)
    acc[UP_VEC + 8 : UP_VEC + 16, :] += fold(grad_tnorm)
    grad_result = grad_final + norm_back(grad_tnorm * w.vec[2:3, :], scaled_tr, inv_tr)
    st.put(grad_ref, grad_result)
    scaled_grad = grad_result * gate
    grad_update = scaled_grad.astype(BF16)
    st.put(gate_ref, scaled_grad * update * (1.0 - gate))
    add_blocks(acc, 8 * LANES, mm(mixed_norm, grad_update))
    grad_norm = mm(w.out[...], grad_update, 1, 1)
    for r, (scaled, inv_scale) in enumerate(mids):
        grad = grad_norm[:, st.lanes(r)]
        cols[0] += grad * scaled
        cols[1] += grad
        st.store(mixed_scr, r, col_back(grad * w.col[0], scaled, inv_scale) * st.mask(r))


def lower_part(st, state, normed, grad_result, grad_gate, left_scr, right_scr, w, acc):
    projected = mm(w.proj_t[...], normed, 1, 1)
    parts = []
    for r in range(st.block):
        lv, lg, rv, rg = (projected[q * LANES : (q + 1) * LANES, st.lanes(r)] for q in range(4))
        ls, rs = sig(lg), sig(rg)
        a, b = st.load(left_scr, r) * ls, st.load(right_scr, r) * rs
        parts.append(jnp.concatenate([v.astype(BF16) for v in (a, a * lv * (1.0 - ls), b, b * rv * (1.0 - rs))], axis=0))
    grad_proj = jnp.concatenate(parts, axis=1)
    acc[: 4 * LANES, :] += mm(grad_proj, normed)
    add_blocks(acc, 4 * LANES, mm(normed, grad_gate, 0, 0))
    grad_normed = jnp.transpose(mm(w.proj[...], grad_proj)) + mm(grad_gate, w.gate[...], 1, 1)
    scaled_in, inv_in = norm_stats(state)
    acc[LOW_VEC : LOW_VEC + 8, :] += fold(grad_normed * scaled_in)
    acc[LOW_VEC + 8 : LOW_VEC + 16, :] += fold(grad_normed)
    return grad_result + norm_back(grad_normed * w.vec[0:1, :], scaled_in, inv_in)


class Weights:
    def __init__(self, group, section, refs, scratch):
        self.wide, self.down, self.vec, self.col, self.proj_t = scratch
        cut = lambda first, count: self.wide.at[:, first * LANES : (first + count) * LANES]
        self.proj, self.gate, self.out, self.up = cut(0, 4), cut(4, 1), cut(5, 1), cut(6, 4)

        @pl.when((pl.program_id(0) == 0) & (pl.program_id(1) == 0))
        def _():
            for chosen, sources in ((group == section, refs[:3]), (group != section, refs[3:])):

                @pl.when(chosen)
                def _():
                    for ref, source in zip((self.wide, self.down, self.vec), sources):
                        ref[...] = source[...]

            for k in range(2):
                self.col[k] = jnp.transpose(jnp.broadcast_to(self.vec[4 + k : 5 + k, :], (LANES, LANES)))
            for q in range(4):
                block = slice(q * LANES, (q + 1) * LANES)
                self.proj_t[block, :] = jnp.transpose(self.wide[:, block])

    @staticmethod
    def scratch():
        return [
            pltpu.VMEM((LANES, 10 * LANES), BF16), pltpu.VMEM((4 * LANES, LANES), BF16), pltpu.VMEM((8, LANES), F32),
            pltpu.VMEM((2, LANES, LANES), F32), pltpu.VMEM((4 * LANES, LANES), BF16),
        ]


def pack_weights(w):
    zero = jnp.zeros_like(w["gain_in"])
    names = ("gain_in", "bias_in", "gain_tr", "bias_tr", "gain_out", "bias_out")
    wide = jnp.concatenate([w[name] for name in ("proj", "gate", "out", "up")], axis=1)
    return wide, w["down"], jnp.stack([w[name] for name in names] + [zero, zero])


UP_VEC = 9 * LANES
UP_ROWS = UP_VEC + 32
LOW_VEC = 5 * LANES
LOW_ROWS = LOW_VEC + 16


def k_pre(cfg, place, own, got, *refs):
    st = Step(place, *cfg)
    w = Weights(st.group, 0, refs[:6], refs[-5:])
    normed, both, left, right = refs[6:-5]
    pre_part(st, st.pick((own, got), 0), w, normed, left, right)

    @at_last
    def _():
        pack(left, both)
        pack(right, both, both.shape[1] // 2)


def k_post_pre(cfg, place, own_0, got_0, own_1, got_1, normed_in, mixed_in, *refs):
    st = Step(place, *cfg)
    w0, w1 = Weights(st.group, 0, refs[:6], refs[-10:-5]), Weights(st.group, 1, refs[:6], refs[-5:])
    *_, home, out, normed, both, mixed, left, right = refs[6:-10]
    at_first(lambda: unpack(mixed_in, mixed))
    kept = post_part(st, st.pick((own_0, got_0), 0), st.flat(normed_in), mixed, w0)
    result = (kept[4] + mm(kept[-1], w0.down[...])).astype(BF16)
    st.put(home, result)
    st.put(out, result)
    pre_part(st, result.astype(F32) + st.pick((own_1, got_1), 1), w1, normed, left, right)

    @at_last
    def _():
        pack(left, both)
        pack(right, both, both.shape[1] // 2)


def k_post_upper(cfg, place, own, got, own_cot, got_cot, before, normed_in, mixed_in, *refs):
    st = Step(place, *cfg)
    w = Weights(st.group, 1, refs[:6], refs[-5:])
    _, *olds, home, out, grad, gate, grad_mixed, sums, mixed, cols = refs[6:-5]
    clear([sums], olds, [cols])
    at_first(lambda: unpack(mixed_in, mixed))
    state = st.flat(before).astype(F32) + st.pick((own, got), 1)
    kept = post_part(st, state, st.flat(normed_in), mixed, w)
    result = kept[4] + mm(kept[-1], w.down[...])
    st.put(home, result)
    st.put(out, result)
    upper_part(st, st.pick((own_cot, got_cot), 1), kept, w, sums, cols, grad, gate, mixed)
    close(st, sums, cols)
    at_last(lambda: pack(mixed, grad_mixed))


def k_lower_upper(
    cfg, place, own_1, got_1, own_0, got_0, own_cot, got_cot, before, normed_1, grad_1, gate_1, normed_0, both, mixed_in, *refs
):
    st = Step(place, *cfg)
    w1, w0 = Weights(st.group, 1, refs[:6], refs[-10:-5]), Weights(st.group, 0, refs[:6], refs[-5:])
    olds = refs[7:9] if cfg[-2] else ()
    home, pair_grad, grad, gate, grad_mixed, low_sums, up_sums, left, right, mixed, cols = refs[-21:-10]
    clear([low_sums, up_sums], olds, [cols])

    @at_first
    def _():
        unpack(both, left)
        unpack(both, right, both.shape[1] // 2)
        unpack(mixed_in, mixed)

    state = st.flat(before).astype(F32) + st.pick((own_1, got_1), 1)
    grad_state = lower_part(
        st, state, st.flat(normed_1), st.flat(grad_1), st.flat(gate_1), left, right, w1, low_sums
    )
    st.put(home, grad_state)
    st.put(pair_grad, grad_state)
    kept = post_part(st, st.pick((own_0, got_0), 0), st.flat(normed_0), mixed, w0)
    grad_final = st.pick((own_cot, got_cot), 0) + grad_state.astype(BF16).astype(F32)
    upper_part(st, grad_final, kept, w0, up_sums, cols, grad, gate, mixed)
    close(st, low_sums)
    close(st, up_sums, cols)
    at_last(lambda: pack(mixed, grad_mixed))


def k_lower(cfg, place, own, got, normed, grad, gate, both, *refs):
    st = Step(place, *cfg)
    w = Weights(st.group, 0, refs[:6], refs[-5:])
    _, *olds, home, pair_grad, sums, parts, left, right = refs[6:-5]
    clear([sums], olds)

    @at_first
    def _():
        unpack(both, left)
        unpack(both, right, both.shape[1] // 2)

    state = st.pick((own, got), 0)
    grad_state = lower_part(
        st, state, st.flat(normed), st.flat(grad), st.flat(gate), left, right, w, sums
    )
    st.put(home, grad_state)
    st.put(pair_grad, grad_state)
    close(st, sums)

    @pl.when((pl.program_id(0) == pl.num_programs(0) - 1) & (pl.program_id(1) == pl.num_programs(1) - 1))
    def _():
        n, rows, _ = parts.shape
        parts[...] = jnp.zeros(parts.shape, BF16)
        for d in range(n):
            count = max(0, min(rows, LOW_ROWS - d * rows))
            if count:
                parts[d, :count, :] = sums[d * rows : d * rows + count, :].astype(BF16)


def k_results(total, proj, gate, gain_in, bias_in, out, gain_out, bias_out, gain_tr, bias_tr, up, down, early, low):
    n = total.shape[0]
    first, second = early.shape[0] // n, low.shape[0] // n
    for d in range(n):
        early[d * first : (d + 1) * first, :] = total[d, :first, :].astype(F32)
        low[d * second : (d + 1) * second, :] = total[d, first:, :].astype(F32)
    low[:LOW_ROWS, :] += early[UP_ROWS : UP_ROWS + LOW_ROWS, :]
    down[0] = early[: 4 * LANES, :]
    for q in range(4):
        up[0, :, q * LANES : (q + 1) * LANES] = early[(4 + q) * LANES : (5 + q) * LANES, :]
        proj[0, :, q * LANES : (q + 1) * LANES] = low[q * LANES : (q + 1) * LANES, :]
    out[0] = early[8 * LANES : UP_VEC, :]
    gate[0] = low[4 * LANES : LOW_VEC, :]
    for k, ref in enumerate((gain_tr, bias_tr, gain_out, bias_out)):
        ref[...] = jnp.sum(early[UP_VEC + 8 * k : UP_VEC + 8 * k + 8, :], axis=0, keepdims=True)
    for k, ref in enumerate((gain_in, bias_in)):
        ref[...] = jnp.sum(low[LOW_VEC + 8 * k : LOW_VEC + 8 * k + 8, :], axis=0, keepdims=True)


def spread(ref, scratch, first=0):
    n, size = ref.shape[0], scratch.shape[1] // ref.shape[0]

    def body(d, carry):
        for c in range(scratch.shape[0]):
            value = ref[d, first : first + size, c * LANES : (c + 1) * LANES]
            scratch[c, pl.ds(pl.multiple_of(d * size, 8), size), :] = value.astype(F32)
        return carry

    lax.fori_loop(0, n, body, 0)


def gather(scratch, ref, first=0):
    n, size = ref.shape[0], scratch.shape[1] // ref.shape[0]

    def body(d, carry):
        for c in range(scratch.shape[0]):
            value = scratch[c, pl.ds(pl.multiple_of(d * size, 8), size), :]
            ref[d, first : first + size, c * LANES : (c + 1) * LANES] = value.astype(ref.dtype)
        return carry

    lax.fori_loop(0, n, body, 0)


def channel(scratch, t, held):
    chunks, size, _ = scratch.shape
    span = pl.ds(t, size // held, stride=held)
    return jnp.concatenate([scratch[c, span, :].astype(BF16) for c in range(chunks)], axis=1)


def put_channel(scratch, t, held, value):
    chunks, size, _ = scratch.shape
    span = pl.ds(t, size // held, stride=held)
    for c in range(chunks):
        scratch[c, span, :] = value[:, c * LANES : (c + 1) * LANES]


def k_product(held, both, out, left, right):
    spread(both, left)
    spread(both, right, both.shape[1] // 2)

    def body(t, carry):
        put_channel(left, t, held, mm(channel(left, t, held), channel(right, t, held), 1, 1))
        return carry

    lax.fori_loop(0, held, body, 0)
    gather(left, out)


def k_product_back(held, grad_in, both, out, grad, left, right):
    spread(grad_in, grad)
    spread(both, left)
    spread(both, right, both.shape[1] // 2)

    def body(t, carry):
        low, lv, rv = channel(grad, t, held), channel(left, t, held), channel(right, t, held)
        put_channel(left, t, held, mm(low, rv))
        put_channel(right, t, held, mm(low, lv, 0, 0))
        return carry

    lax.fori_loop(0, held, body, 0)
    gather(left, out)
    gather(right, out, both.shape[1] // 2)


STEPS = """\
1A SA0 1B SB0 TA0 MA0 TB0 MB0 2A SA1 2B SB1 TA1 MA1 TB1 MB1 3A GA1 3B GB1 tA1 sA1 tB1 sB1 HA HB 4A GA0 4B GB0 tA0 sA0 tB0 sB0 EB0 QB0 5A JA 5B qB0 JB AB0
"""


class Kernels:
    def __init__(self, place, crops, n, rows, cols, channels, block_rows):
        self.place, self.crops = place, crops
        self.n, self.rows, self.cols, self.channels, self.block = n, rows, cols, channels, block_rows
        self.held = channels // n
        self.size = rows * self.held
        self.chunks = cols // LANES

    def row_call(self, body, crop, ins, outs, scratch, micros, cols=0, sections=1):
        rows, block = self.rows, self.block

        def spec(kind, shape):
            if kind == "own":
                return pl.BlockSpec(
                    (pl.squeezed, block, LANES, shape[-1]), lambda c, i, s: (crop, s[3] * (rows // block) + i, c, 0)
                )
            if kind in ("home 0", "home 1"):
                first = int(kind[-1]) * (rows // block)
                return pl.BlockSpec((pl.squeezed, block, LANES, shape[-1]), lambda c, i, s: (crop, first + i, c, 0))
            if kind == "rows":
                return pl.BlockSpec((block, LANES, shape[-1]), lambda c, i, s: (i, c, 0))
            if kind == "moved":
                return pl.BlockSpec(shape[:-1] + (LANES,), lambda c, i, s: (0, 0, c))
            if kind == "kept":
                return pl.BlockSpec(memory_space=pl.ANY)
            zeros = (0,) * len(shape)
            return pl.BlockSpec(shape, lambda c, i, s: zeros)

        aliases = {1 + k: 0 for k, (kind, _) in enumerate(ins) if kind == "kept"}
        return pl.pallas_call(
            functools.partial(body, (self.n, rows, self.held, block, crop, crop == self.crops - 1)),
            out_shape=tuple(v for _, v in outs),
            grid_spec=pltpu.PrefetchScalarGridSpec(
                num_scalar_prefetch=1,
                grid=(self.chunks, rows // block),
                in_specs=[spec(k, v.shape) for k, v in ins],
                out_specs=tuple(spec(k, v.shape) for k, v in outs),
                scratch_shapes=[pltpu.VMEM((self.channels * rows, LANES), F32)] * scratch
                + [pltpu.VMEM((2, self.channels, LANES), F32)] * cols
                + Weights.scratch() * sections,
            ),
            input_output_aliases=aliases,
            compiler_params=pltpu.CompilerParams(vmem_limit_bytes=VMEM),
            cost_estimate=cost(micros),
        )(self.place, *[v for _, v in ins])

    def home(self, section, dtype):
        return (f"home {section}", jax.ShapeDtypeStruct((self.crops, 2 * self.rows, self.cols, self.channels), dtype))

    def pairs(self, dtype):
        return ("rows", jax.ShapeDtypeStruct((self.rows, self.cols, self.channels), dtype))

    def moved(self, count=1):
        return ("moved", jax.ShapeDtypeStruct((self.n, count * self.size, self.cols), BF16))

    def sums(self, rows):
        return ("all", jax.ShapeDtypeStruct((rows, self.channels), F32))

    def channel_call(self, body, ins, out, scratch, micros):
        spec = pl.BlockSpec(memory_space=pltpu.VMEM)
        return pl.pallas_call(
            functools.partial(body, self.held),
            out_shape=out[1],
            in_specs=[spec] * len(ins),
            out_specs=spec,
            scratch_shapes=[pltpu.VMEM((self.chunks, self.n * self.size, LANES), F32)] * scratch,
            compiler_params=pltpu.CompilerParams(vmem_limit_bytes=VMEM),
            cost_estimate=cost(micros),
        )(*ins)


def cost(micros):
    return pl.CostEstimate(flops=int(micros * 1.15e9), bytes_accessed=int(micros * 1e6), transcendentals=0)


def steps(kernels, crops, pair, cot, weights, early, late_share, other_half, meet):
    w = [("all", v) for v in weights]
    call, pairs, moved = kernels.row_call, kernels.pairs, kernels.moved
    up_sums, low_sums = kernels.sums(UP_ROWS), kernels.sums(LOW_ROWS)
    earlier = lambda *names: [("all", state[0][name]) for name in names if name in state[0]]
    homes = {}
    kept = lambda name: [("kept", homes[name])]
    mine = lambda v, crop: [("own", v[0]), ("rows", v[1][crop])]
    part = lambda *vs: [("rows", v) for v in vs]
    far = lambda *vs: [("moved", v) for v in vs]
    swap = lambda v: lax.all_to_all(v, ("row", "grp"), 0, 0)
    spread_rows = lambda v: lax.all_to_all(v, "row", 0, 0)
    state = [dict() for _ in range(crops)]
    last = {}

    def ordered(kind, op, value):
        if kind in last:
            value, _ = lax.optimization_barrier((value, last[kind]))
        result = op(value)
        last[kind] = result[0] if isinstance(result, (tuple, list)) else result
        return result

    def row_kernel(body, crop, ins, *rest):
        return ordered("kernel", lambda v: call(body, crop, [(ins[0][0], v)] + ins[1:], *rest), ins[0][1])

    def channel_kernel(body, ins, *rest):
        return ordered("kernel", lambda v: kernels.channel_call(body, (v,) + tuple(ins[1:]), *rest), ins[0])

    def pre(crop, s):
        s["normed_0"], s["both_0"] = row_kernel(k_pre, crop, mine(pair, crop) + w, [pairs(BF16), moved(2)], 2, 10)

    def post_pre(crop, s):
        homes["out"], s["out_0"], s["normed_1"], s["both_1"] = row_kernel(
            k_post_pre, crop,
            mine(pair, crop) + mine(pair, crop) + part(s["normed_0"]) + far(s["mixed_0"]) + w + (kept("out") if crop else []),
            [kernels.home(0, BF16), pairs(BF16), pairs(BF16), moved(2)], 3, 18, 0, 2,
        )
        s["got_out_0"] = other_half(s["out_0"], 0)

    def post_upper(crop, s):
        homes["out"], s["out_1"], s["grad_1"], s["gate_1"], s["grad_mixed_1"], s["up_1"] = row_kernel(
            k_post_upper, crop,
            mine(pair, crop) + mine(cot, crop) + part(s["out_0"], s["normed_1"]) + far(s["mixed_1"]) + w + kept("out")
            + earlier("up_1"),
            [kernels.home(1, BF16), pairs(BF16), pairs(F32), pairs(BF16), moved(), up_sums], 1, 23, 1,
        )
        s["got_out_1"] = other_half(s["out_1"], 1)

    def lower_upper(crop, s):
        homes["grad"], s["pair_grad_1"], s["grad_0"], s["gate_0"], s["grad_mixed_0"], s["low_1"], s["up_0"] = row_kernel(
            k_lower_upper, crop,
            mine(pair, crop) + mine(pair, crop) + mine(cot, crop)
            + part(s["out_0"], s["normed_1"], s["grad_1"], s["gate_1"], s["normed_0"])
            + far(s["back_1"], s["mixed_0"]) + w + (kept("grad") if crop else []) + earlier("low_1", "up_0"),
            [kernels.home(1, F32), pairs(F32), pairs(F32), pairs(BF16), moved(), low_sums, up_sums], 3, 31, 1, 2,
        )
        s["got_grad_1"] = other_half(s["pair_grad_1"], 1)

    def lower(crop, s):
        homes["grad"], s["pair_grad_0"], s["low_0"], s["late"] = row_kernel(
            k_lower, crop, mine(pair, crop) + part(s["normed_0"], s["grad_0"], s["gate_0"]) + far(s["back_0"]) + w
            + kept("grad") + earlier("low_0"),
            [kernels.home(0, F32), pairs(F32), low_sums, ("all", jax.ShapeDtypeStruct(share_shape(LOW_ROWS), BF16))], 2, 13,
        )
        s["got_grad_0"] = other_half(s["pair_grad_0"], 0)

    def product(s, k):
        s[f"product_{k}"] = channel_kernel(k_product, (s[f"factors_{k}"],), moved(), 2, 6)

    def product_back(s, k):
        s[f"grads_{k}"] = channel_kernel(k_product_back, (s[f"g_{k}"], s[f"factors_{k}"]), moved(2), 3, 12)

    transfers = dict(S=("factors", "both"), M=("mixed", "product"), G=("g", "grad_mixed"), s=("back", "grads"))
    rows_of = {"1": pre, "2": post_pre, "3": post_upper, "4": lower_upper, "5": lower}
    channels_of = {"T": product, "t": product_back}
    for step in STEPS.split():
        what, crop, k = step[0], "AB".index(step[1]), step[2:]
        s = state[crop]
        if what == "E":
            sums = {name: lax.optimization_barrier((s[name], last["kernel"]))[0] for name in ("up_0", "up_1", "low_1")}
            last["kernel"] = s["early"] = early(sums)
        elif what in "QqA":
            if what == "A":
                s["total"] = ordered("swap", spread_rows, late_share(s["share_q"], s["share_Q"]))
            else:
                moved_parts = ordered("swap", spread_rows, s["early" if what == "Q" else "late"])
                s[f"share_{what}"] = jnp.sum(moved_parts.astype(F32), axis=0)
        elif what in "HJ":
            name = "out" if what == "H" else "grad"
            homes[name] = meet(homes[name], crop, s[f"got_{name}_0"], s[f"got_{name}_1"])
            if what == "H":
                last["kernel"] = homes[name]
        elif what in rows_of:
            rows_of[what](crop, s)
        elif what in channels_of:
            channels_of[what](s, k)
        else:
            new, old = transfers[what]
            s[f"{new}_{k}"] = ordered("swap", swap, s[f"{old}_{k}"])

    return state, homes


def share_shape(rows):
    n = lax.axis_size("row")
    return (n, -(-rows // (16 * n)) * 16, LANES)


def early_sums(first, swap, sums):
    early_0 = jnp.concatenate([sums["up_0"], jnp.zeros((LOW_ROWS, LANES), F32)])
    early_1 = jnp.concatenate([sums["up_1"], sums["low_1"]])
    early = jnp.where(first, early_0, early_1) + swap(jnp.where(first, early_1, early_0))
    n, rows, _ = share_shape(early.shape[0])
    rest = jnp.zeros((n * rows - early.shape[0], LANES), F32)
    return jnp.concatenate([early, rest]).astype(BF16).reshape(n, rows, LANES)


def late_share(first, late, early):
    late = jnp.where(first, late, 0.0) + lax.ppermute(late, "grp", [(1, 0)])
    share = jnp.concatenate([early, late]).astype(BF16)
    return jnp.broadcast_to(share[None], (lax.axis_size("row"),) + share.shape)


def plain_steps(n, base, crop_length, pair_0, pair_1, cot_0, cot_1, weights):
    rows, cols = pair_0.shape[:2]
    own_rows = base + jnp.arange(rows)
    mask = (own_rows < crop_length).astype(F32)[:, None, None] * (jnp.arange(cols) < crop_length).astype(F32)[None, :, None]

    def send(*values):
        return swap_rows(jnp.stack([to_channels(v, n) for v in values], axis=1))

    w0, w1 = weights
    state_0 = pair_0.astype(F32)
    normed_0, left, right = pre(state_0, mask, w0)
    lr_0 = send(left, right)
    mixed_0 = from_channels(swap_rows(product(lr_0[:, 0], lr_0[:, 1]))).astype(F32)
    out_0, saved_0 = post(state_0, normed_0, mixed_0, w0)
    state_1 = out_0.astype(F32) + pair_1.astype(F32)
    normed_1, left, right = pre(state_1, mask, w1)
    lr_1 = send(left, right)
    mixed_1 = from_channels(swap_rows(product(lr_1[:, 0], lr_1[:, 1]))).astype(F32)
    out_1, saved_1 = post(state_1, normed_1, mixed_1, w1)
    grad_result, grad_gate, grad_mixed, upper_1 = back_upper(cot_1.astype(F32), saved_1, w1)
    gm = send(grad_mixed)
    glr = swap_rows(jnp.stack(product_back(gm[:, 0], lr_1[:, 0], lr_1[:, 1]), axis=1))
    grad_1, lower_1 = back_lower(
        state_1, normed_1, mask, grad_result, grad_gate, from_channels(glr[:, 0]), from_channels(glr[:, 1]), w1
    )
    grad_final = cot_0.astype(F32) + grad_1.astype(BF16).astype(F32)
    grad_result, grad_gate, grad_mixed, upper_0 = back_upper(grad_final, saved_0, w0)
    gm = send(grad_mixed)
    glr = swap_rows(jnp.stack(product_back(gm[:, 0], lr_0[:, 0], lr_0[:, 1]), axis=1))
    grad_0, lower_0 = back_lower(
        state_0, normed_0, mask, grad_result, grad_gate, from_channels(glr[:, 0]), from_channels(glr[:, 1]), w0
    )
    return out_0, out_1, grad_0, grad_1, {**upper_0, **lower_0}, {**upper_1, **lower_1}


ORDER = ("gain_in", "bias_in", "proj", "gate", "out", "gain_out", "bias_out", "gain_tr", "bias_tr", "up", "down")


def per_device(pair_in, crop_lengths, gain_in, bias_in, proj, gate, out, gain_out, bias_out, gain_tr, bias_tr, up, down, pair_cot):
    own_weights = dict(
        gain_in=gain_in[0], bias_in=bias_in[0], proj=proj[0], gate=gate[0], out=out[0], gain_out=gain_out[0],
        bias_out=bias_out[0], gain_tr=gain_tr[0], bias_tr=bias_tr[0], up=up[0], down=down[0],
    )
    groups, count = lax.axis_size("grp"), lax.axis_size("row")
    crops, rows, cols, channels = pair_in.shape[1:]
    group = lax.axis_index("grp")
    first = group == 0
    base = lax.axis_index("row") * rows
    swap = lambda v: lax.ppermute(v, "grp", [(0, 1), (1, 0)])
    pick = lambda v, i: lax.dynamic_index_in_dim(v, i, 0, keepdims=False)
    n = groups * count
    my_rows = rows // 2
    sizes = channels == LANES and out.shape[1] == LANES and up.shape[2] == 4 * LANES and crops == 2 and groups == 2
    if sizes and rows % 2 == 0 and my_rows % BLOCK_ROWS == 0 and cols % LANES == 0 and channels % n == 0 and n % 8 == 0 and (my_rows * (channels // n)) % 16 == 0:
        place = jnp.stack([crop_lengths[0], crop_lengths[1], base + group * my_rows, group]).astype(jnp.int32)
        kernels = Kernels(place, crops, n, my_rows, cols, channels, BLOCK_ROWS)

        def shared(value):
            other = lambda crop: lax.dynamic_slice(value, (crop, (1 - group) * my_rows, 0, 0), (1, my_rows, cols, channels))
            return value, [swap(other(crop)[0]) for crop in range(crops)]

        def meet(home, crop, got_0, got_1):
            half = jnp.where(first, got_0, got_1)[None]
            return lax.dynamic_update_slice(home, half, (crop, (1 - group) * my_rows, 0, 0))

        other_half = lambda value, section: lax.ppermute(value, "grp", [(1 - section, section)])
        pair, own = shared(pair_in[0]), pack_weights(own_weights)
        state, homes = steps(
            kernels, crops, pair, shared(pair_cot[0]), own + tuple(swap(v) for v in own), functools.partial(early_sums, first, swap),
            functools.partial(late_share, first), other_half, meet,
        )
        total, _ = lax.optimization_barrier((state[-1]["total"], homes["grad"]))
        spec = pl.BlockSpec(memory_space=pltpu.VMEM)
        order = ("proj", "gate", "gain_in", "bias_in", "out", "gain_out", "bias_out", "gain_tr", "bias_tr", "up", "down")
        arrays = dict(
            gain_in=gain_in, bias_in=bias_in, proj=proj, gate=gate, out=out, gain_out=gain_out, bias_out=bias_out, gain_tr=gain_tr,
            bias_tr=bias_tr, up=up, down=down,
        )
        results = pl.pallas_call(
            k_results,
            out_shape=[jax.ShapeDtypeStruct(arrays[name].shape, F32) for name in order],
            in_specs=[spec],
            out_specs=[spec] * len(order),
            scratch_shapes=[pltpu.VMEM((s[0] * s[1], LANES), F32) for s in (share_shape(UP_ROWS + LOW_ROWS), share_shape(LOW_ROWS))],
            compiler_params=pltpu.CompilerParams(vmem_limit_bytes=VMEM),
        )(total)
        results = dict(zip(order, results))
        return (homes["out"][None], homes["grad"][None]) + tuple(results[name] for name in ORDER)

    other_weights = {k: swap(v) for k, v in own_weights.items()}
    weights = [
        {k: jnp.where(first, own_weights[k], other_weights[k]) for k in ORDER},
        {k: jnp.where(first, other_weights[k], own_weights[k]) for k in ORDER},
    ]

    def both(value):
        own, got = pick(value, group), swap(pick(value, 1 - group))
        return jnp.where(first, own, got), jnp.where(first, got, own)

    def home(value_0, value_1):
        own, got = jnp.where(first, value_0, value_1), swap(jnp.where(first, value_1, value_0))
        return jnp.stack([jnp.where(first, own, got), jnp.where(first, got, own)])[None]

    out_0, out_1, grad_0, grad_1, grads_0, grads_1 = plain_steps(
        count, base, pick(crop_lengths, group), *both(pair_in[0]), *both(pair_cot[0]), weights
    )
    pair_out, pair_grad = home(out_0, out_1), home(grad_0, grad_1)
    mine = {k: jnp.where(first, grads_0[k], grads_1[k]) + swap(jnp.where(first, grads_1[k], grads_0[k])) for k in ORDER}
    summed = lax.psum(mine, "row")
    return (pair_out, pair_grad) + tuple(summed[k][None] for k in ORDER)


def solution(mesh):
    pair = P("grp", None, "row", None, None)
    vector, matrix = P("grp", None), P("grp", None, None)
    weights = (vector, vector, matrix, matrix, matrix, vector, vector, vector, vector, matrix, matrix)
    return jax.shard_map(
        per_device,
        mesh=mesh,
        in_specs=(pair, P()) + weights + (pair,),
        out_specs=(pair, pair) + weights,
        check_vma=False,
    )
```

```python
import functools

import jax
import jax.numpy as jnp
from jax import lax
from jax.experimental import pallas as pl
from jax.experimental.pallas import tpu as pltpu
from jax.sharding import PartitionSpec as P

EPSILON = 1e-05
F32 = jnp.float32
BF16 = jnp.bfloat16


def norm_stats(values):
    mean_value = jnp.mean(values, axis=-1, keepdims=True)
    centred = values - mean_value
    inv_scale = lax.rsqrt(jnp.mean(centred * centred, axis=-1, keepdims=True) + EPSILON)
    return (centred * inv_scale, inv_scale)


def norm_back(grad_scaled, scaled, inv_scale):
    mean_grad = jnp.mean(grad_scaled, axis=-1, keepdims=True)
    mean_cross = jnp.mean(grad_scaled * scaled, axis=-1, keepdims=True)
    return inv_scale * (grad_scaled - mean_grad - scaled * mean_cross)


def dot(a, b):
    return jnp.dot(a, b, preferred_element_type=F32)


def dot_t(a, b):
    return jnp.einsum("ijf,cf->ijc", a, b, preferred_element_type=F32)


def outer(a, b):
    return jnp.einsum("ijc,ijf->cf", a, b, preferred_element_type=F32)


def to_channels(value, n):
    rows, cols, channels = value.shape
    return jnp.transpose(value, (2, 0, 1)).reshape(n, channels // n, rows, cols)


def from_channels(value):
    n, held, rows, cols = value.shape
    return jnp.transpose(value.reshape(n * held, rows, cols), (1, 2, 0))


def swap_rows(value):
    return lax.all_to_all(value, "row", 0, 0)


def pre(state, mask, w):
    scaled, _ = norm_stats(state)
    normed = (scaled * w["gain_in"] + w["bias_in"]).astype(BF16)
    projected = dot(normed, w["proj"])
    width = projected.shape[-1] // 4
    lv, lg, rv, rg = (projected[..., i * width : (i + 1) * width] for i in range(4))
    left = (jax.nn.sigmoid(lg) * lv * mask).astype(BF16)
    right = (jax.nn.sigmoid(rg) * rv * mask).astype(BF16)
    return normed, left, right


def post(state, normed, mixed, w):
    gate_logit = dot(normed, w["gate"])
    scaled_mid, inv_mid = norm_stats(mixed)
    mixed_norm = (scaled_mid * w["gain_out"] + w["bias_out"]).astype(BF16)
    update = dot(mixed_norm, w["out"])
    gate_sigma = jax.nn.sigmoid(gate_logit)
    first_state = state + gate_sigma * update
    scaled_tr, inv_tr = norm_stats(first_state)
    trans_normed = (scaled_tr * w["gain_tr"] + w["bias_tr"]).astype(BF16)
    hidden = dot(trans_normed, w["up"])
    activated = jax.nn.silu(hidden).astype(BF16)
    result = (first_state + dot(activated, w["down"])).astype(BF16)
    saved = (gate_sigma, scaled_mid, inv_mid, mixed_norm, update, scaled_tr, inv_tr, trans_normed, hidden, activated)
    return result, saved


def back_upper(grad_final, saved, w):
    gate_sigma, scaled_mid, inv_mid, mixed_norm, update, scaled_tr, inv_tr, trans_normed, hidden, activated = saved
    grads = {}
    grad_trans = grad_final.astype(BF16)
    grads["down"] = outer(activated, grad_trans)
    grad_act = dot_t(grad_trans, w["down"])
    sigma = jax.nn.sigmoid(hidden)
    grad_hidden = (grad_act * sigma * (1.0 + hidden * (1.0 - sigma))).astype(BF16)
    grads["up"] = outer(trans_normed, grad_hidden)
    grad_tnorm = dot_t(grad_hidden, w["up"])
    grads["gain_tr"] = jnp.sum(grad_tnorm * scaled_tr, axis=(0, 1))
    grads["bias_tr"] = jnp.sum(grad_tnorm, axis=(0, 1))
    grad_result = grad_final + norm_back(grad_tnorm * w["gain_tr"], scaled_tr, inv_tr)
    grad_update = (grad_result * gate_sigma).astype(BF16)
    grad_gate = (grad_result * update * gate_sigma * (1.0 - gate_sigma)).astype(BF16)
    grads["out"] = outer(mixed_norm, grad_update)
    grad_norm_mid = dot_t(grad_update, w["out"])
    grads["gain_out"] = jnp.sum(grad_norm_mid * scaled_mid, axis=(0, 1))
    grads["bias_out"] = jnp.sum(grad_norm_mid, axis=(0, 1))
    grad_mixed = norm_back(grad_norm_mid * w["gain_out"], scaled_mid, inv_mid).astype(BF16)
    return grad_result, grad_gate, grad_mixed, grads


def back_lower(state, normed, mask, grad_result, grad_gate, grad_left, grad_right, w):
    scaled_in, inv_in = norm_stats(state)
    projected = dot(normed, w["proj"])
    width = projected.shape[-1] // 4
    lv, lg, rv, rg = (projected[..., i * width : (i + 1) * width] for i in range(4))
    ls = jax.nn.sigmoid(lg)
    rs = jax.nn.sigmoid(rg)
    gl = grad_left.astype(F32) * mask
    gr = grad_right.astype(F32) * mask
    grad_proj = jnp.concatenate(
        [gl * ls, gl * lv * ls * (1.0 - ls), gr * rs, gr * rv * rs * (1.0 - rs)], axis=-1
    ).astype(BF16)
    grads = {"proj": outer(normed, grad_proj), "gate": outer(normed, grad_gate)}
    grad_normed = dot_t(grad_proj, w["proj"]) + dot_t(grad_gate, w["gate"])
    grads["gain_in"] = jnp.sum(grad_normed * scaled_in, axis=(0, 1))
    grads["bias_in"] = jnp.sum(grad_normed, axis=(0, 1))
    return grad_result + norm_back(grad_normed * w["gain_in"], scaled_in, inv_in), grads


def product(left, right):
    n, held, rows, cols = left.shape
    mixed = jnp.einsum("atik,btjk->taibj", left, right, preferred_element_type=F32)
    return jnp.transpose(mixed.reshape(held, n, rows, n * rows), (1, 0, 2, 3)).astype(BF16)


def product_back(grad_mixed, left, right):
    n, held, rows, cols = left.shape
    split = grad_mixed.reshape(n, held, rows, n, rows)
    grad_left = jnp.einsum("atibj,btjk->atik", split, right, preferred_element_type=F32)
    grad_right = jnp.einsum("atibj,atik->btjk", split, left, preferred_element_type=F32)
    return grad_left.astype(BF16), grad_right.astype(BF16)


BLOCK_ROWS = 12
LANES = 128
VMEM = 62 << 20


def sig(x):
    return 0.5 * jnp.tanh(0.5 * x) + 0.5


def mm(a, b, ca=1, cb=0):
    return lax.dot_general(a, b, (((ca,), (cb,)), ((), ())), preferred_element_type=F32)


def col_stats(values):
    centred = values - jnp.mean(values, axis=0, keepdims=True)
    inv_scale = lax.rsqrt(jnp.mean(centred * centred, axis=0, keepdims=True) + EPSILON)
    return centred * inv_scale, inv_scale


def col_back(grad_scaled, scaled, inv_scale):
    mean_grad = jnp.mean(grad_scaled, axis=0, keepdims=True)
    mean_cross = jnp.mean(grad_scaled * scaled, axis=0, keepdims=True)
    return inv_scale * (grad_scaled - mean_grad - scaled * mean_cross)


def fold(values):
    return jnp.sum(values.reshape(values.shape[0] // 8, 8, values.shape[1]), axis=0)


class Step:
    def __init__(self, place, n, rows, held, block_rows, crop, last, used, chunks):
        self.last = last
        self.live = pl.program_id(0) < used if used < chunks else None
        self.n, self.rows, self.held, self.block = n, rows, held, block_rows
        self.row = pl.program_id(1) * block_rows
        self.length, self.base, self.group = place[crop], place[2], place[3]
        column = pl.program_id(0) * LANES + lax.broadcasted_iota(jnp.int32, (1, LANES), 1)
        self.columns = (column < self.length).astype(F32)

    def mask(self, r):
        return self.columns * jnp.where(self.base + self.row + r < self.length, 1.0, 0.0)

    def flat(self, ref):
        return ref[...].reshape(self.block * LANES, ref.shape[-1])

    def pick(self, pair, section):
        own, got = (self.flat(ref).astype(F32) for ref in pair)
        return jnp.where(jnp.full(own.shape, self.group) == section, own, got)

    def put(self, ref, value):
        ref[...] = value.reshape(self.block, LANES, value.shape[-1]).astype(ref.dtype)

    def lanes(self, r):
        return slice(r * LANES, (r + 1) * LANES)

    def spans(self, r):
        return [pl.ds((self.row + r) * self.held + t, self.n, stride=self.rows * self.held) for t in range(self.held)]

    def load(self, scratch, r):
        return jnp.concatenate([scratch[span, :] for span in self.spans(r)], axis=0)

    def store(self, scratch, r, value):
        for t, span in enumerate(self.spans(r)):
            scratch[span, :] = value[t * self.n : (t + 1) * self.n, :]


def unpack(ref, scratch, first=0):
    n, size = ref.shape[0], scratch.shape[0] // ref.shape[0]

    def body(d, carry):
        scratch[pl.ds(pl.multiple_of(d * size, 8), size), :] = ref[d, first : first + size, :].astype(F32)
        return carry

    lax.fori_loop(0, n, body, 0)


def pack(scratch, ref, first=0):
    n, size = ref.shape[0], scratch.shape[0] // ref.shape[0]

    def body(d, carry):
        ref[d, first : first + size, :] = scratch[pl.ds(pl.multiple_of(d * size, 8), size), :].astype(ref.dtype)
        return carry

    lax.fori_loop(0, n, body, 0)


def fetch(st, ref, scratch, first=0):
    if st.live is None:
        return unpack(ref, scratch, first)

    @pl.when(st.live)
    def _():
        unpack(ref, scratch, first)

    @pl.when(jnp.logical_not(st.live))
    def _():
        scratch[...] = jnp.zeros(scratch.shape, scratch.dtype)


def deliver(st, scratch, ref, first=0):
    if st.live is None:
        return pack(scratch, ref, first)
    pl.when(st.live)(lambda: pack(scratch, ref, first))


def at_first(action):
    pl.when(pl.program_id(1) == 0)(action)


def at_last(action):
    pl.when(pl.program_id(1) == pl.num_programs(1) - 1)(action)


def clear(accs, olds, cols=()):
    @pl.when((pl.program_id(0) == 0) & (pl.program_id(1) == 0))
    def _():
        for k, ref in enumerate(accs):
            ref[...] = olds[k][...] if olds else jnp.zeros(ref.shape, ref.dtype)
        for ref in cols:
            ref[...] = jnp.zeros(ref.shape, ref.dtype)


def add_blocks(ref, first, value):
    for q in range(value.shape[1] // LANES):
        ref[first + q * LANES : first + (q + 1) * LANES, :] += value[:, q * LANES : (q + 1) * LANES]


def close(st, ref, cols=None):
    @pl.when((pl.program_id(0) == pl.num_programs(0) - 1) & (pl.program_id(1) == pl.num_programs(1) - 1))
    def _():
        for k in range(2 if cols is not None else 0):
            row = UP_VEC + 16 + 8 * k
            ref[row : row + 1, :] += jnp.sum(jnp.transpose(cols[k]), axis=0, keepdims=True)
        for q in range(4 if st.last else 0):
            block = slice(q * LANES, (q + 1) * LANES)
            ref[block, :] = jnp.transpose(ref[block, :])


def pre_part(st, state, w, normed_ref, left_scr, right_scr):
    scaled, _ = norm_stats(state)
    normed = (scaled * w.vec[0:1, :] + w.vec[1:2, :]).astype(BF16)
    st.put(normed_ref, normed)
    projected = mm(w.proj_t[...], normed, 1, 1)
    for r in range(st.block):
        lv, lg, rv, rg = (projected[q * LANES : (q + 1) * LANES, st.lanes(r)] for q in range(4))
        mask = st.mask(r)
        st.store(left_scr, r, sig(lg) * lv * mask)
        st.store(right_scr, r, sig(rg) * rv * mask)


def post_part(st, state, normed, mixed_scr, w):
    mids = [col_stats(st.load(mixed_scr, r)) for r in range(st.block)]
    gain, bias = w.col[0], w.col[1]
    mixed_norm = jnp.concatenate([(scaled * gain + bias).astype(BF16) for scaled, _ in mids], axis=1)
    update = mm(mixed_norm, w.out[...], 0, 0)
    gate = sig(mm(normed, w.gate[...]))
    first_state = state + gate * update
    scaled_tr, inv_tr = norm_stats(first_state)
    trans = (scaled_tr * w.vec[2:3, :] + w.vec[3:4, :]).astype(BF16)
    hidden = mm(trans, w.up[...])
    sigma = sig(hidden)
    activated = (hidden * sigma).astype(BF16)
    return mids, mixed_norm, update, gate, first_state, scaled_tr, inv_tr, trans, hidden, sigma, activated


def upper_part(st, grad_final, kept, w, acc, cols, grad_ref, gate_ref, mixed_scr):
    mids, mixed_norm, update, gate, first_state, scaled_tr, inv_tr, trans, hidden, sigma, activated = kept
    low = grad_final.astype(BF16)
    add_blocks(acc, 0, mm(low, activated, 0, 0))
    grad_hidden = (mm(low, w.down[...], 1, 1) * (sigma * (1.0 + hidden * (1.0 - sigma)))).astype(BF16)
    add_blocks(acc, 4 * LANES, mm(trans, grad_hidden, 0, 0))
    grad_tnorm = mm(grad_hidden, w.up[...], 1, 1)
    acc[UP_VEC : UP_VEC + 8, :] += fold(grad_tnorm * scaled_tr)
    acc[UP_VEC + 8 : UP_VEC + 16, :] += fold(grad_tnorm)
    grad_result = grad_final + norm_back(grad_tnorm * w.vec[2:3, :], scaled_tr, inv_tr)
    st.put(grad_ref, grad_result)
    scaled_grad = grad_result * gate
    grad_update = scaled_grad.astype(BF16)
    st.put(gate_ref, scaled_grad * update * (1.0 - gate))
    add_blocks(acc, 8 * LANES, mm(mixed_norm, grad_update))
    grad_norm = mm(w.out[...], grad_update, 1, 1)
    for r, (scaled, inv_scale) in enumerate(mids):
        grad = grad_norm[:, st.lanes(r)]
        cols[0] += grad * scaled
        cols[1] += grad
        st.store(mixed_scr, r, col_back(grad * w.col[0], scaled, inv_scale) * st.mask(r))


def lower_part(st, state, normed, grad_result, grad_gate, left_scr, right_scr, w, acc):
    projected = mm(w.proj_t[...], normed, 1, 1)
    parts = []
    for r in range(st.block):
        lv, lg, rv, rg = (projected[q * LANES : (q + 1) * LANES, st.lanes(r)] for q in range(4))
        ls, rs = sig(lg), sig(rg)
        a, b = st.load(left_scr, r) * ls, st.load(right_scr, r) * rs
        parts.append(jnp.concatenate([v.astype(BF16) for v in (a, a * lv * (1.0 - ls), b, b * rv * (1.0 - rs))], axis=0))
    grad_proj = jnp.concatenate(parts, axis=1)
    acc[: 4 * LANES, :] += mm(grad_proj, normed)
    add_blocks(acc, 4 * LANES, mm(normed, grad_gate, 0, 0))
    grad_normed = jnp.transpose(mm(w.proj[...], grad_proj)) + mm(grad_gate, w.gate[...], 1, 1)
    scaled_in, inv_in = norm_stats(state)
    acc[LOW_VEC : LOW_VEC + 8, :] += fold(grad_normed * scaled_in)
    acc[LOW_VEC + 8 : LOW_VEC + 16, :] += fold(grad_normed)
    return grad_result + norm_back(grad_normed * w.vec[0:1, :], scaled_in, inv_in)


class Weights:
    def __init__(self, group, section, refs, scratch):
        self.wide, self.down, self.vec, self.col, self.proj_t = scratch
        cut = lambda first, count: self.wide.at[:, first * LANES : (first + count) * LANES]
        self.proj, self.gate, self.out, self.up = cut(0, 4), cut(4, 1), cut(5, 1), cut(6, 4)

        @pl.when((pl.program_id(0) == 0) & (pl.program_id(1) == 0))
        def _():
            for chosen, sources in ((group == section, refs[:3]), (group != section, refs[3:])):

                @pl.when(chosen)
                def _():
                    for ref, source in zip((self.wide, self.down, self.vec), sources):
                        ref[...] = source[...]

            for k in range(2):
                self.col[k] = jnp.transpose(jnp.broadcast_to(self.vec[4 + k : 5 + k, :], (LANES, LANES)))
            for q in range(4):
                block = slice(q * LANES, (q + 1) * LANES)
                self.proj_t[block, :] = jnp.transpose(self.wide[:, block])

    @staticmethod
    def scratch():
        return [
            pltpu.VMEM((LANES, 10 * LANES), BF16), pltpu.VMEM((4 * LANES, LANES), BF16), pltpu.VMEM((8, LANES), F32),
            pltpu.VMEM((2, LANES, LANES), F32), pltpu.VMEM((4 * LANES, LANES), BF16),
        ]


def pack_weights(w):
    zero = jnp.zeros_like(w["gain_in"])
    names = ("gain_in", "bias_in", "gain_tr", "bias_tr", "gain_out", "bias_out")
    wide = jnp.concatenate([w[name] for name in ("proj", "gate", "out", "up")], axis=1)
    return wide, w["down"], jnp.stack([w[name] for name in names] + [zero, zero])


UP_VEC = 9 * LANES
UP_ROWS = UP_VEC + 32
LOW_VEC = 5 * LANES
LOW_ROWS = LOW_VEC + 16


def k_pre(cfg, place, own, got, *refs):
    st = Step(place, *cfg)
    w = Weights(st.group, 0, refs[:6], refs[-5:])
    normed, both, left, right = refs[6:-5]
    pre_part(st, st.pick((own, got), 0), w, normed, left, right)

    @at_last
    def _():
        deliver(st, left, both)
        deliver(st, right, both, both.shape[1] // 2)


def k_post_pre(cfg, place, own_0, got_0, own_1, got_1, normed_in, mixed_in, *refs):
    st = Step(place, *cfg)
    w0, w1 = Weights(st.group, 0, refs[:6], refs[-10:-5]), Weights(st.group, 1, refs[:6], refs[-5:])
    *_, home, out, normed, both, mixed, left, right = refs[6:-10]
    at_first(lambda: fetch(st, mixed_in, mixed))
    kept = post_part(st, st.pick((own_0, got_0), 0), st.flat(normed_in), mixed, w0)
    result = (kept[4] + mm(kept[-1], w0.down[...])).astype(BF16)
    st.put(home, result)
    st.put(out, result)
    pre_part(st, result.astype(F32) + st.pick((own_1, got_1), 1), w1, normed, left, right)

    @at_last
    def _():
        deliver(st, left, both)
        deliver(st, right, both, both.shape[1] // 2)


def k_post_upper(cfg, place, own, got, own_cot, got_cot, before, normed_in, mixed_in, *refs):
    st = Step(place, *cfg)
    w = Weights(st.group, 1, refs[:6], refs[-5:])
    _, *olds, home, out, grad, gate, grad_mixed, sums, mixed, cols = refs[6:-5]
    clear([sums], olds, [cols])
    at_first(lambda: fetch(st, mixed_in, mixed))
    state = st.flat(before).astype(F32) + st.pick((own, got), 1)
    kept = post_part(st, state, st.flat(normed_in), mixed, w)
    result = kept[4] + mm(kept[-1], w.down[...])
    st.put(home, result)
    st.put(out, result)
    upper_part(st, st.pick((own_cot, got_cot), 1), kept, w, sums, cols, grad, gate, mixed)
    close(st, sums, cols)
    at_last(lambda: deliver(st, mixed, grad_mixed))


def k_lower_upper(
    cfg, place, own_1, got_1, own_0, got_0, own_cot, got_cot, before, normed_1, grad_1, gate_1, normed_0, both, mixed_in, *refs
):
    st = Step(place, *cfg)
    w1, w0 = Weights(st.group, 1, refs[:6], refs[-10:-5]), Weights(st.group, 0, refs[:6], refs[-5:])
    olds = refs[7:9] if cfg[4] else ()
    home, pair_grad, grad, gate, grad_mixed, low_sums, up_sums, left, right, mixed, cols = refs[-21:-10]
    clear([low_sums, up_sums], olds, [cols])

    @at_first
    def _():
        fetch(st, both, left)
        fetch(st, both, right, both.shape[1] // 2)
        fetch(st, mixed_in, mixed)

    state = st.flat(before).astype(F32) + st.pick((own_1, got_1), 1)
    grad_state = lower_part(
        st, state, st.flat(normed_1), st.flat(grad_1), st.flat(gate_1), left, right, w1, low_sums
    )
    st.put(home, grad_state)
    st.put(pair_grad, grad_state)
    kept = post_part(st, st.pick((own_0, got_0), 0), st.flat(normed_0), mixed, w0)
    grad_final = st.pick((own_cot, got_cot), 0) + grad_state.astype(BF16).astype(F32)
    upper_part(st, grad_final, kept, w0, up_sums, cols, grad, gate, mixed)
    close(st, low_sums)
    close(st, up_sums, cols)
    at_last(lambda: deliver(st, mixed, grad_mixed))


def k_lower(cfg, place, own, got, normed, grad, gate, both, *refs):
    st = Step(place, *cfg)
    w = Weights(st.group, 0, refs[:6], refs[-5:])
    _, *olds, home, pair_grad, sums, parts, left, right = refs[6:-5]
    clear([sums], olds)

    @at_first
    def _():
        fetch(st, both, left)
        fetch(st, both, right, both.shape[1] // 2)

    state = st.pick((own, got), 0)
    grad_state = lower_part(
        st, state, st.flat(normed), st.flat(grad), st.flat(gate), left, right, w, sums
    )
    st.put(home, grad_state)
    st.put(pair_grad, grad_state)
    close(st, sums)

    @pl.when((pl.program_id(0) == pl.num_programs(0) - 1) & (pl.program_id(1) == pl.num_programs(1) - 1))
    def _():
        n, rows, _ = parts.shape
        parts[...] = jnp.zeros(parts.shape, BF16)
        for d in range(n):
            count = max(0, min(rows, LOW_ROWS - d * rows))
            if count:
                parts[d, :count, :] = sums[d * rows : d * rows + count, :].astype(BF16)


def k_results(total, proj, gate, gain_in, bias_in, out, gain_out, bias_out, gain_tr, bias_tr, up, down, early, low):
    n = total.shape[0]
    first, second = early.shape[0] // n, low.shape[0] // n
    for d in range(n):
        early[d * first : (d + 1) * first, :] = total[d, :first, :].astype(F32)
        low[d * second : (d + 1) * second, :] = total[d, first:, :].astype(F32)
    low[:LOW_ROWS, :] += early[UP_ROWS : UP_ROWS + LOW_ROWS, :]
    down[0] = early[: 4 * LANES, :]
    for q in range(4):
        up[0, :, q * LANES : (q + 1) * LANES] = early[(4 + q) * LANES : (5 + q) * LANES, :]
        proj[0, :, q * LANES : (q + 1) * LANES] = low[q * LANES : (q + 1) * LANES, :]
    out[0] = early[8 * LANES : UP_VEC, :]
    gate[0] = low[4 * LANES : LOW_VEC, :]
    for k, ref in enumerate((gain_tr, bias_tr, gain_out, bias_out)):
        ref[...] = jnp.sum(early[UP_VEC + 8 * k : UP_VEC + 8 * k + 8, :], axis=0, keepdims=True)
    for k, ref in enumerate((gain_in, bias_in)):
        ref[...] = jnp.sum(low[LOW_VEC + 8 * k : LOW_VEC + 8 * k + 8, :], axis=0, keepdims=True)


def spread(ref, scratch, first=0):
    n, size = ref.shape[0], scratch.shape[1] // ref.shape[0]

    def body(d, carry):
        for c in range(scratch.shape[0]):
            value = ref[d, first : first + size, c * LANES : (c + 1) * LANES]
            scratch[c, pl.ds(pl.multiple_of(d * size, 8), size), :] = value.astype(F32)
        return carry

    lax.fori_loop(0, n, body, 0)


def gather(scratch, ref, first=0):
    n, size = ref.shape[0], scratch.shape[1] // ref.shape[0]

    def body(d, carry):
        for c in range(scratch.shape[0]):
            value = scratch[c, pl.ds(pl.multiple_of(d * size, 8), size), :]
            ref[d, first : first + size, c * LANES : (c + 1) * LANES] = value.astype(ref.dtype)
        return carry

    lax.fori_loop(0, n, body, 0)


def channel(scratch, t, held):
    chunks, size, _ = scratch.shape
    span = pl.ds(t, size // held, stride=held)
    return jnp.concatenate([scratch[c, span, :].astype(BF16) for c in range(chunks)], axis=1)


def put_channel(scratch, t, held, value):
    chunks, size, _ = scratch.shape
    span = pl.ds(t, size // held, stride=held)
    for c in range(chunks):
        scratch[c, span, :] = value[:, c * LANES : (c + 1) * LANES]


def k_product(held, both, out, left, right):
    spread(both, left)
    spread(both, right, both.shape[1] // 2)

    def body(t, carry):
        others = channel(right, t, held)[: left.shape[0] * LANES]
        put_channel(left, t, held, mm(channel(left, t, held), others, 1, 1))
        return carry

    lax.fori_loop(0, held, body, 0)
    gather(left, out)


def k_product_back(held, grad_in, both, out, grad, left, right):
    spread(grad_in, grad)
    spread(both, left)
    spread(both, right, both.shape[1] // 2)

    def body(t, carry):
        low, lv, rv = channel(grad, t, held), channel(left, t, held), channel(right, t, held)
        put_channel(left, t, held, mm(low, rv[: low.shape[1]]))
        grad_right = mm(low, lv, 0, 0)
        if low.shape[1] < rv.shape[0]:
            rest = jnp.zeros((rv.shape[0] - low.shape[1], lv.shape[1]), F32)
            grad_right = jnp.concatenate([grad_right, rest])
        put_channel(right, t, held, grad_right)
        return carry

    lax.fori_loop(0, held, body, 0)
    gather(left, out)
    gather(right, out, both.shape[1] // 2)


STEPS = """\
1A SA0 1B SB0 TA0 MA0 TB0 MB0 2A SA1 2B SB1 TA1 MA1 TB1 MB1 3A GA1 3B GB1 tA1 sA1 tB1 sB1 HA HB 4A GA0 4B GB0 tA0 sA0 tB0 sB0 EB0 QB0 5A JA 5B qB0 JB AB0
"""


class Kernels:
    def __init__(self, place, used, n, rows, cols, channels, block_rows):
        self.place, self.used, self.crops = place, used, len(used)
        self.n, self.rows, self.cols, self.channels, self.block = n, rows, cols, channels, block_rows
        self.held = channels // n
        self.size = rows * self.held
        self.chunks = cols // LANES

    def row_call(self, body, crop, ins, outs, scratch, micros, cols=0, sections=1):
        rows, block = self.rows, self.block

        def spec(kind, shape):
            if kind == "own":
                return pl.BlockSpec(
                    (pl.squeezed, block, LANES, shape[-1]), lambda c, i, s: (s[4 + crop], s[3] * (rows // block) + i, c, 0)
                )
            if kind in ("home 0", "home 1"):
                first = int(kind[-1]) * (rows // block)
                return pl.BlockSpec((pl.squeezed, block, LANES, shape[-1]), lambda c, i, s: (s[4 + crop], first + i, c, 0))
            if kind == "rows":
                return pl.BlockSpec((block, LANES, shape[-1]), lambda c, i, s: (i, c, 0))
            if kind == "moved":
                final = shape[-1] // LANES - 1
                return pl.BlockSpec(shape[:-1] + (LANES,), lambda c, i, s: (0, 0, jnp.minimum(c, final)))
            if kind == "kept":
                return pl.BlockSpec(memory_space=pl.ANY)
            zeros = (0,) * len(shape)
            return pl.BlockSpec(shape, lambda c, i, s: zeros)

        aliases = {1 + k: 0 for k, (kind, _) in enumerate(ins) if kind == "kept"}
        return pl.pallas_call(
            functools.partial(
                body, (self.n, rows, self.held, block, crop, crop == self.crops - 1, self.used[crop], self.chunks)
            ),
            out_shape=tuple(v for _, v in outs),
            grid_spec=pltpu.PrefetchScalarGridSpec(
                num_scalar_prefetch=1,
                grid=(self.chunks, rows // block),
                in_specs=[spec(k, v.shape) for k, v in ins],
                out_specs=tuple(spec(k, v.shape) for k, v in outs),
                scratch_shapes=[pltpu.VMEM((self.channels * rows, LANES), F32)] * scratch
                + [pltpu.VMEM((2, self.channels, LANES), F32)] * cols
                + Weights.scratch() * sections,
            ),
            input_output_aliases=aliases,
            compiler_params=pltpu.CompilerParams(vmem_limit_bytes=VMEM),
            cost_estimate=cost(micros),
        )(self.place, *[v for _, v in ins])

    def home(self, section, dtype):
        return (f"home {section}", jax.ShapeDtypeStruct((self.crops, 2 * self.rows, self.cols, self.channels), dtype))

    def pairs(self, dtype):
        return ("rows", jax.ShapeDtypeStruct((self.rows, self.cols, self.channels), dtype))

    def moved(self, crop, count=1):
        return ("moved", jax.ShapeDtypeStruct((self.n, count * self.size, self.used[crop] * LANES), BF16))

    def sums(self, rows):
        return ("all", jax.ShapeDtypeStruct((rows, self.channels), F32))

    def channel_call(self, body, ins, out, scratch, micros):
        spec = pl.BlockSpec(memory_space=pltpu.VMEM)
        return pl.pallas_call(
            functools.partial(body, self.held),
            out_shape=out[1],
            in_specs=[spec] * len(ins),
            out_specs=spec,
            scratch_shapes=[pltpu.VMEM((out[1].shape[2] // LANES, self.n * self.size, LANES), F32)] * scratch,
            compiler_params=pltpu.CompilerParams(vmem_limit_bytes=VMEM),
            cost_estimate=cost(micros),
        )(*ins)


def cost(micros):
    return pl.CostEstimate(flops=int(micros * 1.15e9), bytes_accessed=int(micros * 1e6), transcendentals=0)


def steps(kernels, crops, pair, cot, weights, early, late_share, other_half, meet):
    w = [("all", v) for v in weights]
    call, pairs, moved = kernels.row_call, kernels.pairs, kernels.moved
    up_sums, low_sums = kernels.sums(UP_ROWS), kernels.sums(LOW_ROWS)
    earlier = lambda *names: [("all", state[0][name]) for name in names if name in state[0]]
    homes = {}
    kept = lambda name: [("kept", homes[name])]
    mine = lambda v, crop: [("own", v[0]), ("rows", v[1][crop])]
    part = lambda *vs: [("rows", v) for v in vs]
    far = lambda *vs: [("moved", v) for v in vs]
    swap = lambda v: lax.all_to_all(v, ("row", "grp"), 0, 0)
    spread_rows = lambda v: lax.all_to_all(v, "row", 0, 0)
    state = [dict() for _ in range(crops)]
    last = {}

    def ordered(kind, op, value):
        if kind in last:
            value, _ = lax.optimization_barrier((value, last[kind]))
        result = op(value)
        last[kind] = result[0] if isinstance(result, (tuple, list)) else result
        return result

    def row_kernel(body, crop, ins, *rest):
        return ordered("kernel", lambda v: call(body, crop, [(ins[0][0], v)] + ins[1:], *rest), ins[0][1])

    def channel_kernel(body, ins, *rest):
        return ordered("kernel", lambda v: kernels.channel_call(body, (v,) + tuple(ins[1:]), *rest), ins[0])

    def pre(crop, s):
        s["normed_0"], s["both_0"] = row_kernel(k_pre, crop, mine(pair, crop) + w, [pairs(BF16), moved(crop, 2)], 2, 10)

    def post_pre(crop, s):
        homes["out"], s["out_0"], s["normed_1"], s["both_1"] = row_kernel(
            k_post_pre, crop,
            mine(pair, crop) + mine(pair, crop) + part(s["normed_0"]) + far(s["mixed_0"]) + w + (kept("out") if crop else []),
            [kernels.home(0, BF16), pairs(BF16), pairs(BF16), moved(crop, 2)], 3, 18, 0, 2,
        )
        s["got_out_0"] = other_half(s["out_0"], 0)

    def post_upper(crop, s):
        homes["out"], s["out_1"], s["grad_1"], s["gate_1"], s["grad_mixed_1"], s["up_1"] = row_kernel(
            k_post_upper, crop,
            mine(pair, crop) + mine(cot, crop) + part(s["out_0"], s["normed_1"]) + far(s["mixed_1"]) + w + kept("out")
            + earlier("up_1"),
            [kernels.home(1, BF16), pairs(BF16), pairs(F32), pairs(BF16), moved(crop), up_sums], 1, 23, 1,
        )
        s["got_out_1"] = other_half(s["out_1"], 1)

    def lower_upper(crop, s):
        homes["grad"], s["pair_grad_1"], s["grad_0"], s["gate_0"], s["grad_mixed_0"], s["low_1"], s["up_0"] = row_kernel(
            k_lower_upper, crop,
            mine(pair, crop) + mine(pair, crop) + mine(cot, crop)
            + part(s["out_0"], s["normed_1"], s["grad_1"], s["gate_1"], s["normed_0"])
            + far(s["back_1"], s["mixed_0"]) + w + (kept("grad") if crop else []) + earlier("low_1", "up_0"),
            [kernels.home(1, F32), pairs(F32), pairs(F32), pairs(BF16), moved(crop), low_sums, up_sums], 3, 31, 1, 2,
        )
        s["got_grad_1"] = other_half(s["pair_grad_1"], 1)

    def lower(crop, s):
        homes["grad"], s["pair_grad_0"], s["low_0"], s["late"] = row_kernel(
            k_lower, crop, mine(pair, crop) + part(s["normed_0"], s["grad_0"], s["gate_0"]) + far(s["back_0"]) + w
            + kept("grad") + earlier("low_0"),
            [kernels.home(0, F32), pairs(F32), low_sums, ("all", jax.ShapeDtypeStruct(share_shape(LOW_ROWS), BF16))], 2, 13,
        )
        s["got_grad_0"] = other_half(s["pair_grad_0"], 0)

    def product(crop, s, k):
        s[f"product_{k}"] = channel_kernel(k_product, (s[f"factors_{k}"],), moved(crop), 2, 6)

    def product_back(crop, s, k):
        s[f"grads_{k}"] = channel_kernel(k_product_back, (s[f"g_{k}"], s[f"factors_{k}"]), moved(crop, 2), 3, 12)

    transfers = dict(S=("factors", "both"), M=("mixed", "product"), G=("g", "grad_mixed"), s=("back", "grads"))
    rows_of = {"1": pre, "2": post_pre, "3": post_upper, "4": lower_upper, "5": lower}
    channels_of = {"T": product, "t": product_back}
    for step in STEPS.split():
        what, crop, k = step[0], "AB".index(step[1]), step[2:]
        s = state[crop]
        if what == "E":
            sums = {name: lax.optimization_barrier((s[name], last["kernel"]))[0] for name in ("up_0", "up_1", "low_1")}
            last["kernel"] = s["early"] = early(sums)
        elif what in "QqA":
            if what == "A":
                s["total"] = ordered("swap", spread_rows, late_share(s["share_q"], s["share_Q"]))
            else:
                moved_parts = ordered("swap", spread_rows, s["early" if what == "Q" else "late"])
                s[f"share_{what}"] = jnp.sum(moved_parts.astype(F32), axis=0)
        elif what in "HJ":
            name = "out" if what == "H" else "grad"
            homes[name] = meet(homes[name], crop, s[f"got_{name}_0"], s[f"got_{name}_1"])
            if what == "H":
                last["kernel"] = homes[name]
        elif what in rows_of:
            rows_of[what](crop, s)
        elif what in channels_of:
            channels_of[what](crop, s, k)
        else:
            new, old = transfers[what]
            s[f"{new}_{k}"] = ordered("swap", swap, s[f"{old}_{k}"])

    return state, homes


def share_shape(rows):
    n = lax.axis_size("row")
    return (n, -(-rows // (16 * n)) * 16, LANES)


def early_sums(first, swap, sums):
    early_0 = jnp.concatenate([sums["up_0"], jnp.zeros((LOW_ROWS, LANES), F32)])
    early_1 = jnp.concatenate([sums["up_1"], sums["low_1"]])
    early = jnp.where(first, early_0, early_1) + swap(jnp.where(first, early_1, early_0))
    n, rows, _ = share_shape(early.shape[0])
    rest = jnp.zeros((n * rows - early.shape[0], LANES), F32)
    return jnp.concatenate([early, rest]).astype(BF16).reshape(n, rows, LANES)


def late_share(first, late, early):
    late = jnp.where(first, late, 0.0) + lax.ppermute(late, "grp", [(1, 0)])
    share = jnp.concatenate([early, late]).astype(BF16)
    return jnp.broadcast_to(share[None], (lax.axis_size("row"),) + share.shape)


def plain_steps(n, base, crop_length, pair_0, pair_1, cot_0, cot_1, weights):
    rows, cols = pair_0.shape[:2]
    own_rows = base + jnp.arange(rows)
    mask = (own_rows < crop_length).astype(F32)[:, None, None] * (jnp.arange(cols) < crop_length).astype(F32)[None, :, None]

    def send(*values):
        return swap_rows(jnp.stack([to_channels(v, n) for v in values], axis=1))

    w0, w1 = weights
    state_0 = pair_0.astype(F32)
    normed_0, left, right = pre(state_0, mask, w0)
    lr_0 = send(left, right)
    mixed_0 = from_channels(swap_rows(product(lr_0[:, 0], lr_0[:, 1]))).astype(F32)
    out_0, saved_0 = post(state_0, normed_0, mixed_0, w0)
    state_1 = out_0.astype(F32) + pair_1.astype(F32)
    normed_1, left, right = pre(state_1, mask, w1)
    lr_1 = send(left, right)
    mixed_1 = from_channels(swap_rows(product(lr_1[:, 0], lr_1[:, 1]))).astype(F32)
    out_1, saved_1 = post(state_1, normed_1, mixed_1, w1)
    grad_result, grad_gate, grad_mixed, upper_1 = back_upper(cot_1.astype(F32), saved_1, w1)
    gm = send(grad_mixed)
    glr = swap_rows(jnp.stack(product_back(gm[:, 0], lr_1[:, 0], lr_1[:, 1]), axis=1))
    grad_1, lower_1 = back_lower(
        state_1, normed_1, mask, grad_result, grad_gate, from_channels(glr[:, 0]), from_channels(glr[:, 1]), w1
    )
    grad_final = cot_0.astype(F32) + grad_1.astype(BF16).astype(F32)
    grad_result, grad_gate, grad_mixed, upper_0 = back_upper(grad_final, saved_0, w0)
    gm = send(grad_mixed)
    glr = swap_rows(jnp.stack(product_back(gm[:, 0], lr_0[:, 0], lr_0[:, 1]), axis=1))
    grad_0, lower_0 = back_lower(
        state_0, normed_0, mask, grad_result, grad_gate, from_channels(glr[:, 0]), from_channels(glr[:, 1]), w0
    )
    return out_0, out_1, grad_0, grad_1, {**upper_0, **lower_0}, {**upper_1, **lower_1}


ORDER = ("gain_in", "bias_in", "proj", "gate", "out", "gain_out", "bias_out", "gain_tr", "bias_tr", "up", "down")


def per_device(pair_in, crop_lengths, gain_in, bias_in, proj, gate, out, gain_out, bias_out, gain_tr, bias_tr, up, down, pair_cot):
    own_weights = dict(
        gain_in=gain_in[0], bias_in=bias_in[0], proj=proj[0], gate=gate[0], out=out[0], gain_out=gain_out[0],
        bias_out=bias_out[0], gain_tr=gain_tr[0], bias_tr=bias_tr[0], up=up[0], down=down[0],
    )
    groups, count = lax.axis_size("grp"), lax.axis_size("row")
    crops, rows, cols, channels = pair_in.shape[1:]
    group = lax.axis_index("grp")
    first = group == 0
    base = lax.axis_index("row") * rows
    swap = lambda v: lax.ppermute(v, "grp", [(0, 1), (1, 0)])
    pick = lambda v, i: lax.dynamic_index_in_dim(v, i, 0, keepdims=False)
    n = groups * count
    my_rows = rows // 2
    sizes = channels == LANES and out.shape[1] == LANES and up.shape[2] == 4 * LANES and crops == 2 and groups == 2
    if sizes and rows % 2 == 0 and my_rows % BLOCK_ROWS == 0 and cols % LANES == 0 and channels % n == 0 and n % 8 == 0 and (my_rows * (channels // n)) % 16 == 0:
        before_last = (cols // LANES - 1) * LANES
        swapped = crop_lengths[0] <= before_last
        which = [jnp.where(swapped, 1, 0), jnp.where(swapped, 0, 1)]
        lengths = [crop_lengths[crop] for crop in which]
        place = jnp.stack(lengths + [base + group * my_rows, group] + which).astype(jnp.int32)
        def shared(value):
            other = lambda crop: lax.dynamic_slice(value, (crop, (1 - group) * my_rows, 0, 0), (1, my_rows, cols, channels))
            return value, [swap(other(crop)[0]) for crop in which]

        def meet(home, crop, got_0, got_1):
            half = jnp.where(first, got_0, got_1)[None]
            return lax.dynamic_update_slice(home, half, (which[crop], (1 - group) * my_rows, 0, 0))

        def run(used):
            other_half = lambda value, section: lax.ppermute(value, "grp", [(1 - section, section)])
            pair, own = shared(pair_in[0]), pack_weights(own_weights)
            kernels = Kernels(place, used, n, my_rows, cols, channels, BLOCK_ROWS)
            state, homes = steps(
                kernels, crops, pair, shared(pair_cot[0]), own + tuple(swap(v) for v in own), functools.partial(early_sums, first, swap),
                functools.partial(late_share, first), other_half, meet,
            )
            total, _ = lax.optimization_barrier((state[-1]["total"], homes["grad"]))
            spec = pl.BlockSpec(memory_space=pltpu.VMEM)
            order = ("proj", "gate", "gain_in", "bias_in", "out", "gain_out", "bias_out", "gain_tr", "bias_tr", "up", "down")
            arrays = dict(
                gain_in=gain_in, bias_in=bias_in, proj=proj, gate=gate, out=out, gain_out=gain_out, bias_out=bias_out, gain_tr=gain_tr,
                bias_tr=bias_tr, up=up, down=down,
            )
            results = pl.pallas_call(
                k_results,
                out_shape=[jax.ShapeDtypeStruct(arrays[name].shape, F32) for name in order],
                in_specs=[spec],
                out_specs=[spec] * len(order),
                scratch_shapes=[pltpu.VMEM((s[0] * s[1], LANES), F32) for s in (share_shape(UP_ROWS + LOW_ROWS), share_shape(LOW_ROWS))],
                compiler_params=pltpu.CompilerParams(vmem_limit_bytes=VMEM),
            )(total)
            results = dict(zip(order, results))
            return (homes["out"][None], homes["grad"][None]) + tuple(results[name] for name in ORDER)

        chunks = cols // LANES
        if chunks == 1:
            return run((1, 1))
        return lax.cond(lengths[1] <= before_last, lambda: run((chunks, chunks - 1)), lambda: run((chunks, chunks)))

    other_weights = {k: swap(v) for k, v in own_weights.items()}
    weights = [
        {k: jnp.where(first, own_weights[k], other_weights[k]) for k in ORDER},
        {k: jnp.where(first, other_weights[k], own_weights[k]) for k in ORDER},
    ]

    def both(value):
        own, got = pick(value, group), swap(pick(value, 1 - group))
        return jnp.where(first, own, got), jnp.where(first, got, own)

    def home(value_0, value_1):
        own, got = jnp.where(first, value_0, value_1), swap(jnp.where(first, value_1, value_0))
        return jnp.stack([jnp.where(first, own, got), jnp.where(first, got, own)])[None]

    out_0, out_1, grad_0, grad_1, grads_0, grads_1 = plain_steps(
        count, base, pick(crop_lengths, group), *both(pair_in[0]), *both(pair_cot[0]), weights
    )
    pair_out, pair_grad = home(out_0, out_1), home(grad_0, grad_1)
    mine = {k: jnp.where(first, grads_0[k], grads_1[k]) + swap(jnp.where(first, grads_1[k], grads_0[k])) for k in ORDER}
    summed = lax.psum(mine, "row")
    return (pair_out, pair_grad) + tuple(summed[k][None] for k in ORDER)


def solution(mesh):
    pair = P("grp", None, "row", None, None)
    vector, matrix = P("grp", None), P("grp", None, None)
    weights = (vector, vector, matrix, matrix, matrix, vector, vector, vector, vector, matrix, matrix)
    return jax.shard_map(
        per_device,
        mesh=mesh,
        in_specs=(pair, P()) + weights + (pair,),
        out_specs=(pair, pair) + weights,
        check_vma=False,
    )
```

```python
import functools

import jax
import jax.numpy as jnp
from jax import lax
from jax.experimental import pallas as pl
from jax.experimental.pallas import tpu as pltpu
from jax.sharding import PartitionSpec as P

EPSILON = 1e-05
F32 = jnp.float32
BF16 = jnp.bfloat16


def norm_stats(values):
    mean_value = jnp.mean(values, axis=-1, keepdims=True)
    centred = values - mean_value
    inv_scale = lax.rsqrt(jnp.mean(centred * centred, axis=-1, keepdims=True) + EPSILON)
    return (centred * inv_scale, inv_scale)


def norm_back(grad_scaled, scaled, inv_scale):
    mean_grad = jnp.mean(grad_scaled, axis=-1, keepdims=True)
    mean_cross = jnp.mean(grad_scaled * scaled, axis=-1, keepdims=True)
    return inv_scale * (grad_scaled - mean_grad - scaled * mean_cross)


def dot(a, b):
    return jnp.dot(a, b, preferred_element_type=F32)


def dot_t(a, b):
    return jnp.einsum("ijf,cf->ijc", a, b, preferred_element_type=F32)


def outer(a, b):
    return jnp.einsum("ijc,ijf->cf", a, b, preferred_element_type=F32)


def to_channels(value, n):
    rows, cols, channels = value.shape
    return jnp.transpose(value, (2, 0, 1)).reshape(n, channels // n, rows, cols)


def from_channels(value):
    n, held, rows, cols = value.shape
    return jnp.transpose(value.reshape(n * held, rows, cols), (1, 2, 0))


def swap_rows(value):
    return lax.all_to_all(value, "row", 0, 0)


def pre(state, mask, w):
    scaled, _ = norm_stats(state)
    normed = (scaled * w["gain_in"] + w["bias_in"]).astype(BF16)
    projected = dot(normed, w["proj"])
    width = projected.shape[-1] // 4
    lv, lg, rv, rg = (projected[..., i * width : (i + 1) * width] for i in range(4))
    left = (jax.nn.sigmoid(lg) * lv * mask).astype(BF16)
    right = (jax.nn.sigmoid(rg) * rv * mask).astype(BF16)
    return normed, left, right


def post(state, normed, mixed, w):
    gate_logit = dot(normed, w["gate"])
    scaled_mid, inv_mid = norm_stats(mixed)
    mixed_norm = (scaled_mid * w["gain_out"] + w["bias_out"]).astype(BF16)
    update = dot(mixed_norm, w["out"])
    gate_sigma = jax.nn.sigmoid(gate_logit)
    first_state = state + gate_sigma * update
    scaled_tr, inv_tr = norm_stats(first_state)
    trans_normed = (scaled_tr * w["gain_tr"] + w["bias_tr"]).astype(BF16)
    hidden = dot(trans_normed, w["up"])
    activated = jax.nn.silu(hidden).astype(BF16)
    result = (first_state + dot(activated, w["down"])).astype(BF16)
    saved = (gate_sigma, scaled_mid, inv_mid, mixed_norm, update, scaled_tr, inv_tr, trans_normed, hidden, activated)
    return result, saved


def back_upper(grad_final, saved, w):
    gate_sigma, scaled_mid, inv_mid, mixed_norm, update, scaled_tr, inv_tr, trans_normed, hidden, activated = saved
    grads = {}
    grad_trans = grad_final.astype(BF16)
    grads["down"] = outer(activated, grad_trans)
    grad_act = dot_t(grad_trans, w["down"])
    sigma = jax.nn.sigmoid(hidden)
    grad_hidden = (grad_act * sigma * (1.0 + hidden * (1.0 - sigma))).astype(BF16)
    grads["up"] = outer(trans_normed, grad_hidden)
    grad_tnorm = dot_t(grad_hidden, w["up"])
    grads["gain_tr"] = jnp.sum(grad_tnorm * scaled_tr, axis=(0, 1))
    grads["bias_tr"] = jnp.sum(grad_tnorm, axis=(0, 1))
    grad_result = grad_final + norm_back(grad_tnorm * w["gain_tr"], scaled_tr, inv_tr)
    grad_update = (grad_result * gate_sigma).astype(BF16)
    grad_gate = (grad_result * update * gate_sigma * (1.0 - gate_sigma)).astype(BF16)
    grads["out"] = outer(mixed_norm, grad_update)
    grad_norm_mid = dot_t(grad_update, w["out"])
    grads["gain_out"] = jnp.sum(grad_norm_mid * scaled_mid, axis=(0, 1))
    grads["bias_out"] = jnp.sum(grad_norm_mid, axis=(0, 1))
    grad_mixed = norm_back(grad_norm_mid * w["gain_out"], scaled_mid, inv_mid).astype(BF16)
    return grad_result, grad_gate, grad_mixed, grads


def back_lower(state, normed, mask, grad_result, grad_gate, grad_left, grad_right, w):
    scaled_in, inv_in = norm_stats(state)
    projected = dot(normed, w["proj"])
    width = projected.shape[-1] // 4
    lv, lg, rv, rg = (projected[..., i * width : (i + 1) * width] for i in range(4))
    ls = jax.nn.sigmoid(lg)
    rs = jax.nn.sigmoid(rg)
    gl = grad_left.astype(F32) * mask
    gr = grad_right.astype(F32) * mask
    grad_proj = jnp.concatenate(
        [gl * ls, gl * lv * ls * (1.0 - ls), gr * rs, gr * rv * rs * (1.0 - rs)], axis=-1
    ).astype(BF16)
    grads = {"proj": outer(normed, grad_proj), "gate": outer(normed, grad_gate)}
    grad_normed = dot_t(grad_proj, w["proj"]) + dot_t(grad_gate, w["gate"])
    grads["gain_in"] = jnp.sum(grad_normed * scaled_in, axis=(0, 1))
    grads["bias_in"] = jnp.sum(grad_normed, axis=(0, 1))
    return grad_result + norm_back(grad_normed * w["gain_in"], scaled_in, inv_in), grads


def product(left, right):
    n, held, rows, cols = left.shape
    mixed = jnp.einsum("atik,btjk->taibj", left, right, preferred_element_type=F32)
    return jnp.transpose(mixed.reshape(held, n, rows, n * rows), (1, 0, 2, 3)).astype(BF16)


def product_back(grad_mixed, left, right):
    n, held, rows, cols = left.shape
    split = grad_mixed.reshape(n, held, rows, n, rows)
    grad_left = jnp.einsum("atibj,btjk->atik", split, right, preferred_element_type=F32)
    grad_right = jnp.einsum("atibj,atik->btjk", split, left, preferred_element_type=F32)
    return grad_left.astype(BF16), grad_right.astype(BF16)


BLOCK_ROWS = 12
LANES = 128
VMEM = 62 << 20


def sig(x):
    return 0.5 * jnp.tanh(0.5 * x) + 0.5


def mm(a, b, ca=1, cb=0):
    return lax.dot_general(a, b, (((ca,), (cb,)), ((), ())), preferred_element_type=F32)


def col_stats(values):
    centred = values - jnp.mean(values, axis=0, keepdims=True)
    inv_scale = lax.rsqrt(jnp.mean(centred * centred, axis=0, keepdims=True) + EPSILON)
    return centred * inv_scale, inv_scale


def col_back(grad_scaled, scaled, inv_scale):
    mean_grad = jnp.mean(grad_scaled, axis=0, keepdims=True)
    mean_cross = jnp.mean(grad_scaled * scaled, axis=0, keepdims=True)
    return inv_scale * (grad_scaled - mean_grad - scaled * mean_cross)


def fold(values):
    return jnp.sum(values.reshape(values.shape[0] // 8, 8, values.shape[1]), axis=0)


class Step:
    def __init__(self, place, n, rows, held, block_rows, crop, last, used, chunks):
        self.last = last
        self.live = pl.program_id(0) < used if used < chunks else None
        self.n, self.rows, self.held, self.block = n, rows, held, block_rows
        self.row = pl.program_id(1) * block_rows
        self.length, self.base, self.group = place[crop], place[2], place[3]
        column = pl.program_id(0) * LANES + lax.broadcasted_iota(jnp.int32, (1, LANES), 1)
        self.columns = (column < self.length).astype(F32)

    def mask(self, r):
        return self.columns * jnp.where(self.base + self.row + r < self.length, 1.0, 0.0)

    def flat(self, ref):
        return ref[...].reshape(self.block * LANES, ref.shape[-1])

    def pick(self, pair, section):
        own, got = (self.flat(ref).astype(F32) for ref in pair)
        return jnp.where(jnp.full(own.shape, self.group) == section, own, got)

    def put(self, ref, value):
        ref[...] = value.reshape(self.block, LANES, value.shape[-1]).astype(ref.dtype)

    def lanes(self, r):
        return slice(r * LANES, (r + 1) * LANES)

    def spans(self, r):
        return [pl.ds((self.row + r) * self.held + t, self.n, stride=self.rows * self.held) for t in range(self.held)]

    def load(self, scratch, r):
        return jnp.concatenate([scratch[span, :] for span in self.spans(r)], axis=0)

    def store(self, scratch, r, value):
        for t, span in enumerate(self.spans(r)):
            scratch[span, :] = value[t * self.n : (t + 1) * self.n, :]


def unpack(ref, scratch, first=0):
    n, size = ref.shape[0], scratch.shape[0] // (ref.shape[0] + 1)

    def body(d, carry):
        scratch[pl.ds(pl.multiple_of(d * size, 8), size), :] = ref[d, first : first + size, :].astype(F32)
        return carry

    lax.fori_loop(0, n, body, 0)


def pack(scratch, ref, first=0):
    n, size = ref.shape[0], scratch.shape[0] // (ref.shape[0] + 1)

    def body(d, carry):
        ref[d, first : first + size, :] = scratch[pl.ds(pl.multiple_of(d * size, 8), size), :].astype(ref.dtype)
        return carry

    lax.fori_loop(0, n, body, 0)


def fetch(st, ref, scratch, first=0):
    if st.live is None:
        return unpack(ref, scratch, first)

    @pl.when(st.live)
    def _():
        unpack(ref, scratch, first)

    @pl.when(jnp.logical_not(st.live))
    def _():
        scratch[...] = jnp.zeros(scratch.shape, scratch.dtype)


def deliver(st, scratch, ref, first=0):
    if st.live is None:
        return pack(scratch, ref, first)
    pl.when(st.live)(lambda: pack(scratch, ref, first))


def at_first(action):
    pl.when(pl.program_id(1) == 0)(action)


def at_last(action):
    pl.when(pl.program_id(1) == pl.num_programs(1) - 1)(action)


def clear(accs, olds, cols=()):
    @pl.when((pl.program_id(0) == 0) & (pl.program_id(1) == 0))
    def _():
        for k, ref in enumerate(accs):
            ref[...] = olds[k][...] if olds else jnp.zeros(ref.shape, ref.dtype)
        for ref in cols:
            ref[...] = jnp.zeros(ref.shape, ref.dtype)


def add_blocks(ref, first, value):
    for q in range(value.shape[1] // LANES):
        ref[first + q * LANES : first + (q + 1) * LANES, :] += value[:, q * LANES : (q + 1) * LANES]


def close(st, ref, cols=None):
    @pl.when((pl.program_id(0) == pl.num_programs(0) - 1) & (pl.program_id(1) == pl.num_programs(1) - 1))
    def _():
        for k in range(2 if cols is not None else 0):
            row = UP_VEC + 16 + 8 * k
            ref[row : row + 1, :] += jnp.sum(jnp.transpose(cols[k]), axis=0, keepdims=True)
        for q in range(4 if st.last else 0):
            block = slice(q * LANES, (q + 1) * LANES)
            ref[block, :] = jnp.transpose(ref[block, :])


def pre_part(st, state, w, normed_ref, left_scr, right_scr):
    scaled, _ = norm_stats(state)
    normed = (scaled * w.vec[0:1, :] + w.vec[1:2, :]).astype(BF16)
    st.put(normed_ref, normed)
    projected = mm(w.proj_t[...], normed, 1, 1)
    for r in range(st.block):
        lv, lg, rv, rg = (projected[q * LANES : (q + 1) * LANES, st.lanes(r)] for q in range(4))
        mask = st.mask(r)
        st.store(left_scr, r, sig(lg) * lv * mask)
        st.store(right_scr, r, sig(rg) * rv * mask)


def post_part(st, state, normed, mixed_scr, w):
    mids = [col_stats(st.load(mixed_scr, r)) for r in range(st.block)]
    gain, bias = w.col[0], w.col[1]
    mixed_norm = jnp.concatenate([(scaled * gain + bias).astype(BF16) for scaled, _ in mids], axis=1)
    update = mm(mixed_norm, w.out[...], 0, 0)
    gate = sig(mm(normed, w.gate[...]))
    first_state = state + gate * update
    scaled_tr, inv_tr = norm_stats(first_state)
    trans = (scaled_tr * w.vec[2:3, :] + w.vec[3:4, :]).astype(BF16)
    hidden = mm(trans, w.up[...])
    sigma = sig(hidden)
    activated = (hidden * sigma).astype(BF16)
    return mids, mixed_norm, update, gate, first_state, scaled_tr, inv_tr, trans, hidden, sigma, activated


def upper_part(st, grad_final, kept, w, acc, cols, grad_ref, gate_ref, mixed_scr):
    mids, mixed_norm, update, gate, first_state, scaled_tr, inv_tr, trans, hidden, sigma, activated = kept
    low = grad_final.astype(BF16)
    add_blocks(acc, 0, mm(low, activated, 0, 0))
    grad_hidden = (mm(low, w.down[...], 1, 1) * (sigma * (1.0 + hidden * (1.0 - sigma)))).astype(BF16)
    add_blocks(acc, 4 * LANES, mm(trans, grad_hidden, 0, 0))
    grad_tnorm = mm(grad_hidden, w.up[...], 1, 1)
    acc[UP_VEC : UP_VEC + 8, :] += fold(grad_tnorm * scaled_tr)
    acc[UP_VEC + 8 : UP_VEC + 16, :] += fold(grad_tnorm)
    grad_result = grad_final + norm_back(grad_tnorm * w.vec[2:3, :], scaled_tr, inv_tr)
    st.put(grad_ref, grad_result)
    scaled_grad = grad_result * gate
    grad_update = scaled_grad.astype(BF16)
    st.put(gate_ref, scaled_grad * update * (1.0 - gate))
    add_blocks(acc, 8 * LANES, mm(mixed_norm, grad_update))
    grad_norm = mm(w.out[...], grad_update, 1, 1)
    for r, (scaled, inv_scale) in enumerate(mids):
        grad = grad_norm[:, st.lanes(r)]
        cols[0] += grad * scaled
        cols[1] += grad
        st.store(mixed_scr, r, col_back(grad * w.col[0], scaled, inv_scale) * st.mask(r))


def lower_part(st, state, normed, grad_result, grad_gate, left_scr, right_scr, w, acc):
    projected = mm(w.proj_t[...], normed, 1, 1)
    parts = []
    for r in range(st.block):
        lv, lg, rv, rg = (projected[q * LANES : (q + 1) * LANES, st.lanes(r)] for q in range(4))
        ls, rs = sig(lg), sig(rg)
        a, b = st.load(left_scr, r) * ls, st.load(right_scr, r) * rs
        parts.append(jnp.concatenate([v.astype(BF16) for v in (a, a * lv * (1.0 - ls), b, b * rv * (1.0 - rs))], axis=0))
    grad_proj = jnp.concatenate(parts, axis=1)
    acc[: 4 * LANES, :] += mm(grad_proj, normed)
    add_blocks(acc, 4 * LANES, mm(normed, grad_gate, 0, 0))
    grad_normed = jnp.transpose(mm(w.proj[...], grad_proj)) + mm(grad_gate, w.gate[...], 1, 1)
    scaled_in, inv_in = norm_stats(state)
    acc[LOW_VEC : LOW_VEC + 8, :] += fold(grad_normed * scaled_in)
    acc[LOW_VEC + 8 : LOW_VEC + 16, :] += fold(grad_normed)
    return grad_result + norm_back(grad_normed * w.vec[0:1, :], scaled_in, inv_in)


class Weights:
    def __init__(self, group, section, refs, scratch):
        self.wide, self.down, self.vec, self.col, self.proj_t = scratch
        cut = lambda first, count: self.wide.at[:, first * LANES : (first + count) * LANES]
        self.proj, self.gate, self.out, self.up = cut(0, 4), cut(4, 1), cut(5, 1), cut(6, 4)

        @pl.when((pl.program_id(0) == 0) & (pl.program_id(1) == 0))
        def _():
            for chosen, sources in ((group == section, refs[:3]), (group != section, refs[3:])):

                @pl.when(chosen)
                def _():
                    for ref, source in zip((self.wide, self.down, self.vec), sources):
                        ref[...] = source[...]

            for k in range(2):
                self.col[k] = jnp.transpose(jnp.broadcast_to(self.vec[4 + k : 5 + k, :], (LANES, LANES)))
            for q in range(4):
                block = slice(q * LANES, (q + 1) * LANES)
                self.proj_t[block, :] = jnp.transpose(self.wide[:, block])

    @staticmethod
    def scratch():
        return [
            pltpu.VMEM((LANES, 10 * LANES), BF16), pltpu.VMEM((4 * LANES, LANES), BF16), pltpu.VMEM((8, LANES), F32),
            pltpu.VMEM((2, LANES, LANES), F32), pltpu.VMEM((4 * LANES, LANES), BF16),
        ]


def pack_weights(w):
    zero = jnp.zeros_like(w["gain_in"])
    names = ("gain_in", "bias_in", "gain_tr", "bias_tr", "gain_out", "bias_out")
    wide = jnp.concatenate([w[name] for name in ("proj", "gate", "out", "up")], axis=1)
    return wide, w["down"], jnp.stack([w[name] for name in names] + [zero, zero])


UP_VEC = 9 * LANES
UP_ROWS = UP_VEC + 32
LOW_VEC = 5 * LANES
LOW_ROWS = LOW_VEC + 16


def k_pre(cfg, place, own, got, *refs):
    st = Step(place, *cfg)
    w = Weights(st.group, 0, refs[:6], refs[-5:])
    normed, both, left, right = refs[6:-5]
    pre_part(st, st.pick((own, got), 0), w, normed, left, right)

    @at_last
    def _():
        deliver(st, left, both)
        deliver(st, right, both, both.shape[1] // 2)


def k_post_pre(cfg, place, own_0, got_0, own_1, got_1, normed_in, mixed_in, *refs):
    st = Step(place, *cfg)
    w0, w1 = Weights(st.group, 0, refs[:6], refs[-10:-5]), Weights(st.group, 1, refs[:6], refs[-5:])
    *_, home, out, normed, both, mixed, left, right = refs[6:-10]
    at_first(lambda: fetch(st, mixed_in, mixed))
    kept = post_part(st, st.pick((own_0, got_0), 0), st.flat(normed_in), mixed, w0)
    result = (kept[4] + mm(kept[-1], w0.down[...])).astype(BF16)
    st.put(home, result)
    st.put(out, result)
    pre_part(st, result.astype(F32) + st.pick((own_1, got_1), 1), w1, normed, left, right)

    @at_last
    def _():
        deliver(st, left, both)
        deliver(st, right, both, both.shape[1] // 2)


def k_post_upper(cfg, place, own, got, own_cot, got_cot, before, normed_in, mixed_in, *refs):
    st = Step(place, *cfg)
    w = Weights(st.group, 1, refs[:6], refs[-5:])
    _, *olds, home, out, grad, gate, grad_mixed, sums, mixed, cols = refs[6:-5]
    clear([sums], olds, [cols])
    at_first(lambda: fetch(st, mixed_in, mixed))
    state = st.flat(before).astype(F32) + st.pick((own, got), 1)
    kept = post_part(st, state, st.flat(normed_in), mixed, w)
    result = kept[4] + mm(kept[-1], w.down[...])
    st.put(home, result)
    st.put(out, result)
    upper_part(st, st.pick((own_cot, got_cot), 1), kept, w, sums, cols, grad, gate, mixed)
    close(st, sums, cols)
    at_last(lambda: deliver(st, mixed, grad_mixed))


def k_lower_upper(
    cfg, place, own_1, got_1, own_0, got_0, own_cot, got_cot, before, normed_1, grad_1, gate_1, normed_0, both, mixed_in, *refs
):
    st = Step(place, *cfg)
    w1, w0 = Weights(st.group, 1, refs[:6], refs[-10:-5]), Weights(st.group, 0, refs[:6], refs[-5:])
    olds = refs[7:9] if cfg[4] else ()
    home, pair_grad, grad, gate, grad_mixed, low_sums, up_sums, left, right, mixed, cols = refs[-21:-10]
    clear([low_sums, up_sums], olds, [cols])

    @at_first
    def _():
        fetch(st, both, left)
        fetch(st, both, right, both.shape[1] // 2)
        fetch(st, mixed_in, mixed)

    state = st.flat(before).astype(F32) + st.pick((own_1, got_1), 1)
    grad_state = lower_part(
        st, state, st.flat(normed_1), st.flat(grad_1), st.flat(gate_1), left, right, w1, low_sums
    )
    st.put(home, grad_state)
    st.put(pair_grad, grad_state)
    kept = post_part(st, st.pick((own_0, got_0), 0), st.flat(normed_0), mixed, w0)
    grad_final = st.pick((own_cot, got_cot), 0) + grad_state.astype(BF16).astype(F32)
    upper_part(st, grad_final, kept, w0, up_sums, cols, grad, gate, mixed)
    close(st, low_sums)
    close(st, up_sums, cols)
    at_last(lambda: deliver(st, mixed, grad_mixed))


def k_lower(cfg, place, own, got, normed, grad, gate, both, *refs):
    st = Step(place, *cfg)
    w = Weights(st.group, 0, refs[:6], refs[-5:])
    _, *olds, home, pair_grad, sums, parts, left, right = refs[6:-5]
    clear([sums], olds)

    @at_first
    def _():
        fetch(st, both, left)
        fetch(st, both, right, both.shape[1] // 2)

    state = st.pick((own, got), 0)
    grad_state = lower_part(
        st, state, st.flat(normed), st.flat(grad), st.flat(gate), left, right, w, sums
    )
    st.put(home, grad_state)
    st.put(pair_grad, grad_state)
    close(st, sums)

    @pl.when((pl.program_id(0) == pl.num_programs(0) - 1) & (pl.program_id(1) == pl.num_programs(1) - 1))
    def _():
        n, rows, _ = parts.shape
        parts[...] = jnp.zeros(parts.shape, BF16)
        for d in range(n):
            count = max(0, min(rows, LOW_ROWS - d * rows))
            if count:
                parts[d, :count, :] = sums[d * rows : d * rows + count, :].astype(BF16)


def k_results(total, proj, gate, gain_in, bias_in, out, gain_out, bias_out, gain_tr, bias_tr, up, down, early, low):
    n = total.shape[0]
    first, second = early.shape[0] // n, low.shape[0] // n
    for d in range(n):
        early[d * first : (d + 1) * first, :] = total[d, :first, :].astype(F32)
        low[d * second : (d + 1) * second, :] = total[d, first:, :].astype(F32)
    low[:LOW_ROWS, :] += early[UP_ROWS : UP_ROWS + LOW_ROWS, :]
    down[0] = early[: 4 * LANES, :]
    for q in range(4):
        up[0, :, q * LANES : (q + 1) * LANES] = early[(4 + q) * LANES : (5 + q) * LANES, :]
        proj[0, :, q * LANES : (q + 1) * LANES] = low[q * LANES : (q + 1) * LANES, :]
    out[0] = early[8 * LANES : UP_VEC, :]
    gate[0] = low[4 * LANES : LOW_VEC, :]
    for k, ref in enumerate((gain_tr, bias_tr, gain_out, bias_out)):
        ref[...] = jnp.sum(early[UP_VEC + 8 * k : UP_VEC + 8 * k + 8, :], axis=0, keepdims=True)
    for k, ref in enumerate((gain_in, bias_in)):
        ref[...] = jnp.sum(low[LOW_VEC + 8 * k : LOW_VEC + 8 * k + 8, :], axis=0, keepdims=True)


def spread(ref, scratch, first=0):
    n, size = ref.shape[0], (scratch.shape[1] - 8) // ref.shape[0]

    def body(d, carry):
        for c in range(scratch.shape[0]):
            value = ref[d, first : first + size, c * LANES : (c + 1) * LANES]
            scratch[c, pl.ds(pl.multiple_of(d * size, 8), size), :] = value.astype(F32)
        return carry

    lax.fori_loop(0, n, body, 0)


def gather(scratch, ref, first=0):
    n, size = ref.shape[0], (scratch.shape[1] - 8) // ref.shape[0]

    def body(d, carry):
        for c in range(scratch.shape[0]):
            value = scratch[c, pl.ds(pl.multiple_of(d * size, 8), size), :]
            ref[d, first : first + size, c * LANES : (c + 1) * LANES] = value.astype(ref.dtype)
        return carry

    lax.fori_loop(0, n, body, 0)


def channel(scratch, t, held):
    chunks, size, _ = scratch.shape
    span = pl.ds(t, (size - 8) // held, stride=held)
    return jnp.concatenate([scratch[c, span, :].astype(BF16) for c in range(chunks)], axis=1)


def put_channel(scratch, t, held, value):
    chunks, size, _ = scratch.shape
    span = pl.ds(t, (size - 8) // held, stride=held)
    for c in range(chunks):
        scratch[c, span, :] = value[:, c * LANES : (c + 1) * LANES]


def k_product(held, both, out, left, right):
    spread(both, left)
    spread(both, right, both.shape[1] // 2)

    def body(t, carry):
        others = channel(right, t, held)[: left.shape[0] * LANES]
        put_channel(left, t, held, mm(channel(left, t, held), others, 1, 1))
        return carry

    lax.fori_loop(0, held, body, 0)
    gather(left, out)


def k_product_back(held, grad_in, both, out, grad, left, right):
    spread(grad_in, grad)
    spread(both, left)
    spread(both, right, both.shape[1] // 2)

    def body(t, carry):
        low, lv, rv = channel(grad, t, held), channel(left, t, held), channel(right, t, held)
        put_channel(left, t, held, mm(low, rv[: low.shape[1]]))
        grad_right = mm(low, lv, 0, 0)
        if low.shape[1] < rv.shape[0]:
            rest = jnp.zeros((rv.shape[0] - low.shape[1], lv.shape[1]), F32)
            grad_right = jnp.concatenate([grad_right, rest])
        put_channel(right, t, held, grad_right)
        return carry

    lax.fori_loop(0, held, body, 0)
    gather(left, out)
    gather(right, out, both.shape[1] // 2)


STEPS = """\
1A SA0 1B SB0 TA0 MA0 TB0 MB0 2A SA1 2B SB1 TA1 MA1 TB1 MB1 3A GA1 3B GB1 tA1 sA1 tB1 sB1 HA HB 4A GA0 4B GB0 tA0 sA0 tB0 sB0 EB0 QB0 5A JA 5B qB0 JB AB0
"""


class Kernels:
    def __init__(self, place, used, n, rows, cols, channels, block_rows):
        self.place, self.used, self.crops = place, used, len(used)
        self.n, self.rows, self.cols, self.channels, self.block = n, rows, cols, channels, block_rows
        self.held = channels // n
        self.size = rows * self.held
        self.chunks = cols // LANES

    def row_call(self, body, crop, ins, outs, scratch, micros, cols=0, sections=1):
        rows, block = self.rows, self.block

        def spec(kind, shape):
            if kind == "own":
                return pl.BlockSpec(
                    (pl.squeezed, block, LANES, shape[-1]), lambda c, i, s: (s[4 + crop], s[3] * (rows // block) + i, c, 0)
                )
            if kind in ("home 0", "home 1"):
                first = int(kind[-1]) * (rows // block)
                return pl.BlockSpec((pl.squeezed, block, LANES, shape[-1]), lambda c, i, s: (s[4 + crop], first + i, c, 0))
            if kind == "rows":
                return pl.BlockSpec((block, LANES, shape[-1]), lambda c, i, s: (i, c, 0))
            if kind == "moved":
                final = shape[-1] // LANES - 1
                return pl.BlockSpec(shape[:-1] + (LANES,), lambda c, i, s: (0, 0, jnp.minimum(c, final)))
            if kind == "kept":
                return pl.BlockSpec(memory_space=pl.ANY)
            zeros = (0,) * len(shape)
            return pl.BlockSpec(shape, lambda c, i, s: zeros)

        aliases = {1 + k: 0 for k, (kind, _) in enumerate(ins) if kind == "kept"}
        return pl.pallas_call(
            functools.partial(
                body, (self.n, rows, self.held, block, crop, crop == self.crops - 1, self.used[crop], self.chunks)
            ),
            out_shape=tuple(v for _, v in outs),
            grid_spec=pltpu.PrefetchScalarGridSpec(
                num_scalar_prefetch=1,
                grid=(self.chunks, rows // block),
                in_specs=[spec(k, v.shape) for k, v in ins],
                out_specs=tuple(spec(k, v.shape) for k, v in outs),
                scratch_shapes=[pltpu.VMEM(((self.n + 1) * self.size, LANES), F32)] * scratch
                + [pltpu.VMEM((2, self.channels, LANES), F32)] * cols
                + Weights.scratch() * sections,
            ),
            input_output_aliases=aliases,
            compiler_params=pltpu.CompilerParams(vmem_limit_bytes=VMEM),
            cost_estimate=cost(micros),
        )(self.place, *[v for _, v in ins])

    def home(self, section, dtype):
        return (f"home {section}", jax.ShapeDtypeStruct((self.crops, 2 * self.rows, self.cols, self.channels), dtype))

    def pairs(self, dtype):
        return ("rows", jax.ShapeDtypeStruct((self.rows, self.cols, self.channels), dtype))

    def moved(self, crop, count=1):
        return ("moved", jax.ShapeDtypeStruct((self.n, count * self.size, self.used[crop] * LANES), BF16))

    def sums(self, rows):
        return ("all", jax.ShapeDtypeStruct((rows, self.channels), F32))

    def channel_call(self, body, ins, out, scratch, micros):
        spec = pl.BlockSpec(memory_space=pltpu.VMEM)
        return pl.pallas_call(
            functools.partial(body, self.held),
            out_shape=out[1],
            in_specs=[spec] * len(ins),
            out_specs=spec,
            scratch_shapes=[pltpu.VMEM((out[1].shape[2] // LANES, self.n * self.size + 8, LANES), F32)] * scratch,
            compiler_params=pltpu.CompilerParams(vmem_limit_bytes=VMEM),
            cost_estimate=cost(micros),
        )(*ins)


def cost(micros):
    return pl.CostEstimate(flops=int(micros * 1.15e9), bytes_accessed=int(micros * 1e6), transcendentals=0)


def steps(kernels, crops, pair, cot, weights, early, late_share, other_half, meet):
    w = [("all", v) for v in weights]
    call, pairs, moved = kernels.row_call, kernels.pairs, kernels.moved
    up_sums, low_sums = kernels.sums(UP_ROWS), kernels.sums(LOW_ROWS)
    earlier = lambda *names: [("all", state[0][name]) for name in names if name in state[0]]
    homes = {}
    kept = lambda name: [("kept", homes[name])]
    mine = lambda v, crop: [("own", v[0]), ("rows", v[1][crop])]
    part = lambda *vs: [("rows", v) for v in vs]
    far = lambda *vs: [("moved", v) for v in vs]
    swap = lambda v: lax.all_to_all(v, ("row", "grp"), 0, 0)
    spread_rows = lambda v: lax.all_to_all(v, "row", 0, 0)
    state = [dict() for _ in range(crops)]
    last = {}

    def ordered(kind, op, value):
        if kind in last:
            value, _ = lax.optimization_barrier((value, last[kind]))
        result = op(value)
        last[kind] = result[0] if isinstance(result, (tuple, list)) else result
        return result

    def row_kernel(body, crop, ins, *rest):
        return ordered("kernel", lambda v: call(body, crop, [(ins[0][0], v)] + ins[1:], *rest), ins[0][1])

    def channel_kernel(body, ins, *rest):
        return ordered("kernel", lambda v: kernels.channel_call(body, (v,) + tuple(ins[1:]), *rest), ins[0])

    def pre(crop, s):
        s["normed_0"], s["both_0"] = row_kernel(k_pre, crop, mine(pair, crop) + w, [pairs(BF16), moved(crop, 2)], 2, 10)

    def post_pre(crop, s):
        homes["out"], s["out_0"], s["normed_1"], s["both_1"] = row_kernel(
            k_post_pre, crop,
            mine(pair, crop) + mine(pair, crop) + part(s["normed_0"]) + far(s["mixed_0"]) + w + (kept("out") if crop else []),
            [kernels.home(0, BF16), pairs(BF16), pairs(BF16), moved(crop, 2)], 3, 18, 0, 2,
        )
        s["got_out_0"] = other_half(s["out_0"], 0)

    def post_upper(crop, s):
        homes["out"], s["out_1"], s["grad_1"], s["gate_1"], s["grad_mixed_1"], s["up_1"] = row_kernel(
            k_post_upper, crop,
            mine(pair, crop) + mine(cot, crop) + part(s["out_0"], s["normed_1"]) + far(s["mixed_1"]) + w + kept("out")
            + earlier("up_1"),
            [kernels.home(1, BF16), pairs(BF16), pairs(F32), pairs(BF16), moved(crop), up_sums], 1, 23, 1,
        )
        s["got_out_1"] = other_half(s["out_1"], 1)

    def lower_upper(crop, s):
        homes["grad"], s["pair_grad_1"], s["grad_0"], s["gate_0"], s["grad_mixed_0"], s["low_1"], s["up_0"] = row_kernel(
            k_lower_upper, crop,
            mine(pair, crop) + mine(pair, crop) + mine(cot, crop)
            + part(s["out_0"], s["normed_1"], s["grad_1"], s["gate_1"], s["normed_0"])
            + far(s["back_1"], s["mixed_0"]) + w + (kept("grad") if crop else []) + earlier("low_1", "up_0"),
            [kernels.home(1, F32), pairs(F32), pairs(F32), pairs(BF16), moved(crop), low_sums, up_sums], 3, 31, 1, 2,
        )
        s["got_grad_1"] = other_half(s["pair_grad_1"], 1)

    def lower(crop, s):
        homes["grad"], s["pair_grad_0"], s["low_0"], s["late"] = row_kernel(
            k_lower, crop, mine(pair, crop) + part(s["normed_0"], s["grad_0"], s["gate_0"]) + far(s["back_0"]) + w
            + kept("grad") + earlier("low_0"),
            [kernels.home(0, F32), pairs(F32), low_sums, ("all", jax.ShapeDtypeStruct(share_shape(LOW_ROWS), BF16))], 2, 13,
        )
        s["got_grad_0"] = other_half(s["pair_grad_0"], 0)

    def product(crop, s, k):
        s[f"product_{k}"] = channel_kernel(k_product, (s[f"factors_{k}"],), moved(crop), 2, 6)

    def product_back(crop, s, k):
        s[f"grads_{k}"] = channel_kernel(k_product_back, (s[f"g_{k}"], s[f"factors_{k}"]), moved(crop, 2), 3, 12)

    transfers = dict(S=("factors", "both"), M=("mixed", "product"), G=("g", "grad_mixed"), s=("back", "grads"))
    rows_of = {"1": pre, "2": post_pre, "3": post_upper, "4": lower_upper, "5": lower}
    channels_of = {"T": product, "t": product_back}
    for step in STEPS.split():
        what, crop, k = step[0], "AB".index(step[1]), step[2:]
        s = state[crop]
        if what == "E":
            sums = {name: lax.optimization_barrier((s[name], last["kernel"]))[0] for name in ("up_0", "up_1", "low_1")}
            last["kernel"] = s["early"] = early(sums)
        elif what in "QqA":
            if what == "A":
                s["total"] = ordered("swap", spread_rows, late_share(s["share_q"], s["share_Q"]))
            else:
                moved_parts = ordered("swap", spread_rows, s["early" if what == "Q" else "late"])
                s[f"share_{what}"] = jnp.sum(moved_parts.astype(F32), axis=0)
        elif what in "HJ":
            name = "out" if what == "H" else "grad"
            homes[name] = meet(homes[name], crop, s[f"got_{name}_0"], s[f"got_{name}_1"])
            if what == "H":
                last["kernel"] = homes[name]
        elif what in rows_of:
            rows_of[what](crop, s)
        elif what in channels_of:
            channels_of[what](crop, s, k)
        else:
            new, old = transfers[what]
            s[f"{new}_{k}"] = ordered("swap", swap, s[f"{old}_{k}"])

    return state, homes


def share_shape(rows):
    n = lax.axis_size("row")
    return (n, -(-rows // (16 * n)) * 16, LANES)


def early_sums(first, swap, sums):
    early_0 = jnp.concatenate([sums["up_0"], jnp.zeros((LOW_ROWS, LANES), F32)])
    early_1 = jnp.concatenate([sums["up_1"], sums["low_1"]])
    early = jnp.where(first, early_0, early_1) + swap(jnp.where(first, early_1, early_0))
    n, rows, _ = share_shape(early.shape[0])
    rest = jnp.zeros((n * rows - early.shape[0], LANES), F32)
    return jnp.concatenate([early, rest]).astype(BF16).reshape(n, rows, LANES)


def late_share(first, late, early):
    late = jnp.where(first, late, 0.0) + lax.ppermute(late, "grp", [(1, 0)])
    share = jnp.concatenate([early, late]).astype(BF16)
    return jnp.broadcast_to(share[None], (lax.axis_size("row"),) + share.shape)


def plain_steps(n, base, crop_length, pair_0, pair_1, cot_0, cot_1, weights):
    rows, cols = pair_0.shape[:2]
    own_rows = base + jnp.arange(rows)
    mask = (own_rows < crop_length).astype(F32)[:, None, None] * (jnp.arange(cols) < crop_length).astype(F32)[None, :, None]

    def send(*values):
        return swap_rows(jnp.stack([to_channels(v, n) for v in values], axis=1))

    w0, w1 = weights
    state_0 = pair_0.astype(F32)
    normed_0, left, right = pre(state_0, mask, w0)
    lr_0 = send(left, right)
    mixed_0 = from_channels(swap_rows(product(lr_0[:, 0], lr_0[:, 1]))).astype(F32)
    out_0, saved_0 = post(state_0, normed_0, mixed_0, w0)
    state_1 = out_0.astype(F32) + pair_1.astype(F32)
    normed_1, left, right = pre(state_1, mask, w1)
    lr_1 = send(left, right)
    mixed_1 = from_channels(swap_rows(product(lr_1[:, 0], lr_1[:, 1]))).astype(F32)
    out_1, saved_1 = post(state_1, normed_1, mixed_1, w1)
    grad_result, grad_gate, grad_mixed, upper_1 = back_upper(cot_1.astype(F32), saved_1, w1)
    gm = send(grad_mixed)
    glr = swap_rows(jnp.stack(product_back(gm[:, 0], lr_1[:, 0], lr_1[:, 1]), axis=1))
    grad_1, lower_1 = back_lower(
        state_1, normed_1, mask, grad_result, grad_gate, from_channels(glr[:, 0]), from_channels(glr[:, 1]), w1
    )
    grad_final = cot_0.astype(F32) + grad_1.astype(BF16).astype(F32)
    grad_result, grad_gate, grad_mixed, upper_0 = back_upper(grad_final, saved_0, w0)
    gm = send(grad_mixed)
    glr = swap_rows(jnp.stack(product_back(gm[:, 0], lr_0[:, 0], lr_0[:, 1]), axis=1))
    grad_0, lower_0 = back_lower(
        state_0, normed_0, mask, grad_result, grad_gate, from_channels(glr[:, 0]), from_channels(glr[:, 1]), w0
    )
    return out_0, out_1, grad_0, grad_1, {**upper_0, **lower_0}, {**upper_1, **lower_1}


ORDER = ("gain_in", "bias_in", "proj", "gate", "out", "gain_out", "bias_out", "gain_tr", "bias_tr", "up", "down")


def per_device(pair_in, crop_lengths, gain_in, bias_in, proj, gate, out, gain_out, bias_out, gain_tr, bias_tr, up, down, pair_cot):
    own_weights = dict(
        gain_in=gain_in[0], bias_in=bias_in[0], proj=proj[0], gate=gate[0], out=out[0], gain_out=gain_out[0],
        bias_out=bias_out[0], gain_tr=gain_tr[0], bias_tr=bias_tr[0], up=up[0], down=down[0],
    )
    groups, count = lax.axis_size("grp"), lax.axis_size("row")
    crops, rows, cols, channels = pair_in.shape[1:]
    group = lax.axis_index("grp")
    first = group == 0
    base = lax.axis_index("row") * rows
    swap = lambda v: lax.ppermute(v, "grp", [(0, 1), (1, 0)])
    pick = lambda v, i: lax.dynamic_index_in_dim(v, i, 0, keepdims=False)
    n = groups * count
    my_rows = rows // 2
    sizes = channels == LANES and out.shape[1] == LANES and up.shape[2] == 4 * LANES and crops == 2 and groups == 2
    if sizes and rows % 2 == 0 and my_rows % BLOCK_ROWS == 0 and cols % LANES == 0 and channels % n == 0 and n % 8 == 0 and (my_rows * (channels // n)) % 16 == 0:
        before_last = (cols // LANES - 1) * LANES
        swapped = crop_lengths[0] <= before_last
        which = [jnp.where(swapped, 1, 0), jnp.where(swapped, 0, 1)]
        lengths = [crop_lengths[crop] for crop in which]
        place = jnp.stack(lengths + [base + group * my_rows, group] + which).astype(jnp.int32)
        def shared(value):
            other = lambda crop: lax.dynamic_slice(value, (crop, (1 - group) * my_rows, 0, 0), (1, my_rows, cols, channels))
            return value, [swap(other(crop)[0]) for crop in which]

        def meet(home, crop, got_0, got_1):
            half = jnp.where(first, got_0, got_1)[None]
            return lax.dynamic_update_slice(home, half, (which[crop], (1 - group) * my_rows, 0, 0))

        def run(used):
            other_half = lambda value, section: lax.ppermute(value, "grp", [(1 - section, section)])
            pair, own = shared(pair_in[0]), pack_weights(own_weights)
            kernels = Kernels(place, used, n, my_rows, cols, channels, BLOCK_ROWS)
            state, homes = steps(
                kernels, crops, pair, shared(pair_cot[0]), own + tuple(swap(v) for v in own), functools.partial(early_sums, first, swap),
                functools.partial(late_share, first), other_half, meet,
            )
            total, _ = lax.optimization_barrier((state[-1]["total"], homes["grad"]))
            spec = pl.BlockSpec(memory_space=pltpu.VMEM)
            order = ("proj", "gate", "gain_in", "bias_in", "out", "gain_out", "bias_out", "gain_tr", "bias_tr", "up", "down")
            arrays = dict(
                gain_in=gain_in, bias_in=bias_in, proj=proj, gate=gate, out=out, gain_out=gain_out, bias_out=bias_out, gain_tr=gain_tr,
                bias_tr=bias_tr, up=up, down=down,
            )
            results = pl.pallas_call(
                k_results,
                out_shape=[jax.ShapeDtypeStruct(arrays[name].shape, F32) for name in order],
                in_specs=[spec],
                out_specs=[spec] * len(order),
                scratch_shapes=[pltpu.VMEM((s[0] * s[1], LANES), F32) for s in (share_shape(UP_ROWS + LOW_ROWS), share_shape(LOW_ROWS))],
                compiler_params=pltpu.CompilerParams(vmem_limit_bytes=VMEM),
            )(total)
            results = dict(zip(order, results))
            return (homes["out"][None], homes["grad"][None]) + tuple(results[name] for name in ORDER)

        chunks = cols // LANES
        if chunks == 1:
            return run((1, 1))
        return lax.cond(lengths[1] <= before_last, lambda: run((chunks, chunks - 1)), lambda: run((chunks, chunks)))

    other_weights = {k: swap(v) for k, v in own_weights.items()}
    weights = [
        {k: jnp.where(first, own_weights[k], other_weights[k]) for k in ORDER},
        {k: jnp.where(first, other_weights[k], own_weights[k]) for k in ORDER},
    ]

    def both(value):
        own, got = pick(value, group), swap(pick(value, 1 - group))
        return jnp.where(first, own, got), jnp.where(first, got, own)

    def home(value_0, value_1):
        own, got = jnp.where(first, value_0, value_1), swap(jnp.where(first, value_1, value_0))
        return jnp.stack([jnp.where(first, own, got), jnp.where(first, got, own)])[None]

    out_0, out_1, grad_0, grad_1, grads_0, grads_1 = plain_steps(
        count, base, pick(crop_lengths, group), *both(pair_in[0]), *both(pair_cot[0]), weights
    )
    pair_out, pair_grad = home(out_0, out_1), home(grad_0, grad_1)
    mine = {k: jnp.where(first, grads_0[k], grads_1[k]) + swap(jnp.where(first, grads_1[k], grads_0[k])) for k in ORDER}
    summed = lax.psum(mine, "row")
    return (pair_out, pair_grad) + tuple(summed[k][None] for k in ORDER)


def solution(mesh):
    pair = P("grp", None, "row", None, None)
    vector, matrix = P("grp", None), P("grp", None, None)
    weights = (vector, vector, matrix, matrix, matrix, vector, vector, vector, vector, matrix, matrix)
    return jax.shard_map(
        per_device,
        mesh=mesh,
        in_specs=(pair, P()) + weights + (pair,),
        out_specs=(pair, pair) + weights,
        check_vma=False,
    )
```

```python
import functools

import jax
import jax.numpy as jnp
from jax import lax
from jax.experimental import pallas as pl
from jax.experimental.pallas import tpu as pltpu
from jax.sharding import PartitionSpec as P

EPSILON = 1e-05
F32 = jnp.float32
BF16 = jnp.bfloat16


def norm_stats(values):
    mean_value = jnp.mean(values, axis=-1, keepdims=True)
    centred = values - mean_value
    inv_scale = lax.rsqrt(jnp.mean(centred * centred, axis=-1, keepdims=True) + EPSILON)
    return (centred * inv_scale, inv_scale)


def norm_back(grad_scaled, scaled, inv_scale):
    mean_grad = jnp.mean(grad_scaled, axis=-1, keepdims=True)
    mean_cross = jnp.mean(grad_scaled * scaled, axis=-1, keepdims=True)
    return inv_scale * (grad_scaled - mean_grad - scaled * mean_cross)


def dot(a, b):
    return jnp.dot(a, b, preferred_element_type=F32)


def dot_t(a, b):
    return jnp.einsum("ijf,cf->ijc", a, b, preferred_element_type=F32)


def outer(a, b):
    return jnp.einsum("ijc,ijf->cf", a, b, preferred_element_type=F32)


def to_channels(value, n):
    rows, cols, channels = value.shape
    return jnp.transpose(value, (2, 0, 1)).reshape(n, channels // n, rows, cols)


def from_channels(value):
    n, held, rows, cols = value.shape
    return jnp.transpose(value.reshape(n * held, rows, cols), (1, 2, 0))


def swap_rows(value):
    return lax.all_to_all(value, "row", 0, 0)


def pre(state, mask, w):
    scaled, _ = norm_stats(state)
    normed = (scaled * w["gain_in"] + w["bias_in"]).astype(BF16)
    projected = dot(normed, w["proj"])
    width = projected.shape[-1] // 4
    lv, lg, rv, rg = (projected[..., i * width : (i + 1) * width] for i in range(4))
    left = (jax.nn.sigmoid(lg) * lv * mask).astype(BF16)
    right = (jax.nn.sigmoid(rg) * rv * mask).astype(BF16)
    return normed, left, right


def post(state, normed, mixed, w):
    gate_logit = dot(normed, w["gate"])
    scaled_mid, inv_mid = norm_stats(mixed)
    mixed_norm = (scaled_mid * w["gain_out"] + w["bias_out"]).astype(BF16)
    update = dot(mixed_norm, w["out"])
    gate_sigma = jax.nn.sigmoid(gate_logit)
    first_state = state + gate_sigma * update
    scaled_tr, inv_tr = norm_stats(first_state)
    trans_normed = (scaled_tr * w["gain_tr"] + w["bias_tr"]).astype(BF16)
    hidden = dot(trans_normed, w["up"])
    activated = jax.nn.silu(hidden).astype(BF16)
    result = (first_state + dot(activated, w["down"])).astype(BF16)
    saved = (gate_sigma, scaled_mid, inv_mid, mixed_norm, update, scaled_tr, inv_tr, trans_normed, hidden, activated)
    return result, saved


def back_upper(grad_final, saved, w):
    gate_sigma, scaled_mid, inv_mid, mixed_norm, update, scaled_tr, inv_tr, trans_normed, hidden, activated = saved
    grads = {}
    grad_trans = grad_final.astype(BF16)
    grads["down"] = outer(activated, grad_trans)
    grad_act = dot_t(grad_trans, w["down"])
    sigma = jax.nn.sigmoid(hidden)
    grad_hidden = (grad_act * sigma * (1.0 + hidden * (1.0 - sigma))).astype(BF16)
    grads["up"] = outer(trans_normed, grad_hidden)
    grad_tnorm = dot_t(grad_hidden, w["up"])
    grads["gain_tr"] = jnp.sum(grad_tnorm * scaled_tr, axis=(0, 1))
    grads["bias_tr"] = jnp.sum(grad_tnorm, axis=(0, 1))
    grad_result = grad_final + norm_back(grad_tnorm * w["gain_tr"], scaled_tr, inv_tr)
    grad_update = (grad_result * gate_sigma).astype(BF16)
    grad_gate = (grad_result * update * gate_sigma * (1.0 - gate_sigma)).astype(BF16)
    grads["out"] = outer(mixed_norm, grad_update)
    grad_norm_mid = dot_t(grad_update, w["out"])
    grads["gain_out"] = jnp.sum(grad_norm_mid * scaled_mid, axis=(0, 1))
    grads["bias_out"] = jnp.sum(grad_norm_mid, axis=(0, 1))
    grad_mixed = norm_back(grad_norm_mid * w["gain_out"], scaled_mid, inv_mid).astype(BF16)
    return grad_result, grad_gate, grad_mixed, grads


def back_lower(state, normed, mask, grad_result, grad_gate, grad_left, grad_right, w):
    scaled_in, inv_in = norm_stats(state)
    projected = dot(normed, w["proj"])
    width = projected.shape[-1] // 4
    lv, lg, rv, rg = (projected[..., i * width : (i + 1) * width] for i in range(4))
    ls = jax.nn.sigmoid(lg)
    rs = jax.nn.sigmoid(rg)
    gl = grad_left.astype(F32) * mask
    gr = grad_right.astype(F32) * mask
    grad_proj = jnp.concatenate(
        [gl * ls, gl * lv * ls * (1.0 - ls), gr * rs, gr * rv * rs * (1.0 - rs)], axis=-1
    ).astype(BF16)
    grads = {"proj": outer(normed, grad_proj), "gate": outer(normed, grad_gate)}
    grad_normed = dot_t(grad_proj, w["proj"]) + dot_t(grad_gate, w["gate"])
    grads["gain_in"] = jnp.sum(grad_normed * scaled_in, axis=(0, 1))
    grads["bias_in"] = jnp.sum(grad_normed, axis=(0, 1))
    return grad_result + norm_back(grad_normed * w["gain_in"], scaled_in, inv_in), grads


def product(left, right):
    n, held, rows, cols = left.shape
    mixed = jnp.einsum("atik,btjk->taibj", left, right, preferred_element_type=F32)
    return jnp.transpose(mixed.reshape(held, n, rows, n * rows), (1, 0, 2, 3)).astype(BF16)


def product_back(grad_mixed, left, right):
    n, held, rows, cols = left.shape
    split = grad_mixed.reshape(n, held, rows, n, rows)
    grad_left = jnp.einsum("atibj,btjk->atik", split, right, preferred_element_type=F32)
    grad_right = jnp.einsum("atibj,atik->btjk", split, left, preferred_element_type=F32)
    return grad_left.astype(BF16), grad_right.astype(BF16)


BLOCK_ROWS = 12
LANES = 128
VMEM = 62 << 20


def sig(x):
    return 0.5 * jnp.tanh(0.5 * x) + 0.5


def mm(a, b, ca=1, cb=0):
    return lax.dot_general(a, b, (((ca,), (cb,)), ((), ())), preferred_element_type=F32)


def col_stats(values):
    centred = values - jnp.mean(values, axis=0, keepdims=True)
    inv_scale = lax.rsqrt(jnp.mean(centred * centred, axis=0, keepdims=True) + EPSILON)
    return centred * inv_scale, inv_scale


def col_back(grad_scaled, scaled, inv_scale):
    mean_grad = jnp.mean(grad_scaled, axis=0, keepdims=True)
    mean_cross = jnp.mean(grad_scaled * scaled, axis=0, keepdims=True)
    return inv_scale * (grad_scaled - mean_grad - scaled * mean_cross)


def fold(values):
    return jnp.sum(values.reshape(values.shape[0] // 8, 8, values.shape[1]), axis=0)


class Step:
    def __init__(self, place, n, rows, held, block_rows, crop, last, used, chunks):
        self.last = last
        self.live = pl.program_id(0) < used if used < chunks else None
        self.n, self.rows, self.held, self.block = n, rows, held, block_rows
        self.row = pl.program_id(1) * block_rows
        self.length, self.base, self.group = place[crop], place[2], place[3]
        column = pl.program_id(0) * LANES + lax.broadcasted_iota(jnp.int32, (1, LANES), 1)
        self.columns = (column < self.length).astype(F32)

    def mask(self, r):
        return self.columns * jnp.where(self.base + self.row + r < self.length, 1.0, 0.0)

    def flat(self, ref):
        return ref[...].reshape(self.block * LANES, ref.shape[-1])

    def pick(self, pair, section):
        own, got = (self.flat(ref).astype(F32) for ref in pair)
        return jnp.where(jnp.full(own.shape, self.group) == section, own, got)

    def put(self, ref, value):
        ref[...] = value.reshape(self.block, LANES, value.shape[-1]).astype(ref.dtype)

    def lanes(self, r):
        return slice(r * LANES, (r + 1) * LANES)

    def spans(self, r):
        return [pl.ds((self.row + r) * self.held + t, self.n, stride=self.rows * self.held) for t in range(self.held)]

    def load(self, scratch, r):
        return jnp.concatenate([scratch[span, :] for span in self.spans(r)], axis=0)

    def store(self, scratch, r, value):
        for t, span in enumerate(self.spans(r)):
            scratch[span, :] = value[t * self.n : (t + 1) * self.n, :]


def unpack(ref, scratch, first=0):
    n, size = ref.shape[0], scratch.shape[0] // (ref.shape[0] + 1)

    def body(d, carry):
        scratch[pl.ds(pl.multiple_of(d * size, 8), size), :] = ref[d, first : first + size, :].astype(F32)
        return carry

    lax.fori_loop(0, n, body, 0)


def pack(scratch, ref, first=0):
    n, size = ref.shape[0], scratch.shape[0] // (ref.shape[0] + 1)

    def body(d, carry):
        ref[d, first : first + size, :] = scratch[pl.ds(pl.multiple_of(d * size, 8), size), :].astype(ref.dtype)
        return carry

    lax.fori_loop(0, n, body, 0)


def fetch(st, ref, scratch, first=0):
    if st.live is None:
        return unpack(ref, scratch, first)

    @pl.when(st.live)
    def _():
        unpack(ref, scratch, first)

    @pl.when(jnp.logical_not(st.live))
    def _():
        scratch[...] = jnp.zeros(scratch.shape, scratch.dtype)


def deliver(st, scratch, ref, first=0):
    if st.live is None:
        return pack(scratch, ref, first)
    pl.when(st.live)(lambda: pack(scratch, ref, first))


def at_first(action):
    pl.when(pl.program_id(1) == 0)(action)


def at_last(action):
    pl.when(pl.program_id(1) == pl.num_programs(1) - 1)(action)


def clear(accs, olds, cols=()):
    @pl.when((pl.program_id(0) == 0) & (pl.program_id(1) == 0))
    def _():
        for k, ref in enumerate(accs):
            ref[...] = olds[k][...] if olds else jnp.zeros(ref.shape, ref.dtype)
        for ref in cols:
            ref[...] = jnp.zeros(ref.shape, ref.dtype)


def add_blocks(ref, first, value):
    for q in range(value.shape[1] // LANES):
        ref[first + q * LANES : first + (q + 1) * LANES, :] += value[:, q * LANES : (q + 1) * LANES]


def close(st, ref, cols=None):
    @pl.when((pl.program_id(0) == pl.num_programs(0) - 1) & (pl.program_id(1) == pl.num_programs(1) - 1))
    def _():
        for k in range(2 if cols is not None else 0):
            row = UP_VEC + 16 + 8 * k
            ref[row : row + 1, :] += jnp.sum(jnp.transpose(cols[k]), axis=0, keepdims=True)
        for q in range(4 if st.last else 0):
            block = slice(q * LANES, (q + 1) * LANES)
            ref[block, :] = jnp.transpose(ref[block, :])


def pre_part(st, state, w, normed_ref, left_scr, right_scr):
    scaled, _ = norm_stats(state)
    normed = (scaled * w.vec[0:1, :] + w.vec[1:2, :]).astype(BF16)
    st.put(normed_ref, normed)
    projected = mm(w.proj_t[...], normed, 1, 1)
    for r in range(st.block):
        lv, lg, rv, rg = (projected[q * LANES : (q + 1) * LANES, st.lanes(r)] for q in range(4))
        mask = st.mask(r)
        st.store(left_scr, r, sig(lg) * lv * mask)
        st.store(right_scr, r, sig(rg) * rv * mask)


def post_part(st, state, normed, mixed_scr, w):
    mids = [col_stats(st.load(mixed_scr, r)) for r in range(st.block)]
    gain, bias = w.col[0], w.col[1]
    mixed_norm = jnp.concatenate([(scaled * gain + bias).astype(BF16) for scaled, _ in mids], axis=1)
    update = mm(mixed_norm, w.out[...], 0, 0)
    gate = sig(mm(normed, w.gate[...]))
    first_state = state + gate * update
    scaled_tr, inv_tr = norm_stats(first_state)
    trans = (scaled_tr * w.vec[2:3, :] + w.vec[3:4, :]).astype(BF16)
    hidden = mm(trans, w.up[...])
    sigma = sig(hidden)
    activated = (hidden * sigma).astype(BF16)
    return mids, mixed_norm, update, gate, first_state, scaled_tr, inv_tr, trans, hidden, sigma, activated


def upper_part(st, grad_final, kept, w, acc, cols, grad_ref, gate_ref, mixed_scr):
    mids, mixed_norm, update, gate, first_state, scaled_tr, inv_tr, trans, hidden, sigma, activated = kept
    low = grad_final.astype(BF16)
    add_blocks(acc, 0, mm(low, activated, 0, 0))
    grad_hidden = (mm(low, w.down[...], 1, 1) * (sigma * (1.0 + hidden * (1.0 - sigma)))).astype(BF16)
    add_blocks(acc, 4 * LANES, mm(trans, grad_hidden, 0, 0))
    grad_tnorm = mm(grad_hidden, w.up[...], 1, 1)
    acc[UP_VEC : UP_VEC + 8, :] += fold(grad_tnorm * scaled_tr)
    acc[UP_VEC + 8 : UP_VEC + 16, :] += fold(grad_tnorm)
    grad_result = grad_final + norm_back(grad_tnorm * w.vec[2:3, :], scaled_tr, inv_tr)
    st.put(grad_ref, grad_result)
    scaled_grad = grad_result * gate
    grad_update = scaled_grad.astype(BF16)
    st.put(gate_ref, scaled_grad * update * (1.0 - gate))
    add_blocks(acc, 8 * LANES, mm(mixed_norm, grad_update))
    grad_norm = mm(w.out[...], grad_update, 1, 1)
    for r, (scaled, inv_scale) in enumerate(mids):
        grad = grad_norm[:, st.lanes(r)]
        cols[0] += grad * scaled
        cols[1] += grad
        st.store(mixed_scr, r, col_back(grad * w.col[0], scaled, inv_scale) * st.mask(r))


def lower_part(st, state, normed, grad_result, grad_gate, left_scr, right_scr, w, acc):
    projected = mm(w.proj_t[...], normed, 1, 1)
    parts = []
    for r in range(st.block):
        lv, lg, rv, rg = (projected[q * LANES : (q + 1) * LANES, st.lanes(r)] for q in range(4))
        ls, rs = sig(lg), sig(rg)
        a, b = st.load(left_scr, r) * ls, st.load(right_scr, r) * rs
        parts.append(jnp.concatenate([v.astype(BF16) for v in (a, a * lv * (1.0 - ls), b, b * rv * (1.0 - rs))], axis=0))
    grad_proj = jnp.concatenate(parts, axis=1)
    acc[: 4 * LANES, :] += mm(grad_proj, normed)
    add_blocks(acc, 4 * LANES, mm(normed, grad_gate, 0, 0))
    grad_normed = jnp.transpose(mm(w.proj[...], grad_proj)) + mm(grad_gate, w.gate[...], 1, 1)
    scaled_in, inv_in = norm_stats(state)
    acc[LOW_VEC : LOW_VEC + 8, :] += fold(grad_normed * scaled_in)
    acc[LOW_VEC + 8 : LOW_VEC + 16, :] += fold(grad_normed)
    return grad_result + norm_back(grad_normed * w.vec[0:1, :], scaled_in, inv_in)


class Weights:
    def __init__(self, group, section, refs, scratch):
        self.wide, self.down, self.vec, self.col, self.proj_t = scratch
        cut = lambda first, count: self.wide.at[:, first * LANES : (first + count) * LANES]
        self.proj, self.gate, self.out, self.up = cut(0, 4), cut(4, 1), cut(5, 1), cut(6, 4)

        @pl.when((pl.program_id(0) == 0) & (pl.program_id(1) == 0))
        def _():
            for chosen, sources in ((group == section, refs[:3]), (group != section, refs[3:])):

                @pl.when(chosen)
                def _():
                    for ref, source in zip((self.wide, self.down, self.vec), sources):
                        ref[...] = source[...]

            for k in range(2):
                self.col[k] = jnp.transpose(jnp.broadcast_to(self.vec[4 + k : 5 + k, :], (LANES, LANES)))
            for q in range(4):
                block = slice(q * LANES, (q + 1) * LANES)
                self.proj_t[block, :] = jnp.transpose(self.wide[:, block])

    @staticmethod
    def scratch():
        return [
            pltpu.VMEM((LANES, 10 * LANES), BF16), pltpu.VMEM((4 * LANES, LANES), BF16), pltpu.VMEM((8, LANES), F32),
            pltpu.VMEM((2, LANES, LANES), F32), pltpu.VMEM((4 * LANES, LANES), BF16),
        ]


def pack_weights(w):
    zero = jnp.zeros_like(w["gain_in"])
    names = ("gain_in", "bias_in", "gain_tr", "bias_tr", "gain_out", "bias_out")
    wide = jnp.concatenate([w[name] for name in ("proj", "gate", "out", "up")], axis=1)
    return wide, w["down"], jnp.stack([w[name] for name in names] + [zero, zero])


UP_VEC = 9 * LANES
UP_ROWS = UP_VEC + 32
LOW_VEC = 5 * LANES
LOW_ROWS = LOW_VEC + 16


def k_pre(cfg, place, own, got, *refs):
    st = Step(place, *cfg)
    w = Weights(st.group, 0, refs[:6], refs[-5:])
    normed, both, left, right = refs[6:-5]
    pre_part(st, st.pick((own, got), 0), w, normed, left, right)

    @at_last
    def _():
        deliver(st, left, both)
        deliver(st, right, both, both.shape[1] // 2)


def k_post_pre(cfg, place, own_0, got_0, own_1, got_1, normed_in, mixed_in, *refs):
    st = Step(place, *cfg)
    w0, w1 = Weights(st.group, 0, refs[:6], refs[-10:-5]), Weights(st.group, 1, refs[:6], refs[-5:])
    *_, home, out, normed, both, mixed, left, right = refs[6:-10]
    at_first(lambda: fetch(st, mixed_in, mixed))
    kept = post_part(st, st.pick((own_0, got_0), 0), st.flat(normed_in), mixed, w0)
    result = (kept[4] + mm(kept[-1], w0.down[...])).astype(BF16)
    st.put(home, result)
    st.put(out, result)
    pre_part(st, result.astype(F32) + st.pick((own_1, got_1), 1), w1, normed, left, right)

    @at_last
    def _():
        deliver(st, left, both)
        deliver(st, right, both, both.shape[1] // 2)


def k_post_upper(cfg, place, own, got, own_cot, got_cot, before, normed_in, mixed_in, *refs):
    st = Step(place, *cfg)
    w = Weights(st.group, 1, refs[:6], refs[-5:])
    _, *olds, home, out, grad, gate, grad_mixed, sums, mixed, cols = refs[6:-5]
    clear([sums], olds, [cols])
    at_first(lambda: fetch(st, mixed_in, mixed))
    state = st.flat(before).astype(F32) + st.pick((own, got), 1)
    kept = post_part(st, state, st.flat(normed_in), mixed, w)
    result = kept[4] + mm(kept[-1], w.down[...])
    st.put(home, result)
    st.put(out, result)
    upper_part(st, st.pick((own_cot, got_cot), 1), kept, w, sums, cols, grad, gate, mixed)
    close(st, sums, cols)
    at_last(lambda: deliver(st, mixed, grad_mixed))


def k_lower_upper(
    cfg, place, own_1, got_1, own_0, got_0, own_cot, got_cot, before, normed_1, grad_1, gate_1, normed_0, both, mixed_in, *refs
):
    st = Step(place, *cfg)
    w1, w0 = Weights(st.group, 1, refs[:6], refs[-10:-5]), Weights(st.group, 0, refs[:6], refs[-5:])
    olds = refs[7:9] if cfg[4] else ()
    home, pair_grad, grad, gate, grad_mixed, low_sums, up_sums, left, right, mixed, cols = refs[-21:-10]
    clear([low_sums, up_sums], olds, [cols])

    @at_first
    def _():
        fetch(st, both, left)
        fetch(st, both, right, both.shape[1] // 2)
        fetch(st, mixed_in, mixed)

    state = st.flat(before).astype(F32) + st.pick((own_1, got_1), 1)
    grad_state = lower_part(
        st, state, st.flat(normed_1), st.flat(grad_1), st.flat(gate_1), left, right, w1, low_sums
    )
    st.put(home, grad_state)
    st.put(pair_grad, grad_state)
    kept = post_part(st, st.pick((own_0, got_0), 0), st.flat(normed_0), mixed, w0)
    grad_final = st.pick((own_cot, got_cot), 0) + grad_state.astype(BF16).astype(F32)
    upper_part(st, grad_final, kept, w0, up_sums, cols, grad, gate, mixed)
    close(st, low_sums)
    close(st, up_sums, cols)
    at_last(lambda: deliver(st, mixed, grad_mixed))


def k_lower(cfg, place, own, got, normed, grad, gate, both, *refs):
    st = Step(place, *cfg)
    w = Weights(st.group, 0, refs[:6], refs[-5:])
    _, *olds, home, pair_grad, sums, parts, left, right = refs[6:-5]
    clear([sums], olds)

    @at_first
    def _():
        fetch(st, both, left)
        fetch(st, both, right, both.shape[1] // 2)

    state = st.pick((own, got), 0)
    grad_state = lower_part(
        st, state, st.flat(normed), st.flat(grad), st.flat(gate), left, right, w, sums
    )
    st.put(home, grad_state)
    st.put(pair_grad, grad_state)
    close(st, sums)

    @pl.when((pl.program_id(0) == pl.num_programs(0) - 1) & (pl.program_id(1) == pl.num_programs(1) - 1))
    def _():
        n, rows, _ = parts.shape
        parts[...] = jnp.zeros(parts.shape, BF16)
        for d in range(n):
            count = max(0, min(rows, LOW_ROWS - d * rows))
            if count:
                parts[d, :count, :] = sums[d * rows : d * rows + count, :].astype(BF16)


def k_results(total, proj, gate, gain_in, bias_in, out, gain_out, bias_out, gain_tr, bias_tr, up, down, early, low):
    n = total.shape[0]
    first, second = early.shape[0] // n, low.shape[0] // n
    for d in range(n):
        early[d * first : (d + 1) * first, :] = total[d, :first, :].astype(F32)
        low[d * second : (d + 1) * second, :] = total[d, first:, :].astype(F32)
    down[0] = early[: 4 * LANES, :]
    for q in range(4):
        up[0, :, q * LANES : (q + 1) * LANES] = early[(4 + q) * LANES : (5 + q) * LANES, :]
        proj[0, :, q * LANES : (q + 1) * LANES] = low[q * LANES : (q + 1) * LANES, :]
    out[0] = early[8 * LANES : UP_VEC, :]
    gate[0] = low[4 * LANES : LOW_VEC, :]
    for k, ref in enumerate((gain_tr, bias_tr, gain_out, bias_out)):
        ref[...] = jnp.sum(early[UP_VEC + 8 * k : UP_VEC + 8 * k + 8, :], axis=0, keepdims=True)
    for k, ref in enumerate((gain_in, bias_in)):
        ref[...] = jnp.sum(low[LOW_VEC + 8 * k : LOW_VEC + 8 * k + 8, :], axis=0, keepdims=True)


def spread(ref, scratch, first=0):
    n, size = ref.shape[0], (scratch.shape[1] - 8) // ref.shape[0]

    def body(d, carry):
        for c in range(scratch.shape[0]):
            value = ref[d, first : first + size, c * LANES : (c + 1) * LANES]
            scratch[c, pl.ds(pl.multiple_of(d * size, 8), size), :] = value.astype(F32)
        return carry

    lax.fori_loop(0, n, body, 0)


def gather(scratch, ref, first=0):
    n, size = ref.shape[0], (scratch.shape[1] - 8) // ref.shape[0]

    def body(d, carry):
        for c in range(scratch.shape[0]):
            value = scratch[c, pl.ds(pl.multiple_of(d * size, 8), size), :]
            ref[d, first : first + size, c * LANES : (c + 1) * LANES] = value.astype(ref.dtype)
        return carry

    lax.fori_loop(0, n, body, 0)


def channel(scratch, t, held):
    chunks, size, _ = scratch.shape
    span = pl.ds(t, (size - 8) // held, stride=held)
    return jnp.concatenate([scratch[c, span, :].astype(BF16) for c in range(chunks)], axis=1)


def put_channel(scratch, t, held, value):
    chunks, size, _ = scratch.shape
    span = pl.ds(t, (size - 8) // held, stride=held)
    for c in range(chunks):
        scratch[c, span, :] = value[:, c * LANES : (c + 1) * LANES]


def k_product(held, both, out, left, right):
    spread(both, left)
    spread(both, right, both.shape[1] // 2)

    def body(t, carry):
        others = channel(right, t, held)[: left.shape[0] * LANES]
        put_channel(left, t, held, mm(channel(left, t, held), others, 1, 1))
        return carry

    lax.fori_loop(0, held, body, 0)
    gather(left, out)


def k_product_back(held, grad_in, both, out, grad, left, right):
    spread(grad_in, grad)
    spread(both, left)
    spread(both, right, both.shape[1] // 2)

    def body(t, carry):
        low, lv, rv = channel(grad, t, held), channel(left, t, held), channel(right, t, held)
        put_channel(left, t, held, mm(low, rv[: low.shape[1]]))
        grad_right = mm(low, lv, 0, 0)
        if low.shape[1] < rv.shape[0]:
            rest = jnp.zeros((rv.shape[0] - low.shape[1], lv.shape[1]), F32)
            grad_right = jnp.concatenate([grad_right, rest])
        put_channel(right, t, held, grad_right)
        return carry

    lax.fori_loop(0, held, body, 0)
    gather(left, out)
    gather(right, out, both.shape[1] // 2)


STEPS = """\
1A SA0 1B SB0 TA0 MA0 TB0 MB0 2A SA1 2B SB1 TA1 MA1 TB1 MB1 3A GA1 3B GB1 tA1 sA1 tB1 sB1 HA HB 4A GA0 4B GB0 tA0 sA0 tB0 sB0 EB0 QB0 5A JA 5B qB0 JB AB0
"""


class Kernels:
    def __init__(self, place, used, n, rows, cols, channels, block_rows):
        self.place, self.used, self.crops = place, used, len(used)
        self.n, self.rows, self.cols, self.channels, self.block = n, rows, cols, channels, block_rows
        self.held = channels // n
        self.size = rows * self.held
        self.chunks = cols // LANES

    def row_call(self, body, crop, ins, outs, scratch, micros, cols=0, sections=1):
        rows, block = self.rows, self.block

        def spec(kind, shape):
            if kind == "own":
                return pl.BlockSpec(
                    (pl.squeezed, block, LANES, shape[-1]), lambda c, i, s: (s[4 + crop], s[3] * (rows // block) + i, c, 0)
                )
            if kind in ("home 0", "home 1"):
                first = int(kind[-1]) * (rows // block)
                return pl.BlockSpec((pl.squeezed, block, LANES, shape[-1]), lambda c, i, s: (s[4 + crop], first + i, c, 0))
            if kind == "rows":
                return pl.BlockSpec((block, LANES, shape[-1]), lambda c, i, s: (i, c, 0))
            if kind == "moved":
                final = shape[-1] // LANES - 1
                return pl.BlockSpec(shape[:-1] + (LANES,), lambda c, i, s: (0, 0, jnp.minimum(c, final)))
            if kind == "kept":
                return pl.BlockSpec(memory_space=pl.ANY)
            zeros = (0,) * len(shape)
            return pl.BlockSpec(shape, lambda c, i, s: zeros)

        aliases = {1 + k: 0 for k, (kind, _) in enumerate(ins) if kind == "kept"}
        return pl.pallas_call(
            functools.partial(
                body, (self.n, rows, self.held, block, crop, crop == self.crops - 1, self.used[crop], self.chunks)
            ),
            out_shape=tuple(v for _, v in outs),
            grid_spec=pltpu.PrefetchScalarGridSpec(
                num_scalar_prefetch=1,
                grid=(self.chunks, rows // block),
                in_specs=[spec(k, v.shape) for k, v in ins],
                out_specs=tuple(spec(k, v.shape) for k, v in outs),
                scratch_shapes=[pltpu.VMEM(((self.n + 1) * self.size, LANES), F32)] * scratch
                + [pltpu.VMEM((2, self.channels, LANES), F32)] * cols
                + Weights.scratch() * sections,
            ),
            input_output_aliases=aliases,
            compiler_params=pltpu.CompilerParams(vmem_limit_bytes=VMEM),
            cost_estimate=cost(micros),
        )(self.place, *[v for _, v in ins])

    def home(self, section, dtype):
        return (f"home {section}", jax.ShapeDtypeStruct((self.crops, 2 * self.rows, self.cols, self.channels), dtype))

    def pairs(self, dtype):
        return ("rows", jax.ShapeDtypeStruct((self.rows, self.cols, self.channels), dtype))

    def moved(self, crop, count=1):
        return ("moved", jax.ShapeDtypeStruct((self.n, count * self.size, self.used[crop] * LANES), BF16))

    def sums(self, rows):
        return ("all", jax.ShapeDtypeStruct((rows, self.channels), F32))

    def channel_call(self, body, ins, out, scratch, micros):
        spec = pl.BlockSpec(memory_space=pltpu.VMEM)
        return pl.pallas_call(
            functools.partial(body, self.held),
            out_shape=out[1],
            in_specs=[spec] * len(ins),
            out_specs=spec,
            scratch_shapes=[pltpu.VMEM((out[1].shape[2] // LANES, self.n * self.size + 8, LANES), F32)] * scratch,
            compiler_params=pltpu.CompilerParams(vmem_limit_bytes=VMEM),
            cost_estimate=cost(micros),
        )(*ins)


def cost(micros):
    return pl.CostEstimate(flops=int(micros * 1.15e9), bytes_accessed=int(micros * 1e6), transcendentals=0)


def steps(kernels, crops, pair, cot, weights, early, late_share, other_half, meet):
    w = [("all", v) for v in weights]
    call, pairs, moved = kernels.row_call, kernels.pairs, kernels.moved
    up_sums, low_sums = kernels.sums(UP_ROWS), kernels.sums(LOW_ROWS)
    earlier = lambda *names: [("all", state[0][name]) for name in names if name in state[0]]
    homes = {}
    kept = lambda name: [("kept", homes[name])]
    mine = lambda v, crop: [("own", v[0]), ("rows", v[1][crop])]
    part = lambda *vs: [("rows", v) for v in vs]
    far = lambda *vs: [("moved", v) for v in vs]
    swap = lambda v: lax.all_to_all(v, ("row", "grp"), 0, 0)
    spread_rows = lambda v: lax.all_to_all(v, "row", 0, 0)
    state = [dict() for _ in range(crops)]
    last = {}

    def ordered(kind, op, value):
        if kind in last:
            value, _ = lax.optimization_barrier((value, last[kind]))
        result = op(value)
        last[kind] = result[0] if isinstance(result, (tuple, list)) else result
        return result

    def row_kernel(body, crop, ins, *rest):
        return ordered("kernel", lambda v: call(body, crop, [(ins[0][0], v)] + ins[1:], *rest), ins[0][1])

    def channel_kernel(body, ins, *rest):
        return ordered("kernel", lambda v: kernels.channel_call(body, (v,) + tuple(ins[1:]), *rest), ins[0])

    def pre(crop, s):
        s["normed_0"], s["both_0"] = row_kernel(k_pre, crop, mine(pair, crop) + w, [pairs(BF16), moved(crop, 2)], 2, 10)

    def post_pre(crop, s):
        homes["out"], s["out_0"], s["normed_1"], s["both_1"] = row_kernel(
            k_post_pre, crop,
            mine(pair, crop) + mine(pair, crop) + part(s["normed_0"]) + far(s["mixed_0"]) + w + (kept("out") if crop else []),
            [kernels.home(0, BF16), pairs(BF16), pairs(BF16), moved(crop, 2)], 3, 18, 0, 2,
        )
        s["got_out_0"] = other_half(s["out_0"], 0)

    def post_upper(crop, s):
        homes["out"], s["out_1"], s["grad_1"], s["gate_1"], s["grad_mixed_1"], s["up_1"] = row_kernel(
            k_post_upper, crop,
            mine(pair, crop) + mine(cot, crop) + part(s["out_0"], s["normed_1"]) + far(s["mixed_1"]) + w + kept("out")
            + earlier("up_1"),
            [kernels.home(1, BF16), pairs(BF16), pairs(F32), pairs(BF16), moved(crop), up_sums], 1, 23, 1,
        )
        s["got_out_1"] = other_half(s["out_1"], 1)

    def lower_upper(crop, s):
        homes["grad"], s["pair_grad_1"], s["grad_0"], s["gate_0"], s["grad_mixed_0"], s["low_1"], s["up_0"] = row_kernel(
            k_lower_upper, crop,
            mine(pair, crop) + mine(pair, crop) + mine(cot, crop)
            + part(s["out_0"], s["normed_1"], s["grad_1"], s["gate_1"], s["normed_0"])
            + far(s["back_1"], s["mixed_0"]) + w + (kept("grad") if crop else []) + earlier("low_1", "up_0"),
            [kernels.home(1, F32), pairs(F32), pairs(F32), pairs(BF16), moved(crop), low_sums, up_sums], 3, 31, 1, 2,
        )
        s["got_grad_1"] = other_half(s["pair_grad_1"], 1)

    def lower(crop, s):
        homes["grad"], s["pair_grad_0"], s["low_0"], s["late"] = row_kernel(
            k_lower, crop, mine(pair, crop) + part(s["normed_0"], s["grad_0"], s["gate_0"]) + far(s["back_0"]) + w
            + kept("grad") + earlier("low_0"),
            [kernels.home(0, F32), pairs(F32), low_sums, ("all", jax.ShapeDtypeStruct(share_shape(LOW_ROWS), BF16))], 2, 13,
        )
        s["got_grad_0"] = other_half(s["pair_grad_0"], 0)

    def product(crop, s, k):
        s[f"product_{k}"] = channel_kernel(k_product, (s[f"factors_{k}"],), moved(crop), 2, 6)

    def product_back(crop, s, k):
        s[f"grads_{k}"] = channel_kernel(k_product_back, (s[f"g_{k}"], s[f"factors_{k}"]), moved(crop, 2), 3, 12)

    transfers = dict(S=("factors", "both"), M=("mixed", "product"), G=("g", "grad_mixed"), s=("back", "grads"))
    rows_of = {"1": pre, "2": post_pre, "3": post_upper, "4": lower_upper, "5": lower}
    channels_of = {"T": product, "t": product_back}
    for step in STEPS.split():
        what, crop, k = step[0], "AB".index(step[1]), step[2:]
        s = state[crop]
        if what == "E":
            sums = {name: lax.optimization_barrier((s[name], last["kernel"]))[0] for name in ("up_0", "up_1", "low_1")}
            last["kernel"] = s["early"] = early(sums)
        elif what in "QqA":
            if what == "A":
                s["total"] = ordered("swap", spread_rows, late_share(s["share_q"], s["share_Q"]))
            else:
                moved_parts = ordered("swap", spread_rows, s["early" if what == "Q" else "late"])
                s[f"share_{what}"] = jnp.sum(moved_parts.astype(F32), axis=0)
        elif what in "HJ":
            name = "out" if what == "H" else "grad"
            homes[name] = meet(homes[name], crop, s[f"got_{name}_0"], s[f"got_{name}_1"])
            if what == "H":
                last["kernel"] = homes[name]
        elif what in rows_of:
            rows_of[what](crop, s)
        elif what in channels_of:
            channels_of[what](crop, s, k)
        else:
            new, old = transfers[what]
            s[f"{new}_{k}"] = ordered("swap", swap, s[f"{old}_{k}"])

    return state, homes


def share_shape(rows):
    n = lax.axis_size("row")
    return (n, -(-rows // (16 * n)) * 16, LANES)


def in_shares(sums):
    n, rows, _ = share_shape(sums.shape[0])
    return jnp.pad(sums, ((0, n * rows - sums.shape[0]), (0, 0))).reshape(n, rows, LANES)


def early_sums(first, swap, sums):
    early_0 = jnp.concatenate([sums["up_0"], jnp.zeros((LOW_ROWS, LANES), F32)])
    early_1 = jnp.concatenate([sums["up_1"], sums["low_1"]])
    early = jnp.where(first, early_0, early_1) + swap(jnp.where(first, early_1, early_0))
    return jnp.concatenate([in_shares(early[:UP_ROWS]), in_shares(early[UP_ROWS:])], axis=1).astype(BF16)


def late_share(first, late, early):
    late = jnp.where(first, late, 0.0) + lax.ppermute(late, "grp", [(1, 0)])
    rows = early.shape[0] - late.shape[0]
    share = jnp.concatenate([early[:rows], early[rows:] + late]).astype(BF16)
    return jnp.broadcast_to(share[None], (lax.axis_size("row"),) + share.shape)


def plain_steps(n, base, crop_length, pair_0, pair_1, cot_0, cot_1, weights):
    rows, cols = pair_0.shape[:2]
    own_rows = base + jnp.arange(rows)
    mask = (own_rows < crop_length).astype(F32)[:, None, None] * (jnp.arange(cols) < crop_length).astype(F32)[None, :, None]

    def send(*values):
        return swap_rows(jnp.stack([to_channels(v, n) for v in values], axis=1))

    w0, w1 = weights
    state_0 = pair_0.astype(F32)
    normed_0, left, right = pre(state_0, mask, w0)
    lr_0 = send(left, right)
    mixed_0 = from_channels(swap_rows(product(lr_0[:, 0], lr_0[:, 1]))).astype(F32)
    out_0, saved_0 = post(state_0, normed_0, mixed_0, w0)
    state_1 = out_0.astype(F32) + pair_1.astype(F32)
    normed_1, left, right = pre(state_1, mask, w1)
    lr_1 = send(left, right)
    mixed_1 = from_channels(swap_rows(product(lr_1[:, 0], lr_1[:, 1]))).astype(F32)
    out_1, saved_1 = post(state_1, normed_1, mixed_1, w1)
    grad_result, grad_gate, grad_mixed, upper_1 = back_upper(cot_1.astype(F32), saved_1, w1)
    gm = send(grad_mixed)
    glr = swap_rows(jnp.stack(product_back(gm[:, 0], lr_1[:, 0], lr_1[:, 1]), axis=1))
    grad_1, lower_1 = back_lower(
        state_1, normed_1, mask, grad_result, grad_gate, from_channels(glr[:, 0]), from_channels(glr[:, 1]), w1
    )
    grad_final = cot_0.astype(F32) + grad_1.astype(BF16).astype(F32)
    grad_result, grad_gate, grad_mixed, upper_0 = back_upper(grad_final, saved_0, w0)
    gm = send(grad_mixed)
    glr = swap_rows(jnp.stack(product_back(gm[:, 0], lr_0[:, 0], lr_0[:, 1]), axis=1))
    grad_0, lower_0 = back_lower(
        state_0, normed_0, mask, grad_result, grad_gate, from_channels(glr[:, 0]), from_channels(glr[:, 1]), w0
    )
    return out_0, out_1, grad_0, grad_1, {**upper_0, **lower_0}, {**upper_1, **lower_1}


ORDER = ("gain_in", "bias_in", "proj", "gate", "out", "gain_out", "bias_out", "gain_tr", "bias_tr", "up", "down")


def per_device(pair_in, crop_lengths, gain_in, bias_in, proj, gate, out, gain_out, bias_out, gain_tr, bias_tr, up, down, pair_cot):
    own_weights = dict(
        gain_in=gain_in[0], bias_in=bias_in[0], proj=proj[0], gate=gate[0], out=out[0], gain_out=gain_out[0],
        bias_out=bias_out[0], gain_tr=gain_tr[0], bias_tr=bias_tr[0], up=up[0], down=down[0],
    )
    groups, count = lax.axis_size("grp"), lax.axis_size("row")
    crops, rows, cols, channels = pair_in.shape[1:]
    group = lax.axis_index("grp")
    first = group == 0
    base = lax.axis_index("row") * rows
    swap = lambda v: lax.ppermute(v, "grp", [(0, 1), (1, 0)])
    pick = lambda v, i: lax.dynamic_index_in_dim(v, i, 0, keepdims=False)
    n = groups * count
    my_rows = rows // 2
    sizes = channels == LANES and out.shape[1] == LANES and up.shape[2] == 4 * LANES and crops == 2 and groups == 2
    if sizes and rows % 2 == 0 and my_rows % BLOCK_ROWS == 0 and cols % LANES == 0 and channels % n == 0 and n % 8 == 0 and (my_rows * (channels // n)) % 16 == 0:
        before_last = (cols // LANES - 1) * LANES
        swapped = crop_lengths[0] <= before_last
        which = [jnp.where(swapped, 1, 0), jnp.where(swapped, 0, 1)]
        lengths = [crop_lengths[crop] for crop in which]
        place = jnp.stack(lengths + [base + group * my_rows, group] + which).astype(jnp.int32)
        def shared(value):
            other = lambda crop: lax.dynamic_slice(value, (crop, (1 - group) * my_rows, 0, 0), (1, my_rows, cols, channels))
            return value, [swap(other(crop)[0]) for crop in which]

        def meet(home, crop, got_0, got_1):
            half = jnp.where(first, got_0, got_1)[None]
            return lax.dynamic_update_slice(home, half, (which[crop], (1 - group) * my_rows, 0, 0))

        def run(used):
            other_half = lambda value, section: lax.ppermute(value, "grp", [(1 - section, section)])
            pair, own = shared(pair_in[0]), pack_weights(own_weights)
            kernels = Kernels(place, used, n, my_rows, cols, channels, BLOCK_ROWS)
            state, homes = steps(
                kernels, crops, pair, shared(pair_cot[0]), own + tuple(swap(v) for v in own), functools.partial(early_sums, first, swap),
                functools.partial(late_share, first), other_half, meet,
            )
            total, _ = lax.optimization_barrier((state[-1]["total"], homes["grad"]))
            spec = pl.BlockSpec(memory_space=pltpu.VMEM)
            order = ("proj", "gate", "gain_in", "bias_in", "out", "gain_out", "bias_out", "gain_tr", "bias_tr", "up", "down")
            arrays = dict(
                gain_in=gain_in, bias_in=bias_in, proj=proj, gate=gate, out=out, gain_out=gain_out, bias_out=bias_out, gain_tr=gain_tr,
                bias_tr=bias_tr, up=up, down=down,
            )
            results = pl.pallas_call(
                k_results,
                out_shape=[jax.ShapeDtypeStruct(arrays[name].shape, F32) for name in order],
                in_specs=[spec],
                out_specs=[spec] * len(order),
                scratch_shapes=[pltpu.VMEM((s[0] * s[1], LANES), F32) for s in (share_shape(UP_ROWS), share_shape(LOW_ROWS))],
                compiler_params=pltpu.CompilerParams(vmem_limit_bytes=VMEM),
            )(total)
            results = dict(zip(order, results))
            return (homes["out"][None], homes["grad"][None]) + tuple(results[name] for name in ORDER)

        chunks = cols // LANES
        if chunks == 1:
            return run((1, 1))
        return lax.cond(lengths[1] <= before_last, lambda: run((chunks, chunks - 1)), lambda: run((chunks, chunks)))

    other_weights = {k: swap(v) for k, v in own_weights.items()}
    weights = [
        {k: jnp.where(first, own_weights[k], other_weights[k]) for k in ORDER},
        {k: jnp.where(first, other_weights[k], own_weights[k]) for k in ORDER},
    ]

    def both(value):
        own, got = pick(value, group), swap(pick(value, 1 - group))
        return jnp.where(first, own, got), jnp.where(first, got, own)

    def home(value_0, value_1):
        own, got = jnp.where(first, value_0, value_1), swap(jnp.where(first, value_1, value_0))
        return jnp.stack([jnp.where(first, own, got), jnp.where(first, got, own)])[None]

    out_0, out_1, grad_0, grad_1, grads_0, grads_1 = plain_steps(
        count, base, pick(crop_lengths, group), *both(pair_in[0]), *both(pair_cot[0]), weights
    )
    pair_out, pair_grad = home(out_0, out_1), home(grad_0, grad_1)
    mine = {k: jnp.where(first, grads_0[k], grads_1[k]) + swap(jnp.where(first, grads_1[k], grads_0[k])) for k in ORDER}
    summed = lax.psum(mine, "row")
    return (pair_out, pair_grad) + tuple(summed[k][None] for k in ORDER)


def solution(mesh):
    pair = P("grp", None, "row", None, None)
    vector, matrix = P("grp", None), P("grp", None, None)
    weights = (vector, vector, matrix, matrix, matrix, vector, vector, vector, vector, matrix, matrix)
    return jax.shard_map(
        per_device,
        mesh=mesh,
        in_specs=(pair, P()) + weights + (pair,),
        out_specs=(pair, pair) + weights,
        check_vma=False,
    )
```

```python
import functools

import jax
import jax.numpy as jnp
from jax import lax
from jax.experimental import pallas as pl
from jax.experimental.pallas import tpu as pltpu
from jax.sharding import PartitionSpec as P

EPSILON = 1e-05
F32 = jnp.float32
BF16 = jnp.bfloat16


def norm_stats(values):
    mean_value = jnp.mean(values, axis=-1, keepdims=True)
    centred = values - mean_value
    inv_scale = lax.rsqrt(jnp.mean(centred * centred, axis=-1, keepdims=True) + EPSILON)
    return (centred * inv_scale, inv_scale)


def norm_back(grad_scaled, scaled, inv_scale):
    mean_grad = jnp.mean(grad_scaled, axis=-1, keepdims=True)
    mean_cross = jnp.mean(grad_scaled * scaled, axis=-1, keepdims=True)
    return inv_scale * (grad_scaled - mean_grad - scaled * mean_cross)


def dot(a, b):
    return jnp.dot(a, b, preferred_element_type=F32)


def dot_t(a, b):
    return jnp.einsum("ijf,cf->ijc", a, b, preferred_element_type=F32)


def outer(a, b):
    return jnp.einsum("ijc,ijf->cf", a, b, preferred_element_type=F32)


def to_channels(value, n):
    rows, cols, channels = value.shape
    return jnp.transpose(value, (2, 0, 1)).reshape(n, channels // n, rows, cols)


def from_channels(value):
    n, held, rows, cols = value.shape
    return jnp.transpose(value.reshape(n * held, rows, cols), (1, 2, 0))


def swap_rows(value):
    return lax.all_to_all(value, "row", 0, 0)


def pre(state, mask, w):
    scaled, _ = norm_stats(state)
    normed = (scaled * w["gain_in"] + w["bias_in"]).astype(BF16)
    projected = dot(normed, w["proj"])
    width = projected.shape[-1] // 4
    lv, lg, rv, rg = (projected[..., i * width : (i + 1) * width] for i in range(4))
    left = (jax.nn.sigmoid(lg) * lv * mask).astype(BF16)
    right = (jax.nn.sigmoid(rg) * rv * mask).astype(BF16)
    return normed, left, right


def post(state, normed, mixed, w):
    gate_logit = dot(normed, w["gate"])
    scaled_mid, inv_mid = norm_stats(mixed)
    mixed_norm = (scaled_mid * w["gain_out"] + w["bias_out"]).astype(BF16)
    update = dot(mixed_norm, w["out"])
    gate_sigma = jax.nn.sigmoid(gate_logit)
    first_state = state + gate_sigma * update
    scaled_tr, inv_tr = norm_stats(first_state)
    trans_normed = (scaled_tr * w["gain_tr"] + w["bias_tr"]).astype(BF16)
    hidden = dot(trans_normed, w["up"])
    activated = jax.nn.silu(hidden).astype(BF16)
    result = (first_state + dot(activated, w["down"])).astype(BF16)
    saved = (gate_sigma, scaled_mid, inv_mid, mixed_norm, update, scaled_tr, inv_tr, trans_normed, hidden, activated)
    return result, saved


def back_upper(grad_final, saved, w):
    gate_sigma, scaled_mid, inv_mid, mixed_norm, update, scaled_tr, inv_tr, trans_normed, hidden, activated = saved
    grads = {}
    grad_trans = grad_final.astype(BF16)
    grads["down"] = outer(activated, grad_trans)
    grad_act = dot_t(grad_trans, w["down"])
    sigma = jax.nn.sigmoid(hidden)
    grad_hidden = (grad_act * sigma * (1.0 + hidden * (1.0 - sigma))).astype(BF16)
    grads["up"] = outer(trans_normed, grad_hidden)
    grad_tnorm = dot_t(grad_hidden, w["up"])
    grads["gain_tr"] = jnp.sum(grad_tnorm * scaled_tr, axis=(0, 1))
    grads["bias_tr"] = jnp.sum(grad_tnorm, axis=(0, 1))
    grad_result = grad_final + norm_back(grad_tnorm * w["gain_tr"], scaled_tr, inv_tr)
    grad_update = (grad_result * gate_sigma).astype(BF16)
    grad_gate = (grad_result * update * gate_sigma * (1.0 - gate_sigma)).astype(BF16)
    grads["out"] = outer(mixed_norm, grad_update)
    grad_norm_mid = dot_t(grad_update, w["out"])
    grads["gain_out"] = jnp.sum(grad_norm_mid * scaled_mid, axis=(0, 1))
    grads["bias_out"] = jnp.sum(grad_norm_mid, axis=(0, 1))
    grad_mixed = norm_back(grad_norm_mid * w["gain_out"], scaled_mid, inv_mid).astype(BF16)
    return grad_result, grad_gate, grad_mixed, grads


def back_lower(state, normed, mask, grad_result, grad_gate, grad_left, grad_right, w):
    scaled_in, inv_in = norm_stats(state)
    projected = dot(normed, w["proj"])
    width = projected.shape[-1] // 4
    lv, lg, rv, rg = (projected[..., i * width : (i + 1) * width] for i in range(4))
    ls = jax.nn.sigmoid(lg)
    rs = jax.nn.sigmoid(rg)
    gl = grad_left.astype(F32) * mask
    gr = grad_right.astype(F32) * mask
    grad_proj = jnp.concatenate(
        [gl * ls, gl * lv * ls * (1.0 - ls), gr * rs, gr * rv * rs * (1.0 - rs)], axis=-1
    ).astype(BF16)
    grads = {"proj": outer(normed, grad_proj), "gate": outer(normed, grad_gate)}
    grad_normed = dot_t(grad_proj, w["proj"]) + dot_t(grad_gate, w["gate"])
    grads["gain_in"] = jnp.sum(grad_normed * scaled_in, axis=(0, 1))
    grads["bias_in"] = jnp.sum(grad_normed, axis=(0, 1))
    return grad_result + norm_back(grad_normed * w["gain_in"], scaled_in, inv_in), grads


def product(left, right):
    n, held, rows, cols = left.shape
    mixed = jnp.einsum("atik,btjk->taibj", left, right, preferred_element_type=F32)
    return jnp.transpose(mixed.reshape(held, n, rows, n * rows), (1, 0, 2, 3)).astype(BF16)


def product_back(grad_mixed, left, right):
    n, held, rows, cols = left.shape
    split = grad_mixed.reshape(n, held, rows, n, rows)
    grad_left = jnp.einsum("atibj,btjk->atik", split, right, preferred_element_type=F32)
    grad_right = jnp.einsum("atibj,atik->btjk", split, left, preferred_element_type=F32)
    return grad_left.astype(BF16), grad_right.astype(BF16)


BLOCK_ROWS = 12
LANES = 128
VMEM = 62 << 20


def sig(x):
    return 0.5 * jnp.tanh(0.5 * x) + 0.5


def mm(a, b, ca=1, cb=0):
    return lax.dot_general(a, b, (((ca,), (cb,)), ((), ())), preferred_element_type=F32)


def col_stats(values):
    centred = values - jnp.mean(values, axis=0, keepdims=True)
    inv_scale = lax.rsqrt(jnp.mean(centred * centred, axis=0, keepdims=True) + EPSILON)
    return centred * inv_scale, inv_scale


def col_back(grad_scaled, scaled, inv_scale):
    mean_grad = jnp.mean(grad_scaled, axis=0, keepdims=True)
    mean_cross = jnp.mean(grad_scaled * scaled, axis=0, keepdims=True)
    return inv_scale * (grad_scaled - mean_grad - scaled * mean_cross)


def fold(values):
    return jnp.sum(values.reshape(values.shape[0] // 8, 8, values.shape[1]), axis=0)


class Step:
    def __init__(self, place, n, rows, held, block_rows, crop, last, used, chunks):
        self.last = last
        self.live = pl.program_id(0) < used if used < chunks else None
        self.n, self.rows, self.held, self.block = n, rows, held, block_rows
        self.row = pl.program_id(1) * block_rows
        self.length, self.base, self.group = place[crop], place[2], place[3]
        column = pl.program_id(0) * LANES + lax.broadcasted_iota(jnp.int32, (1, LANES), 1)
        self.columns = (column < self.length).astype(F32)

    def mask(self, r):
        return self.columns * jnp.where(self.base + self.row + r < self.length, 1.0, 0.0)

    def flat(self, ref):
        return ref[...].reshape(self.block * LANES, ref.shape[-1])

    def pick(self, pair, section):
        own, got = (self.flat(ref).astype(F32) for ref in pair)
        return jnp.where(jnp.full(own.shape, self.group) == section, own, got)

    def put(self, ref, value):
        ref[...] = value.reshape(self.block, LANES, value.shape[-1]).astype(ref.dtype)

    def lanes(self, r):
        return slice(r * LANES, (r + 1) * LANES)

    def spans(self, r):
        return [pl.ds((self.row + r) * self.held + t, self.n, stride=self.rows * self.held) for t in range(self.held)]

    def load(self, scratch, r):
        return jnp.concatenate([scratch[span, :] for span in self.spans(r)], axis=0)

    def store(self, scratch, r, value):
        for t, span in enumerate(self.spans(r)):
            scratch[span, :] = value[t * self.n : (t + 1) * self.n, :]


def unpack(ref, scratch, first=0):
    n, size = ref.shape[0], scratch.shape[0] // (ref.shape[0] + 1)

    def body(d, carry):
        scratch[pl.ds(pl.multiple_of(d * size, 8), size), :] = ref[d, first : first + size, :].astype(F32)
        return carry

    lax.fori_loop(0, n, body, 0)


def pack(scratch, ref, first=0):
    n, size = ref.shape[0], scratch.shape[0] // (ref.shape[0] + 1)

    def body(d, carry):
        ref[d, first : first + size, :] = scratch[pl.ds(pl.multiple_of(d * size, 8), size), :].astype(ref.dtype)
        return carry

    lax.fori_loop(0, n, body, 0)


def fetch(st, ref, scratch, first=0):
    if st.live is None:
        return unpack(ref, scratch, first)

    @pl.when(st.live)
    def _():
        unpack(ref, scratch, first)

    @pl.when(jnp.logical_not(st.live))
    def _():
        scratch[...] = jnp.zeros(scratch.shape, scratch.dtype)


def deliver(st, scratch, ref, first=0):
    if st.live is None:
        return pack(scratch, ref, first)
    pl.when(st.live)(lambda: pack(scratch, ref, first))


def at_first(action):
    pl.when(pl.program_id(1) == 0)(action)


def at_last(action):
    pl.when(pl.program_id(1) == pl.num_programs(1) - 1)(action)


def clear(accs, olds, cols=()):
    @pl.when((pl.program_id(0) == 0) & (pl.program_id(1) == 0))
    def _():
        for k, ref in enumerate(accs):
            ref[...] = olds[k][...] if olds else jnp.zeros(ref.shape, ref.dtype)
        for ref in cols:
            ref[...] = jnp.zeros(ref.shape, ref.dtype)


def add_blocks(ref, first, value):
    for q in range(value.shape[1] // LANES):
        ref[first + q * LANES : first + (q + 1) * LANES, :] += value[:, q * LANES : (q + 1) * LANES]


def close(st, ref, cols=None):
    @pl.when((pl.program_id(0) == pl.num_programs(0) - 1) & (pl.program_id(1) == pl.num_programs(1) - 1))
    def _():
        for k in range(2 if cols is not None else 0):
            row = UP_VEC + 16 + 8 * k
            ref[row : row + 1, :] += jnp.sum(jnp.transpose(cols[k]), axis=0, keepdims=True)
        for q in range(4 if st.last else 0):
            block = slice(q * LANES, (q + 1) * LANES)
            ref[block, :] = jnp.transpose(ref[block, :])


def pre_part(st, state, w, normed_ref, left_scr, right_scr):
    scaled, _ = norm_stats(state)
    normed = (scaled * w.vec[0:1, :] + w.vec[1:2, :]).astype(BF16)
    st.put(normed_ref, normed)
    projected = mm(w.proj_t[...], normed, 1, 1)
    for r in range(st.block):
        lv, lg, rv, rg = (projected[q * LANES : (q + 1) * LANES, st.lanes(r)] for q in range(4))
        mask = st.mask(r)
        st.store(left_scr, r, sig(lg) * lv * mask)
        st.store(right_scr, r, sig(rg) * rv * mask)


def post_part(st, state, normed, mixed_scr, w):
    mids = [col_stats(st.load(mixed_scr, r)) for r in range(st.block)]
    gain, bias = w.col[0], w.col[1]
    mixed_norm = jnp.concatenate([(scaled * gain + bias).astype(BF16) for scaled, _ in mids], axis=1)
    update = mm(mixed_norm, w.out[...], 0, 0)
    gate = sig(mm(normed, w.gate[...]))
    first_state = state + gate * update
    scaled_tr, inv_tr = norm_stats(first_state)
    trans = (scaled_tr * w.vec[2:3, :] + w.vec[3:4, :]).astype(BF16)
    hidden = mm(trans, w.up[...])
    sigma = sig(hidden)
    activated = (hidden * sigma).astype(BF16)
    return mids, mixed_norm, update, gate, first_state, scaled_tr, inv_tr, trans, hidden, sigma, activated


def upper_part(st, grad_final, kept, w, acc, cols, grad_ref, gate_ref, mixed_scr):
    mids, mixed_norm, update, gate, first_state, scaled_tr, inv_tr, trans, hidden, sigma, activated = kept
    low = grad_final.astype(BF16)
    add_blocks(acc, 0, mm(low, activated, 0, 0))
    grad_hidden = (mm(low, w.down[...], 1, 1) * (sigma * (1.0 + hidden * (1.0 - sigma)))).astype(BF16)
    add_blocks(acc, 4 * LANES, mm(trans, grad_hidden, 0, 0))
    grad_tnorm = mm(grad_hidden, w.up[...], 1, 1)
    acc[UP_VEC : UP_VEC + 8, :] += fold(grad_tnorm * scaled_tr)
    acc[UP_VEC + 8 : UP_VEC + 16, :] += fold(grad_tnorm)
    grad_result = grad_final + norm_back(grad_tnorm * w.vec[2:3, :], scaled_tr, inv_tr)
    st.put(grad_ref, grad_result)
    scaled_grad = grad_result * gate
    grad_update = scaled_grad.astype(BF16)
    st.put(gate_ref, scaled_grad * update * (1.0 - gate))
    add_blocks(acc, 8 * LANES, mm(mixed_norm, grad_update))
    grad_norm = mm(w.out[...], grad_update, 1, 1)
    for r, (scaled, inv_scale) in enumerate(mids):
        grad = grad_norm[:, st.lanes(r)]
        cols[0] += grad * scaled
        cols[1] += grad
        st.store(mixed_scr, r, col_back(grad * w.col[0], scaled, inv_scale) * st.mask(r))


def lower_part(st, state, normed, grad_result, grad_gate, left_scr, right_scr, w, acc):
    projected = mm(w.proj_t[...], normed, 1, 1)
    parts = []
    for r in range(st.block):
        lv, lg, rv, rg = (projected[q * LANES : (q + 1) * LANES, st.lanes(r)] for q in range(4))
        ls, rs = sig(lg), sig(rg)
        a, b = st.load(left_scr, r) * ls, st.load(right_scr, r) * rs
        parts.append(jnp.concatenate([v.astype(BF16) for v in (a, a * lv * (1.0 - ls), b, b * rv * (1.0 - rs))], axis=0))
    grad_proj = jnp.concatenate(parts, axis=1)
    acc[: 4 * LANES, :] += mm(grad_proj, normed)
    add_blocks(acc, 4 * LANES, mm(normed, grad_gate, 0, 0))
    grad_normed = jnp.transpose(mm(w.proj[...], grad_proj)) + mm(grad_gate, w.gate[...], 1, 1)
    scaled_in, inv_in = norm_stats(state)
    acc[LOW_VEC : LOW_VEC + 8, :] += fold(grad_normed * scaled_in)
    acc[LOW_VEC + 8 : LOW_VEC + 16, :] += fold(grad_normed)
    return grad_result + norm_back(grad_normed * w.vec[0:1, :], scaled_in, inv_in)


class Weights:
    def __init__(self, group, section, refs, scratch):
        self.wide, self.down, self.vec, self.col, self.proj_t = scratch
        cut = lambda first, count: self.wide.at[:, first * LANES : (first + count) * LANES]
        self.proj, self.gate, self.out, self.up = cut(0, 4), cut(4, 1), cut(5, 1), cut(6, 4)

        @pl.when((pl.program_id(0) == 0) & (pl.program_id(1) == 0))
        def _():
            for chosen, sources in ((group == section, refs[:3]), (group != section, refs[3:])):

                @pl.when(chosen)
                def _():
                    for ref, source in zip((self.wide, self.down, self.vec), sources):
                        ref[...] = source[...]

            for k in range(2):
                self.col[k] = jnp.transpose(jnp.broadcast_to(self.vec[4 + k : 5 + k, :], (LANES, LANES)))
            for q in range(4):
                block = slice(q * LANES, (q + 1) * LANES)
                self.proj_t[block, :] = jnp.transpose(self.wide[:, block])

    @staticmethod
    def scratch():
        return [
            pltpu.VMEM((LANES, 10 * LANES), BF16), pltpu.VMEM((4 * LANES, LANES), BF16), pltpu.VMEM((8, LANES), F32),
            pltpu.VMEM((2, LANES, LANES), F32), pltpu.VMEM((4 * LANES, LANES), BF16),
        ]


def pack_weights(w):
    zero = jnp.zeros_like(w["gain_in"])
    names = ("gain_in", "bias_in", "gain_tr", "bias_tr", "gain_out", "bias_out")
    wide = jnp.concatenate([w[name] for name in ("proj", "gate", "out", "up")], axis=1)
    return wide, w["down"], jnp.stack([w[name] for name in names] + [zero, zero])


UP_VEC = 9 * LANES
UP_ROWS = UP_VEC + 32
LOW_VEC = 5 * LANES
LOW_ROWS = LOW_VEC + 16


def k_pre(cfg, place, own, got, *refs):
    st = Step(place, *cfg)
    w = Weights(st.group, 0, refs[:6], refs[-5:])
    normed, both, left, right = refs[6:-5]
    pre_part(st, st.pick((own, got), 0), w, normed, left, right)

    @at_last
    def _():
        deliver(st, left, both)
        deliver(st, right, both, both.shape[1] // 2)


def k_post_pre(cfg, place, own_0, got_0, own_1, got_1, normed_in, mixed_in, *refs):
    st = Step(place, *cfg)
    w0, w1 = Weights(st.group, 0, refs[:6], refs[-10:-5]), Weights(st.group, 1, refs[:6], refs[-5:])
    *_, home, out, normed, both, mixed, left, right = refs[6:-10]
    at_first(lambda: fetch(st, mixed_in, mixed))
    kept = post_part(st, st.pick((own_0, got_0), 0), st.flat(normed_in), mixed, w0)
    result = (kept[4] + mm(kept[-1], w0.down[...])).astype(BF16)
    st.put(home, result)
    st.put(out, result)
    pre_part(st, result.astype(F32) + st.pick((own_1, got_1), 1), w1, normed, left, right)

    @at_last
    def _():
        deliver(st, left, both)
        deliver(st, right, both, both.shape[1] // 2)


def k_post_upper(cfg, place, own, got, own_cot, got_cot, before, normed_in, mixed_in, *refs):
    st = Step(place, *cfg)
    w = Weights(st.group, 1, refs[:6], refs[-5:])
    _, *olds, home, out, grad, gate, grad_mixed, sums, mixed, cols = refs[6:-5]
    clear([sums], olds, [cols])
    at_first(lambda: fetch(st, mixed_in, mixed))
    state = st.flat(before).astype(F32) + st.pick((own, got), 1)
    kept = post_part(st, state, st.flat(normed_in), mixed, w)
    result = kept[4] + mm(kept[-1], w.down[...])
    st.put(home, result)
    st.put(out, result)
    upper_part(st, st.pick((own_cot, got_cot), 1), kept, w, sums, cols, grad, gate, mixed)
    close(st, sums, cols)
    at_last(lambda: deliver(st, mixed, grad_mixed))


def k_lower_upper(
    cfg, place, own_1, got_1, own_0, got_0, own_cot, got_cot, before, normed_1, grad_1, gate_1, normed_0, both, mixed_in, *refs
):
    st = Step(place, *cfg)
    w1, w0 = Weights(st.group, 1, refs[:6], refs[-10:-5]), Weights(st.group, 0, refs[:6], refs[-5:])
    olds = refs[7:9] if cfg[4] else ()
    home, pair_grad, grad, gate, grad_mixed, low_sums, up_sums, left, right, mixed, cols = refs[-21:-10]
    clear([low_sums, up_sums], olds, [cols])

    @at_first
    def _():
        fetch(st, both, left)
        fetch(st, both, right, both.shape[1] // 2)
        fetch(st, mixed_in, mixed)

    state = st.flat(before).astype(F32) + st.pick((own_1, got_1), 1)
    grad_state = lower_part(
        st, state, st.flat(normed_1), st.flat(grad_1), st.flat(gate_1), left, right, w1, low_sums
    )
    st.put(home, grad_state)
    st.put(pair_grad, grad_state)
    kept = post_part(st, st.pick((own_0, got_0), 0), st.flat(normed_0), mixed, w0)
    grad_final = st.pick((own_cot, got_cot), 0) + grad_state.astype(BF16).astype(F32)
    upper_part(st, grad_final, kept, w0, up_sums, cols, grad, gate, mixed)
    close(st, low_sums)
    close(st, up_sums, cols)
    at_last(lambda: deliver(st, mixed, grad_mixed))


def k_lower(cfg, place, own, got, normed, grad, gate, both, *refs):
    st = Step(place, *cfg)
    w = Weights(st.group, 0, refs[:6], refs[-5:])
    _, *olds, home, pair_grad, sums, parts, left, right = refs[6:-5]
    clear([sums], olds)

    @at_first
    def _():
        fetch(st, both, left)
        fetch(st, both, right, both.shape[1] // 2)

    state = st.pick((own, got), 0)
    grad_state = lower_part(
        st, state, st.flat(normed), st.flat(grad), st.flat(gate), left, right, w, sums
    )
    st.put(home, grad_state)
    st.put(pair_grad, grad_state)
    close(st, sums)

    @pl.when((pl.program_id(0) == pl.num_programs(0) - 1) & (pl.program_id(1) == pl.num_programs(1) - 1))
    def _():
        n, rows, _ = parts.shape
        parts[...] = jnp.zeros(parts.shape, BF16)
        for d in range(n):
            count = max(0, min(rows, LOW_ROWS - d * rows))
            if count:
                parts[d, :count, :] = sums[d * rows : d * rows + count, :].astype(BF16)


def k_results(total, proj, gate, gain_in, bias_in, out, gain_out, bias_out, gain_tr, bias_tr, up, down, early, low):
    n = total.shape[0]
    first, second = early.shape[0] // n, low.shape[0] // n
    for d in range(n):
        early[d * first : (d + 1) * first, :] = total[d, :first, :].astype(F32)
        low[d * second : (d + 1) * second, :] = total[d, first:, :].astype(F32)
    down[0] = early[: 4 * LANES, :]
    for q in range(4):
        up[0, :, q * LANES : (q + 1) * LANES] = early[(4 + q) * LANES : (5 + q) * LANES, :]
        proj[0, :, q * LANES : (q + 1) * LANES] = low[q * LANES : (q + 1) * LANES, :]
    out[0] = early[8 * LANES : UP_VEC, :]
    gate[0] = low[4 * LANES : LOW_VEC, :]
    for k, ref in enumerate((gain_tr, bias_tr, gain_out, bias_out)):
        ref[...] = jnp.sum(early[UP_VEC + 8 * k : UP_VEC + 8 * k + 8, :], axis=0, keepdims=True)
    for k, ref in enumerate((gain_in, bias_in)):
        ref[...] = jnp.sum(low[LOW_VEC + 8 * k : LOW_VEC + 8 * k + 8, :], axis=0, keepdims=True)


def spread(ref, scratch, first=0):
    n, size = ref.shape[0], (scratch.shape[1] - 8) // ref.shape[0]

    def body(d, carry):
        for c in range(scratch.shape[0]):
            value = ref[d, first : first + size, c * LANES : (c + 1) * LANES]
            scratch[c, pl.ds(pl.multiple_of(d * size, 8), size), :] = value.astype(F32)
        return carry

    lax.fori_loop(0, n, body, 0)


def gather(scratch, ref, first=0):
    n, size = ref.shape[0], (scratch.shape[1] - 8) // ref.shape[0]

    def body(d, carry):
        for c in range(scratch.shape[0]):
            value = scratch[c, pl.ds(pl.multiple_of(d * size, 8), size), :]
            ref[d, first : first + size, c * LANES : (c + 1) * LANES] = value.astype(ref.dtype)
        return carry

    lax.fori_loop(0, n, body, 0)


def channel(scratch, t, held):
    chunks, size, _ = scratch.shape
    span = pl.ds(t, (size - 8) // held, stride=held)
    return jnp.concatenate([scratch[c, span, :].astype(BF16) for c in range(chunks)], axis=1)


def put_channel(scratch, t, held, value):
    chunks, size, _ = scratch.shape
    span = pl.ds(t, (size - 8) // held, stride=held)
    for c in range(chunks):
        scratch[c, span, :] = value[:, c * LANES : (c + 1) * LANES]


def k_product(held, both, out, left, right):
    spread(both, left)
    spread(both, right, both.shape[1] // 2)

    def body(t, carry):
        others = channel(right, t, held)[: left.shape[0] * LANES]
        put_channel(left, t, held, mm(channel(left, t, held), others, 1, 1))
        return carry

    lax.fori_loop(0, held, body, 0)
    gather(left, out)


def k_product_back(held, grad_in, both, out, grad, left, right):
    spread(grad_in, grad)
    spread(both, left)
    spread(both, right, both.shape[1] // 2)

    def body(t, carry):
        low, lv, rv = channel(grad, t, held), channel(left, t, held), channel(right, t, held)
        put_channel(left, t, held, mm(low, rv[: low.shape[1]]))
        grad_right = mm(low, lv, 0, 0)
        if low.shape[1] < rv.shape[0]:
            rest = jnp.zeros((rv.shape[0] - low.shape[1], lv.shape[1]), F32)
            grad_right = jnp.concatenate([grad_right, rest])
        put_channel(right, t, held, grad_right)
        return carry

    lax.fori_loop(0, held, body, 0)
    gather(left, out)
    gather(right, out, both.shape[1] // 2)


STEPS = """\
1A SA0 1B SB0 TA0 MA0 TB0 MB0 2A SA1 2B SB1 TA1 MA1 TB1 MB1 3A GA1 3B GB1 tA1 sA1 tB1 sB1 HA HB 4A GA0 4B GB0 tA0 sA0 tB0 sB0 EB0 QB0 5A JA 5B qB0 JB AB0
"""


class Kernels:
    def __init__(self, place, used, n, rows, cols, channels, block_rows):
        self.place, self.used, self.crops = place, used, len(used)
        self.n, self.rows, self.cols, self.channels, self.block = n, rows, cols, channels, block_rows
        self.held = channels // n
        self.size = rows * self.held
        self.chunks = cols // LANES

    def row_call(self, body, crop, ins, outs, scratch, micros, cols=0, sections=1):
        rows, block = self.rows, self.block

        def spec(kind, shape):
            if kind == "own":
                return pl.BlockSpec(
                    (pl.squeezed, block, LANES, shape[-1]), lambda c, i, s: (s[4 + crop], s[3] * (rows // block) + i, c, 0)
                )
            if kind in ("home 0", "home 1"):
                first = int(kind[-1]) * (rows // block)
                return pl.BlockSpec((pl.squeezed, block, LANES, shape[-1]), lambda c, i, s: (s[4 + crop], first + i, c, 0))
            if kind == "rows":
                return pl.BlockSpec((block, LANES, shape[-1]), lambda c, i, s: (i, c, 0))
            if kind == "moved":
                final = shape[-1] // LANES - 1
                return pl.BlockSpec(shape[:-1] + (LANES,), lambda c, i, s: (0, 0, jnp.minimum(c, final)))
            if kind == "kept":
                return pl.BlockSpec(memory_space=pl.ANY)
            zeros = (0,) * len(shape)
            return pl.BlockSpec(shape, lambda c, i, s: zeros)

        aliases = {1 + k: 0 for k, (kind, _) in enumerate(ins) if kind == "kept"}
        return pl.pallas_call(
            functools.partial(
                body, (self.n, rows, self.held, block, crop, crop == self.crops - 1, self.used[crop], self.chunks)
            ),
            out_shape=tuple(v for _, v in outs),
            grid_spec=pltpu.PrefetchScalarGridSpec(
                num_scalar_prefetch=1,
                grid=(self.chunks, rows // block),
                in_specs=[spec(k, v.shape) for k, v in ins],
                out_specs=tuple(spec(k, v.shape) for k, v in outs),
                scratch_shapes=[pltpu.VMEM(((self.n + 1) * self.size, LANES), F32)] * scratch
                + [pltpu.VMEM((2, self.channels, LANES), F32)] * cols
                + Weights.scratch() * sections,
            ),
            input_output_aliases=aliases,
            compiler_params=pltpu.CompilerParams(vmem_limit_bytes=VMEM),
            cost_estimate=cost(micros),
        )(self.place, *[v for _, v in ins])

    def home(self, section, dtype):
        return (f"home {section}", jax.ShapeDtypeStruct((self.crops, 2 * self.rows, self.cols, self.channels), dtype))

    def pairs(self, dtype):
        return ("rows", jax.ShapeDtypeStruct((self.rows, self.cols, self.channels), dtype))

    def moved(self, crop, count=1):
        return ("moved", jax.ShapeDtypeStruct((self.n, count * self.size, self.used[crop] * LANES), BF16))

    def sums(self, rows):
        return ("all", jax.ShapeDtypeStruct((rows, self.channels), F32))

    def channel_call(self, body, ins, out, scratch, micros):
        spec = pl.BlockSpec(memory_space=pltpu.VMEM)
        return pl.pallas_call(
            functools.partial(body, self.held),
            out_shape=out[1],
            in_specs=[spec] * len(ins),
            out_specs=spec,
            scratch_shapes=[pltpu.VMEM((out[1].shape[2] // LANES, self.n * self.size + 8, LANES), F32)] * scratch,
            compiler_params=pltpu.CompilerParams(vmem_limit_bytes=VMEM),
            cost_estimate=cost(micros),
        )(*ins)


def cost(micros):
    return pl.CostEstimate(flops=int(micros * 1.15e9), bytes_accessed=int(micros * 1e6), transcendentals=0)


def steps(kernels, crops, pair, cot, weights, early, late_share, other_half, meet):
    w = [("all", v) for v in weights]
    call, pairs, moved = kernels.row_call, kernels.pairs, kernels.moved
    up_sums, low_sums = kernels.sums(UP_ROWS), kernels.sums(LOW_ROWS)
    earlier = lambda *names: [("all", state[0][name]) for name in names if name in state[0]]
    homes = {}
    kept = lambda name: [("kept", homes[name])]
    mine = lambda v, crop: [("own", v[0]), ("rows", v[1][crop])]
    part = lambda *vs: [("rows", v) for v in vs]
    far = lambda *vs: [("moved", v) for v in vs]
    swap = lambda v: lax.all_to_all(v, ("row", "grp"), 0, 0)
    spread_rows = lambda v: lax.all_to_all(v, "row", 0, 0)
    state = [dict() for _ in range(crops)]
    last = {}

    def ordered(kind, op, value):
        if kind in last:
            value, _ = lax.optimization_barrier((value, last[kind]))
        result = op(value)
        last[kind] = result[0] if isinstance(result, (tuple, list)) else result
        return result

    def row_kernel(body, crop, ins, *rest):
        return ordered("kernel", lambda v: call(body, crop, [(ins[0][0], v)] + ins[1:], *rest), ins[0][1])

    def channel_kernel(body, ins, *rest):
        return ordered("kernel", lambda v: kernels.channel_call(body, (v,) + tuple(ins[1:]), *rest), ins[0])

    def pre(crop, s):
        s["normed_0"], s["both_0"] = row_kernel(k_pre, crop, mine(pair, crop) + w, [pairs(BF16), moved(crop, 2)], 2, 10)

    def post_pre(crop, s):
        homes["out"], s["out_0"], s["normed_1"], s["both_1"] = row_kernel(
            k_post_pre, crop,
            mine(pair, crop) + mine(pair, crop) + part(s["normed_0"]) + far(s["mixed_0"]) + w + (kept("out") if crop else []),
            [kernels.home(0, BF16), pairs(BF16), pairs(BF16), moved(crop, 2)], 3, 18, 0, 2,
        )
        s["got_out_0"] = other_half(s["out_0"], 0)

    def post_upper(crop, s):
        homes["out"], s["out_1"], s["grad_1"], s["gate_1"], s["grad_mixed_1"], s["up_1"] = row_kernel(
            k_post_upper, crop,
            mine(pair, crop) + mine(cot, crop) + part(s["out_0"], s["normed_1"]) + far(s["mixed_1"]) + w + kept("out")
            + earlier("up_1"),
            [kernels.home(1, BF16), pairs(BF16), pairs(F32), pairs(BF16), moved(crop), up_sums], 1, 23, 1,
        )
        s["got_out_1"] = other_half(s["out_1"], 1)

    def lower_upper(crop, s):
        homes["grad"], s["pair_grad_1"], s["grad_0"], s["gate_0"], s["grad_mixed_0"], s["low_1"], s["up_0"] = row_kernel(
            k_lower_upper, crop,
            mine(pair, crop) + mine(pair, crop) + mine(cot, crop)
            + part(s["out_0"], s["normed_1"], s["grad_1"], s["gate_1"], s["normed_0"])
            + far(s["back_1"], s["mixed_0"]) + w + (kept("grad") if crop else []) + earlier("low_1", "up_0"),
            [kernels.home(1, F32), pairs(F32), pairs(F32), pairs(BF16), moved(crop), low_sums, up_sums], 3, 31, 1, 2,
        )
        s["got_grad_1"] = other_half(s["pair_grad_1"], 1)

    def lower(crop, s):
        homes["grad"], s["pair_grad_0"], s["low_0"], s["late"] = row_kernel(
            k_lower, crop, mine(pair, crop) + part(s["normed_0"], s["grad_0"], s["gate_0"]) + far(s["back_0"]) + w
            + kept("grad") + earlier("low_0"),
            [kernels.home(0, F32), pairs(F32), low_sums, ("all", jax.ShapeDtypeStruct(share_shape(LOW_ROWS), BF16))], 2, 13,
        )
        s["got_grad_0"] = other_half(s["pair_grad_0"], 0)

    def product(crop, s, k):
        s[f"product_{k}"] = channel_kernel(k_product, (s[f"factors_{k}"],), moved(crop), 2, 6)

    def product_back(crop, s, k):
        s[f"grads_{k}"] = channel_kernel(k_product_back, (s[f"g_{k}"], s[f"factors_{k}"]), moved(crop, 2), 3, 12)

    transfers = dict(S=("factors", "both"), M=("mixed", "product"), G=("g", "grad_mixed"), s=("back", "grads"))
    rows_of = {"1": pre, "2": post_pre, "3": post_upper, "4": lower_upper, "5": lower}
    channels_of = {"T": product, "t": product_back}
    for step in STEPS.split():
        what, crop, k = step[0], "AB".index(step[1]), step[2:]
        s = state[crop]
        if what == "E":
            sums = {name: lax.optimization_barrier((s[name], last["kernel"]))[0] for name in ("up_0", "up_1", "low_1")}
            last["kernel"] = s["early"] = early(sums)
        elif what in "QqA":
            if what == "A":
                s["total"] = ordered("swap", spread_rows, late_share(s["share_q"], s["share_Q"]))
            else:
                moved_parts = ordered("swap", spread_rows, s["early" if what == "Q" else "late"])
                s[f"share_{what}"] = jnp.sum(moved_parts.astype(F32), axis=0)
        elif what in "HJ":
            name = "out" if what == "H" else "grad"
            homes[name] = meet(homes[name], crop, s[f"got_{name}_0"], s[f"got_{name}_1"])
            if what == "H":
                last["kernel"] = homes[name]
        elif what in rows_of:
            rows_of[what](crop, s)
        elif what in channels_of:
            channels_of[what](crop, s, k)
        else:
            new, old = transfers[what]
            s[f"{new}_{k}"] = ordered("swap", swap, s[f"{old}_{k}"])

    return state, homes


def share_shape(rows):
    n = lax.axis_size("row")
    return (n, -(-rows // (16 * n)) * 16, LANES)


def in_shares(sums):
    n, rows, _ = share_shape(sums.shape[0])
    return jnp.pad(sums, ((0, n * rows - sums.shape[0]), (0, 0))).reshape(n, rows, LANES)


def early_sums(first, swap, sums):
    early_0 = jnp.concatenate([sums["up_0"], jnp.zeros((LOW_ROWS, LANES), F32)])
    early_1 = jnp.concatenate([sums["up_1"], sums["low_1"]])
    early = jnp.where(first, early_0, early_1) + swap(jnp.where(first, early_1, early_0))
    return jnp.concatenate([in_shares(early[:UP_ROWS]), in_shares(early[UP_ROWS:])], axis=1).astype(BF16)


def late_share(first, late, early):
    late = jnp.where(first, late, 0.0) + lax.ppermute(late, "grp", [(1, 0)])
    rows = early.shape[0] - late.shape[0]
    share = jnp.concatenate([early[:rows], early[rows:] + late]).astype(BF16)
    return jnp.broadcast_to(share[None], (lax.axis_size("row"),) + share.shape)


def plain_steps(n, base, crop_length, pair_0, pair_1, cot_0, cot_1, weights):
    rows, cols = pair_0.shape[:2]
    own_rows = base + jnp.arange(rows)
    mask = (own_rows < crop_length).astype(F32)[:, None, None] * (jnp.arange(cols) < crop_length).astype(F32)[None, :, None]

    def send(*values):
        return swap_rows(jnp.stack([to_channels(v, n) for v in values], axis=1))

    w0, w1 = weights
    state_0 = pair_0.astype(F32)
    normed_0, left, right = pre(state_0, mask, w0)
    lr_0 = send(left, right)
    mixed_0 = from_channels(swap_rows(product(lr_0[:, 0], lr_0[:, 1]))).astype(F32)
    out_0, saved_0 = post(state_0, normed_0, mixed_0, w0)
    state_1 = out_0.astype(F32) + pair_1.astype(F32)
    normed_1, left, right = pre(state_1, mask, w1)
    lr_1 = send(left, right)
    mixed_1 = from_channels(swap_rows(product(lr_1[:, 0], lr_1[:, 1]))).astype(F32)
    out_1, saved_1 = post(state_1, normed_1, mixed_1, w1)
    grad_result, grad_gate, grad_mixed, upper_1 = back_upper(cot_1.astype(F32), saved_1, w1)
    gm = send(grad_mixed)
    glr = swap_rows(jnp.stack(product_back(gm[:, 0], lr_1[:, 0], lr_1[:, 1]), axis=1))
    grad_1, lower_1 = back_lower(
        state_1, normed_1, mask, grad_result, grad_gate, from_channels(glr[:, 0]), from_channels(glr[:, 1]), w1
    )
    grad_final = cot_0.astype(F32) + grad_1.astype(BF16).astype(F32)
    grad_result, grad_gate, grad_mixed, upper_0 = back_upper(grad_final, saved_0, w0)
    gm = send(grad_mixed)
    glr = swap_rows(jnp.stack(product_back(gm[:, 0], lr_0[:, 0], lr_0[:, 1]), axis=1))
    grad_0, lower_0 = back_lower(
        state_0, normed_0, mask, grad_result, grad_gate, from_channels(glr[:, 0]), from_channels(glr[:, 1]), w0
    )
    return out_0, out_1, grad_0, grad_1, {**upper_0, **lower_0}, {**upper_1, **lower_1}


ORDER = ("gain_in", "bias_in", "proj", "gate", "out", "gain_out", "bias_out", "gain_tr", "bias_tr", "up", "down")


def per_device(pair_in, crop_lengths, gain_in, bias_in, proj, gate, out, gain_out, bias_out, gain_tr, bias_tr, up, down, pair_cot):
    own_weights = dict(
        gain_in=gain_in[0], bias_in=bias_in[0], proj=proj[0], gate=gate[0], out=out[0], gain_out=gain_out[0],
        bias_out=bias_out[0], gain_tr=gain_tr[0], bias_tr=bias_tr[0], up=up[0], down=down[0],
    )
    groups, count = lax.axis_size("grp"), lax.axis_size("row")
    crops, rows, cols, channels = pair_in.shape[1:]
    group = lax.axis_index("grp")
    first = group == 0
    base = lax.axis_index("row") * rows
    swap = lambda v: lax.ppermute(v, "grp", [(0, 1), (1, 0)])
    pick = lambda v, i: lax.dynamic_index_in_dim(v, i, 0, keepdims=False)
    n = groups * count
    my_rows = rows // 2
    sizes = channels == LANES and out.shape[1] == LANES and up.shape[2] == 4 * LANES and crops == 2 and groups == 2
    if sizes and rows % 2 == 0 and my_rows % BLOCK_ROWS == 0 and cols % LANES == 0 and channels % n == 0 and n % 8 == 0 and (my_rows * (channels // n)) % 16 == 0:
        before_last = (cols // LANES - 1) * LANES
        swapped = crop_lengths[0] <= before_last
        which = [jnp.where(swapped, 1, 0), jnp.where(swapped, 0, 1)]
        lengths = [crop_lengths[crop] for crop in which]
        place = jnp.stack(lengths + [base + group * my_rows, group] + which).astype(jnp.int32)
        def shared(value):
            other = lambda crop: lax.dynamic_slice(value, (crop, (1 - group) * my_rows, 0, 0), (1, my_rows, cols, channels))
            return value, [swap(other(crop)[0]) for crop in which]

        def meet(home, crop, got_0, got_1):
            half = jnp.where(first, got_0, got_1)[None]
            return lax.dynamic_update_slice(home, half, (which[crop], (1 - group) * my_rows, 0, 0))

        def run(used):
            other_half = lambda value, section: lax.ppermute(value, "grp", [(1 - section, section)])
            pair, own = shared(pair_in[0]), pack_weights(own_weights)
            kernels = Kernels(place, used, n, my_rows, cols, channels, BLOCK_ROWS)
            state, homes = steps(
                kernels, crops, pair, shared(pair_cot[0]), own + tuple(swap(v) for v in own), functools.partial(early_sums, first, swap),
                functools.partial(late_share, first), other_half, meet,
            )
            total, _ = lax.optimization_barrier((state[-1]["total"], homes["grad"]))
            spec = pl.BlockSpec(memory_space=pltpu.VMEM)
            order = ("proj", "gate", "gain_in", "bias_in", "out", "gain_out", "bias_out", "gain_tr", "bias_tr", "up", "down")
            arrays = dict(
                gain_in=gain_in, bias_in=bias_in, proj=proj, gate=gate, out=out, gain_out=gain_out, bias_out=bias_out, gain_tr=gain_tr,
                bias_tr=bias_tr, up=up, down=down,
            )
            results = pl.pallas_call(
                k_results,
                out_shape=[jax.ShapeDtypeStruct(arrays[name].shape, F32) for name in order],
                in_specs=[spec],
                out_specs=[spec] * len(order),
                scratch_shapes=[pltpu.VMEM((s[0] * s[1], LANES), F32) for s in (share_shape(UP_ROWS), share_shape(LOW_ROWS))],
                compiler_params=pltpu.CompilerParams(vmem_limit_bytes=VMEM),
            )(total)
            results = dict(zip(order, results))
            return (homes["out"][None], homes["grad"][None]) + tuple(results[name] for name in ORDER)

        chunks = cols // LANES
        return run((chunks, chunks))

    other_weights = {k: swap(v) for k, v in own_weights.items()}
    weights = [
        {k: jnp.where(first, own_weights[k], other_weights[k]) for k in ORDER},
        {k: jnp.where(first, other_weights[k], own_weights[k]) for k in ORDER},
    ]

    def both(value):
        own, got = pick(value, group), swap(pick(value, 1 - group))
        return jnp.where(first, own, got), jnp.where(first, got, own)

    def home(value_0, value_1):
        own, got = jnp.where(first, value_0, value_1), swap(jnp.where(first, value_1, value_0))
        return jnp.stack([jnp.where(first, own, got), jnp.where(first, got, own)])[None]

    out_0, out_1, grad_0, grad_1, grads_0, grads_1 = plain_steps(
        count, base, pick(crop_lengths, group), *both(pair_in[0]), *both(pair_cot[0]), weights
    )
    pair_out, pair_grad = home(out_0, out_1), home(grad_0, grad_1)
    mine = {k: jnp.where(first, grads_0[k], grads_1[k]) + swap(jnp.where(first, grads_1[k], grads_0[k])) for k in ORDER}
    summed = lax.psum(mine, "row")
    return (pair_out, pair_grad) + tuple(summed[k][None] for k in ORDER)


def solution(mesh):
    pair = P("grp", None, "row", None, None)
    vector, matrix = P("grp", None), P("grp", None, None)
    weights = (vector, vector, matrix, matrix, matrix, vector, vector, vector, vector, matrix, matrix)
    return jax.shard_map(
        per_device,
        mesh=mesh,
        in_specs=(pair, P()) + weights + (pair,),
        out_specs=(pair, pair) + weights,
        check_vma=False,
    )
```

```python
import functools

import jax
import jax.numpy as jnp
from jax import lax
from jax.experimental import pallas as pl
from jax.experimental.pallas import tpu as pltpu
from jax.sharding import PartitionSpec as P

EPSILON = 1e-05
F32 = jnp.float32
BF16 = jnp.bfloat16


def norm_stats(values):
    mean_value = jnp.mean(values, axis=-1, keepdims=True)
    centred = values - mean_value
    inv_scale = lax.rsqrt(jnp.mean(centred * centred, axis=-1, keepdims=True) + EPSILON)
    return (centred * inv_scale, inv_scale)


def norm_back(grad_scaled, scaled, inv_scale):
    mean_grad = jnp.mean(grad_scaled, axis=-1, keepdims=True)
    mean_cross = jnp.mean(grad_scaled * scaled, axis=-1, keepdims=True)
    return inv_scale * (grad_scaled - mean_grad - scaled * mean_cross)


def dot(a, b):
    return jnp.dot(a, b, preferred_element_type=F32)


def dot_t(a, b):
    return jnp.einsum("ijf,cf->ijc", a, b, preferred_element_type=F32)


def outer(a, b):
    return jnp.einsum("ijc,ijf->cf", a, b, preferred_element_type=F32)


def to_channels(value, n):
    rows, cols, channels = value.shape
    return jnp.transpose(value, (2, 0, 1)).reshape(n, channels // n, rows, cols)


def from_channels(value):
    n, held, rows, cols = value.shape
    return jnp.transpose(value.reshape(n * held, rows, cols), (1, 2, 0))


def swap_rows(value):
    return lax.all_to_all(value, "row", 0, 0)


def pre(state, mask, w):
    scaled, _ = norm_stats(state)
    normed = (scaled * w["gain_in"] + w["bias_in"]).astype(BF16)
    projected = dot(normed, w["proj"])
    width = projected.shape[-1] // 4
    lv, lg, rv, rg = (projected[..., i * width : (i + 1) * width] for i in range(4))
    left = (jax.nn.sigmoid(lg) * lv * mask).astype(BF16)
    right = (jax.nn.sigmoid(rg) * rv * mask).astype(BF16)
    return normed, left, right


def post(state, normed, mixed, w):
    gate_logit = dot(normed, w["gate"])
    scaled_mid, inv_mid = norm_stats(mixed)
    mixed_norm = (scaled_mid * w["gain_out"] + w["bias_out"]).astype(BF16)
    update = dot(mixed_norm, w["out"])
    gate_sigma = jax.nn.sigmoid(gate_logit)
    first_state = state + gate_sigma * update
    scaled_tr, inv_tr = norm_stats(first_state)
    trans_normed = (scaled_tr * w["gain_tr"] + w["bias_tr"]).astype(BF16)
    hidden = dot(trans_normed, w["up"])
    activated = jax.nn.silu(hidden).astype(BF16)
    result = (first_state + dot(activated, w["down"])).astype(BF16)
    saved = (gate_sigma, scaled_mid, inv_mid, mixed_norm, update, scaled_tr, inv_tr, trans_normed, hidden, activated)
    return result, saved


def back_upper(grad_final, saved, w):
    gate_sigma, scaled_mid, inv_mid, mixed_norm, update, scaled_tr, inv_tr, trans_normed, hidden, activated = saved
    grads = {}
    grad_trans = grad_final.astype(BF16)
    grads["down"] = outer(activated, grad_trans)
    grad_act = dot_t(grad_trans, w["down"])
    sigma = jax.nn.sigmoid(hidden)
    grad_hidden = (grad_act * sigma * (1.0 + hidden * (1.0 - sigma))).astype(BF16)
    grads["up"] = outer(trans_normed, grad_hidden)
    grad_tnorm = dot_t(grad_hidden, w["up"])
    grads["gain_tr"] = jnp.sum(grad_tnorm * scaled_tr, axis=(0, 1))
    grads["bias_tr"] = jnp.sum(grad_tnorm, axis=(0, 1))
    grad_result = grad_final + norm_back(grad_tnorm * w["gain_tr"], scaled_tr, inv_tr)
    grad_update = (grad_result * gate_sigma).astype(BF16)
    grad_gate = (grad_result * update * gate_sigma * (1.0 - gate_sigma)).astype(BF16)
    grads["out"] = outer(mixed_norm, grad_update)
    grad_norm_mid = dot_t(grad_update, w["out"])
    grads["gain_out"] = jnp.sum(grad_norm_mid * scaled_mid, axis=(0, 1))
    grads["bias_out"] = jnp.sum(grad_norm_mid, axis=(0, 1))
    grad_mixed = norm_back(grad_norm_mid * w["gain_out"], scaled_mid, inv_mid).astype(BF16)
    return grad_result, grad_gate, grad_mixed, grads


def back_lower(state, normed, mask, grad_result, grad_gate, grad_left, grad_right, w):
    scaled_in, inv_in = norm_stats(state)
    projected = dot(normed, w["proj"])
    width = projected.shape[-1] // 4
    lv, lg, rv, rg = (projected[..., i * width : (i + 1) * width] for i in range(4))
    ls = jax.nn.sigmoid(lg)
    rs = jax.nn.sigmoid(rg)
    gl = grad_left.astype(F32) * mask
    gr = grad_right.astype(F32) * mask
    grad_proj = jnp.concatenate(
        [gl * ls, gl * lv * ls * (1.0 - ls), gr * rs, gr * rv * rs * (1.0 - rs)], axis=-1
    ).astype(BF16)
    grads = {"proj": outer(normed, grad_proj), "gate": outer(normed, grad_gate)}
    grad_normed = dot_t(grad_proj, w["proj"]) + dot_t(grad_gate, w["gate"])
    grads["gain_in"] = jnp.sum(grad_normed * scaled_in, axis=(0, 1))
    grads["bias_in"] = jnp.sum(grad_normed, axis=(0, 1))
    return grad_result + norm_back(grad_normed * w["gain_in"], scaled_in, inv_in), grads


def product(left, right):
    n, held, rows, cols = left.shape
    mixed = jnp.einsum("atik,btjk->taibj", left, right, preferred_element_type=F32)
    return jnp.transpose(mixed.reshape(held, n, rows, n * rows), (1, 0, 2, 3)).astype(BF16)


def product_back(grad_mixed, left, right):
    n, held, rows, cols = left.shape
    split = grad_mixed.reshape(n, held, rows, n, rows)
    grad_left = jnp.einsum("atibj,btjk->atik", split, right, preferred_element_type=F32)
    grad_right = jnp.einsum("atibj,atik->btjk", split, left, preferred_element_type=F32)
    return grad_left.astype(BF16), grad_right.astype(BF16)


BLOCK_ROWS = 12
LANES = 128
VMEM = 63 << 20


def sig(x):
    return 0.5 * jnp.tanh(0.5 * x) + 0.5


def mm(a, b, ca=1, cb=0):
    return lax.dot_general(a, b, (((ca,), (cb,)), ((), ())), preferred_element_type=F32)


def col_stats(values):
    centred = values - jnp.mean(values, axis=0, keepdims=True)
    inv_scale = lax.rsqrt(jnp.mean(centred * centred, axis=0, keepdims=True) + EPSILON)
    return centred * inv_scale, inv_scale


def col_back(grad_scaled, scaled, inv_scale):
    mean_grad = jnp.mean(grad_scaled, axis=0, keepdims=True)
    mean_cross = jnp.mean(grad_scaled * scaled, axis=0, keepdims=True)
    return inv_scale * (grad_scaled - mean_grad - scaled * mean_cross)


def fold(values):
    return jnp.sum(values.reshape(values.shape[0] // 8, 8, values.shape[1]), axis=0)


class Step:
    def __init__(self, place, n, rows, held, block_rows, crop, last, used, chunks):
        self.last = last
        self.live = pl.program_id(0) < used if used < chunks else None
        self.n, self.rows, self.held, self.block = n, rows, held, block_rows
        self.row = pl.program_id(1) * block_rows
        self.length, self.base, self.group = place[crop], place[2], place[3]
        column = pl.program_id(0) * LANES + lax.broadcasted_iota(jnp.int32, (1, LANES), 1)
        self.columns = (column < self.length).astype(F32)

    def mask(self, r):
        return self.columns * jnp.where(self.base + self.row + r < self.length, 1.0, 0.0)

    def flat(self, ref):
        return ref[...].reshape(self.block * LANES, ref.shape[-1])

    def pick(self, pair, section):
        own, got = (self.flat(ref).astype(F32) for ref in pair)
        return jnp.where(jnp.full(own.shape, self.group) == section, own, got)

    def put(self, ref, value):
        ref[...] = value.reshape(self.block, LANES, value.shape[-1]).astype(ref.dtype)

    def lanes(self, r):
        return slice(r * LANES, (r + 1) * LANES)

    def spans(self, r):
        return [pl.ds((self.row + r) * self.held + t, self.n, stride=self.rows * self.held) for t in range(self.held)]

    def load(self, scratch, r):
        return jnp.concatenate([scratch[span, :] for span in self.spans(r)], axis=0)

    def store(self, scratch, r, value):
        for t, span in enumerate(self.spans(r)):
            scratch[span, :] = value[t * self.n : (t + 1) * self.n, :]


def unpack(ref, scratch, first=0):
    n, size = ref.shape[0], scratch.shape[0] // (ref.shape[0] + 1)

    def body(d, carry):
        scratch[pl.ds(pl.multiple_of(d * size, 8), size), :] = ref[d, first : first + size, :].astype(F32)
        return carry

    lax.fori_loop(0, n, body, 0)


def pack(scratch, ref, first=0):
    n, size = ref.shape[0], scratch.shape[0] // (ref.shape[0] + 1)

    def body(d, carry):
        ref[d, first : first + size, :] = scratch[pl.ds(pl.multiple_of(d * size, 8), size), :].astype(ref.dtype)
        return carry

    lax.fori_loop(0, n, body, 0)


def fetch(st, ref, scratch, first=0):
    if st.live is None:
        return unpack(ref, scratch, first)

    @pl.when(st.live)
    def _():
        unpack(ref, scratch, first)

    @pl.when(jnp.logical_not(st.live))
    def _():
        scratch[...] = jnp.zeros(scratch.shape, scratch.dtype)


def deliver(st, scratch, ref, first=0):
    if st.live is None:
        return pack(scratch, ref, first)
    pl.when(st.live)(lambda: pack(scratch, ref, first))


def at_first(action):
    pl.when(pl.program_id(1) == 0)(action)


def at_last(action):
    pl.when(pl.program_id(1) == pl.num_programs(1) - 1)(action)


def clear(accs, olds, cols=()):
    @pl.when((pl.program_id(0) == 0) & (pl.program_id(1) == 0))
    def _():
        for k, ref in enumerate(accs):
            ref[...] = olds[k][...] if olds else jnp.zeros(ref.shape, ref.dtype)
        for ref in cols:
            ref[...] = jnp.zeros(ref.shape, ref.dtype)


def add_blocks(ref, first, value):
    for q in range(value.shape[1] // LANES):
        ref[first + q * LANES : first + (q + 1) * LANES, :] += value[:, q * LANES : (q + 1) * LANES]


def close(st, ref, cols=None):
    @pl.when((pl.program_id(0) == pl.num_programs(0) - 1) & (pl.program_id(1) == pl.num_programs(1) - 1))
    def _():
        for k in range(2 if cols is not None else 0):
            row = UP_VEC + 16 + 8 * k
            ref[row : row + 1, :] += jnp.sum(jnp.transpose(cols[k]), axis=0, keepdims=True)
        for q in range(4 if st.last else 0):
            block = slice(q * LANES, (q + 1) * LANES)
            ref[block, :] = jnp.transpose(ref[block, :])


def pre_part(st, state, w, normed_ref, left_scr, right_scr):
    scaled, _ = norm_stats(state)
    normed = (scaled * w.vec[0:1, :] + w.vec[1:2, :]).astype(BF16)
    st.put(normed_ref, normed)
    projected = mm(w.proj_t[...], normed, 1, 1)
    for r in range(st.block):
        lv, lg, rv, rg = (projected[q * LANES : (q + 1) * LANES, st.lanes(r)] for q in range(4))
        mask = st.mask(r)
        st.store(left_scr, r, sig(lg) * lv * mask)
        st.store(right_scr, r, sig(rg) * rv * mask)


def post_part(st, state, normed, mixed_scr, w):
    mids = [col_stats(st.load(mixed_scr, r)) for r in range(st.block)]
    gain, bias = w.col[0], w.col[1]
    mixed_norm = jnp.concatenate([(scaled * gain + bias).astype(BF16) for scaled, _ in mids], axis=1)
    update = mm(mixed_norm, w.out[...], 0, 0)
    gate = sig(mm(normed, w.gate[...]))
    first_state = state + gate * update
    scaled_tr, inv_tr = norm_stats(first_state)
    trans = (scaled_tr * w.vec[2:3, :] + w.vec[3:4, :]).astype(BF16)
    hidden = mm(trans, w.up[...])
    sigma = sig(hidden)
    activated = (hidden * sigma).astype(BF16)
    return mids, mixed_norm, update, gate, first_state, scaled_tr, inv_tr, trans, hidden, sigma, activated


def upper_part(st, grad_final, kept, w, acc, cols, grad_ref, gate_ref, mixed_scr):
    mids, mixed_norm, update, gate, first_state, scaled_tr, inv_tr, trans, hidden, sigma, activated = kept
    low = grad_final.astype(BF16)
    add_blocks(acc, 0, mm(low, activated, 0, 0))
    grad_hidden = (mm(low, w.down[...], 1, 1) * (sigma * (1.0 + hidden * (1.0 - sigma)))).astype(BF16)
    add_blocks(acc, 4 * LANES, mm(trans, grad_hidden, 0, 0))
    grad_tnorm = mm(grad_hidden, w.up[...], 1, 1)
    acc[UP_VEC : UP_VEC + 8, :] += fold(grad_tnorm * scaled_tr)
    acc[UP_VEC + 8 : UP_VEC + 16, :] += fold(grad_tnorm)
    grad_result = grad_final + norm_back(grad_tnorm * w.vec[2:3, :], scaled_tr, inv_tr)
    st.put(grad_ref, grad_result)
    scaled_grad = grad_result * gate
    grad_update = scaled_grad.astype(BF16)
    st.put(gate_ref, scaled_grad * update * (1.0 - gate))
    add_blocks(acc, 8 * LANES, mm(mixed_norm, grad_update))
    grad_norm = mm(w.out[...], grad_update, 1, 1)
    for r, (scaled, inv_scale) in enumerate(mids):
        grad = grad_norm[:, st.lanes(r)]
        cols[0] += grad * scaled
        cols[1] += grad
        st.store(mixed_scr, r, col_back(grad * w.col[0], scaled, inv_scale) * st.mask(r))


def lower_part(st, state, normed, grad_result, grad_gate, left_scr, right_scr, w, acc):
    projected = mm(w.proj_t[...], normed, 1, 1)
    parts = []
    for r in range(st.block):
        lv, lg, rv, rg = (projected[q * LANES : (q + 1) * LANES, st.lanes(r)] for q in range(4))
        ls, rs = sig(lg), sig(rg)
        a, b = st.load(left_scr, r) * ls, st.load(right_scr, r) * rs
        parts.append(jnp.concatenate([v.astype(BF16) for v in (a, a * lv * (1.0 - ls), b, b * rv * (1.0 - rs))], axis=0))
    grad_proj = jnp.concatenate(parts, axis=1)
    acc[: 4 * LANES, :] += mm(grad_proj, normed)
    add_blocks(acc, 4 * LANES, mm(normed, grad_gate, 0, 0))
    grad_normed = jnp.transpose(mm(w.proj[...], grad_proj)) + mm(grad_gate, w.gate[...], 1, 1)
    scaled_in, inv_in = norm_stats(state)
    acc[LOW_VEC : LOW_VEC + 8, :] += fold(grad_normed * scaled_in)
    acc[LOW_VEC + 8 : LOW_VEC + 16, :] += fold(grad_normed)
    return grad_result + norm_back(grad_normed * w.vec[0:1, :], scaled_in, inv_in)


class Weights:
    def __init__(self, group, section, refs, scratch):
        self.wide, self.down, self.vec, self.col, self.proj_t = scratch
        cut = lambda first, count: self.wide.at[:, first * LANES : (first + count) * LANES]
        self.proj, self.gate, self.out, self.up = cut(0, 4), cut(4, 1), cut(5, 1), cut(6, 4)

        @pl.when((pl.program_id(0) == 0) & (pl.program_id(1) == 0))
        def _():
            for chosen, sources in ((group == section, refs[:3]), (group != section, refs[3:])):

                @pl.when(chosen)
                def _():
                    for ref, source in zip((self.wide, self.down, self.vec), sources):
                        ref[...] = source[...]

            for k in range(2):
                self.col[k] = jnp.transpose(jnp.broadcast_to(self.vec[4 + k : 5 + k, :], (LANES, LANES)))
            for q in range(4):
                block = slice(q * LANES, (q + 1) * LANES)
                self.proj_t[block, :] = jnp.transpose(self.wide[:, block])

    @staticmethod
    def scratch():
        return [
            pltpu.VMEM((LANES, 10 * LANES), BF16), pltpu.VMEM((4 * LANES, LANES), BF16), pltpu.VMEM((8, LANES), F32),
            pltpu.VMEM((2, LANES, LANES), F32), pltpu.VMEM((4 * LANES, LANES), BF16),
        ]


def pack_weights(w):
    zero = jnp.zeros_like(w["gain_in"])
    names = ("gain_in", "bias_in", "gain_tr", "bias_tr", "gain_out", "bias_out")
    wide = jnp.concatenate([w[name] for name in ("proj", "gate", "out", "up")], axis=1)
    return wide, w["down"], jnp.stack([w[name] for name in names] + [zero, zero])


UP_VEC = 9 * LANES
UP_ROWS = UP_VEC + 32
LOW_VEC = 5 * LANES
LOW_ROWS = LOW_VEC + 16


def k_pre(cfg, place, own, got, *refs):
    st = Step(place, *cfg)
    w = Weights(st.group, 0, refs[:6], refs[-5:])
    normed, both, left, right = refs[6:-5]
    pre_part(st, st.pick((own, got), 0), w, normed, left, right)

    @at_last
    def _():
        deliver(st, left, both)
        deliver(st, right, both, both.shape[1] // 2)


def k_post_pre(cfg, place, own_0, got_0, own_1, got_1, normed_in, mixed_in, *refs):
    st = Step(place, *cfg)
    w0, w1 = Weights(st.group, 0, refs[:6], refs[-10:-5]), Weights(st.group, 1, refs[:6], refs[-5:])
    *_, home, out, normed, both, mixed, left, right = refs[6:-10]
    at_first(lambda: fetch(st, mixed_in, mixed))
    kept = post_part(st, st.pick((own_0, got_0), 0), st.flat(normed_in), mixed, w0)
    result = (kept[4] + mm(kept[-1], w0.down[...])).astype(BF16)
    st.put(home, result)
    st.put(out, result)
    pre_part(st, result.astype(F32) + st.pick((own_1, got_1), 1), w1, normed, left, right)

    @at_last
    def _():
        deliver(st, left, both)
        deliver(st, right, both, both.shape[1] // 2)


def k_post_upper(cfg, place, own, got, own_cot, got_cot, before, normed_in, mixed_in, *refs):
    st = Step(place, *cfg)
    w = Weights(st.group, 1, refs[:6], refs[-5:])
    _, *olds, home, out, grad, gate, grad_mixed, sums, mixed, cols = refs[6:-5]
    clear([sums], olds, [cols])
    at_first(lambda: fetch(st, mixed_in, mixed))
    state = st.flat(before).astype(F32) + st.pick((own, got), 1)
    kept = post_part(st, state, st.flat(normed_in), mixed, w)
    result = kept[4] + mm(kept[-1], w.down[...])
    st.put(home, result)
    st.put(out, result)
    upper_part(st, st.pick((own_cot, got_cot), 1), kept, w, sums, cols, grad, gate, mixed)
    close(st, sums, cols)
    at_last(lambda: deliver(st, mixed, grad_mixed))


def k_lower_upper(
    cfg, place, own_1, got_1, own_0, got_0, own_cot, got_cot, before, normed_1, grad_1, gate_1, normed_0, both, mixed_in, *refs
):
    st = Step(place, *cfg)
    w1, w0 = Weights(st.group, 1, refs[:6], refs[-10:-5]), Weights(st.group, 0, refs[:6], refs[-5:])
    olds = refs[7:9] if cfg[4] else ()
    home, pair_grad, grad, gate, grad_mixed, low_sums, up_sums, left, right, mixed, cols = refs[-21:-10]
    clear([low_sums, up_sums], olds, [cols])

    @at_first
    def _():
        fetch(st, both, left)
        fetch(st, both, right, both.shape[1] // 2)
        fetch(st, mixed_in, mixed)

    state = st.flat(before).astype(F32) + st.pick((own_1, got_1), 1)
    grad_state = lower_part(
        st, state, st.flat(normed_1), st.flat(grad_1), st.flat(gate_1), left, right, w1, low_sums
    )
    st.put(home, grad_state)
    st.put(pair_grad, grad_state)
    kept = post_part(st, st.pick((own_0, got_0), 0), st.flat(normed_0), mixed, w0)
    grad_final = st.pick((own_cot, got_cot), 0) + grad_state.astype(BF16).astype(F32)
    upper_part(st, grad_final, kept, w0, up_sums, cols, grad, gate, mixed)
    close(st, low_sums)
    close(st, up_sums, cols)
    at_last(lambda: deliver(st, mixed, grad_mixed))


def k_lower(cfg, place, own, got, normed, grad, gate, both, *refs):
    st = Step(place, *cfg)
    w = Weights(st.group, 0, refs[:6], refs[-5:])
    _, *olds, home, pair_grad, sums, parts, left, right = refs[6:-5]
    clear([sums], olds)

    @at_first
    def _():
        fetch(st, both, left)
        fetch(st, both, right, both.shape[1] // 2)

    state = st.pick((own, got), 0)
    grad_state = lower_part(
        st, state, st.flat(normed), st.flat(grad), st.flat(gate), left, right, w, sums
    )
    st.put(home, grad_state)
    st.put(pair_grad, grad_state)
    close(st, sums)

    @pl.when((pl.program_id(0) == pl.num_programs(0) - 1) & (pl.program_id(1) == pl.num_programs(1) - 1))
    def _():
        n, rows, _ = parts.shape
        parts[...] = jnp.zeros(parts.shape, BF16)
        for d in range(n):
            count = max(0, min(rows, LOW_ROWS - d * rows))
            if count:
                parts[d, :count, :] = sums[d * rows : d * rows + count, :].astype(BF16)


def k_results(total, proj, gate, gain_in, bias_in, out, gain_out, bias_out, gain_tr, bias_tr, up, down, early, low):
    n = total.shape[0]
    first, second = early.shape[0] // n, low.shape[0] // n
    for d in range(n):
        early[d * first : (d + 1) * first, :] = total[d, :first, :].astype(F32)
        low[d * second : (d + 1) * second, :] = total[d, first:, :].astype(F32)
    down[0] = early[: 4 * LANES, :]
    for q in range(4):
        up[0, :, q * LANES : (q + 1) * LANES] = early[(4 + q) * LANES : (5 + q) * LANES, :]
        proj[0, :, q * LANES : (q + 1) * LANES] = low[q * LANES : (q + 1) * LANES, :]
    out[0] = early[8 * LANES : UP_VEC, :]
    gate[0] = low[4 * LANES : LOW_VEC, :]
    for k, ref in enumerate((gain_tr, bias_tr, gain_out, bias_out)):
        ref[...] = jnp.sum(early[UP_VEC + 8 * k : UP_VEC + 8 * k + 8, :], axis=0, keepdims=True)
    for k, ref in enumerate((gain_in, bias_in)):
        ref[...] = jnp.sum(low[LOW_VEC + 8 * k : LOW_VEC + 8 * k + 8, :], axis=0, keepdims=True)


def spread(ref, scratch, first=0):
    n, size = ref.shape[0], (scratch.shape[1] - 8) // ref.shape[0]

    def body(d, carry):
        for c in range(scratch.shape[0]):
            value = ref[d, first : first + size, c * LANES : (c + 1) * LANES]
            scratch[c, pl.ds(pl.multiple_of(d * size, 8), size), :] = value.astype(F32)
        return carry

    lax.fori_loop(0, n, body, 0)


def gather(scratch, ref, first=0):
    n, size = ref.shape[0], (scratch.shape[1] - 8) // ref.shape[0]

    def body(d, carry):
        for c in range(scratch.shape[0]):
            value = scratch[c, pl.ds(pl.multiple_of(d * size, 8), size), :]
            ref[d, first : first + size, c * LANES : (c + 1) * LANES] = value.astype(ref.dtype)
        return carry

    lax.fori_loop(0, n, body, 0)


def channel(scratch, t, held):
    chunks, size, _ = scratch.shape
    span = pl.ds(t, (size - 8) // held, stride=held)
    return jnp.concatenate([scratch[c, span, :].astype(BF16) for c in range(chunks)], axis=1)


def put_channel(scratch, t, held, value):
    chunks, size, _ = scratch.shape
    span = pl.ds(t, (size - 8) // held, stride=held)
    for c in range(chunks):
        scratch[c, span, :] = value[:, c * LANES : (c + 1) * LANES]


def k_product(held, both, out, left, right):
    spread(both, left)
    spread(both, right, both.shape[1] // 2)

    def body(t, carry):
        others = channel(right, t, held)[: left.shape[0] * LANES]
        put_channel(left, t, held, mm(channel(left, t, held), others, 1, 1))
        return carry

    lax.fori_loop(0, held, body, 0)
    gather(left, out)


def k_product_back(held, grad_in, both, out, grad, left, right):
    spread(grad_in, grad)
    spread(both, left)
    spread(both, right, both.shape[1] // 2)

    def body(t, carry):
        low, lv, rv = channel(grad, t, held), channel(left, t, held), channel(right, t, held)
        put_channel(left, t, held, mm(low, rv[: low.shape[1]]))
        grad_right = mm(low, lv, 0, 0)
        if low.shape[1] < rv.shape[0]:
            rest = jnp.zeros((rv.shape[0] - low.shape[1], lv.shape[1]), F32)
            grad_right = jnp.concatenate([grad_right, rest])
        put_channel(right, t, held, grad_right)
        return carry

    lax.fori_loop(0, held, body, 0)
    gather(left, out)
    gather(right, out, both.shape[1] // 2)


STEPS = """\
1A SA0 1B SB0 TA0 MA0 TB0 MB0 2A SA1 2B SB1 TA1 MA1 TB1 MB1 3A GA1 3B GB1 tA1 sA1 tB1 sB1 HA HB 4A GA0 4B GB0 tA0 sA0 tB0 sB0 EB0 QB0 5A JA 5B qB0 JB AB0
"""


class Kernels:
    def __init__(self, place, used, n, rows, cols, channels, block_rows):
        self.place, self.used, self.crops = place, used, len(used)
        self.n, self.rows, self.cols, self.channels, self.block = n, rows, cols, channels, block_rows
        self.held = channels // n
        self.size = rows * self.held
        self.chunks = cols // LANES

    def row_call(self, body, crop, ins, outs, scratch, micros, cols=0, sections=1):
        rows, block = self.rows, self.block

        def spec(kind, shape):
            if kind == "own":
                return pl.BlockSpec(
                    (pl.squeezed, block, LANES, shape[-1]), lambda c, i, s: (s[4 + crop], s[3] * (rows // block) + i, c, 0)
                )
            if kind in ("home 0", "home 1"):
                first = int(kind[-1]) * (rows // block)
                return pl.BlockSpec((pl.squeezed, block, LANES, shape[-1]), lambda c, i, s: (s[4 + crop], first + i, c, 0))
            if kind == "rows":
                return pl.BlockSpec((block, LANES, shape[-1]), lambda c, i, s: (i, c, 0))
            if kind == "moved":
                final = shape[-1] // LANES - 1
                return pl.BlockSpec(shape[:-1] + (LANES,), lambda c, i, s: (0, 0, jnp.minimum(c, final)))
            if kind == "kept":
                return pl.BlockSpec(memory_space=pl.ANY)
            zeros = (0,) * len(shape)
            return pl.BlockSpec(shape, lambda c, i, s: zeros)

        aliases = {1 + k: 0 for k, (kind, _) in enumerate(ins) if kind == "kept"}
        return pl.pallas_call(
            functools.partial(
                body, (self.n, rows, self.held, block, crop, crop == self.crops - 1, self.used[crop], self.chunks)
            ),
            out_shape=tuple(v for _, v in outs),
            grid_spec=pltpu.PrefetchScalarGridSpec(
                num_scalar_prefetch=1,
                grid=(self.chunks, rows // block),
                in_specs=[spec(k, v.shape) for k, v in ins],
                out_specs=tuple(spec(k, v.shape) for k, v in outs),
                scratch_shapes=[pltpu.VMEM(((self.n + 1) * self.size, LANES), F32)] * scratch
                + [pltpu.VMEM((2, self.channels, LANES), F32)] * cols
                + Weights.scratch() * sections,
            ),
            input_output_aliases=aliases,
            compiler_params=pltpu.CompilerParams(vmem_limit_bytes=VMEM),
            cost_estimate=cost(micros),
        )(self.place, *[v for _, v in ins])

    def home(self, section, dtype):
        return (f"home {section}", jax.ShapeDtypeStruct((self.crops, 2 * self.rows, self.cols, self.channels), dtype))

    def pairs(self, dtype):
        return ("rows", jax.ShapeDtypeStruct((self.rows, self.cols, self.channels), dtype))

    def moved(self, crop, count=1):
        return ("moved", jax.ShapeDtypeStruct((self.n, count * self.size, self.used[crop] * LANES), BF16))

    def sums(self, rows):
        return ("all", jax.ShapeDtypeStruct((rows, self.channels), F32))

    def channel_call(self, body, ins, out, scratch, micros):
        spec = pl.BlockSpec(memory_space=pltpu.VMEM)
        return pl.pallas_call(
            functools.partial(body, self.held),
            out_shape=out[1],
            in_specs=[spec] * len(ins),
            out_specs=spec,
            scratch_shapes=[pltpu.VMEM((out[1].shape[2] // LANES, self.n * self.size + 8, LANES), F32)] * scratch,
            compiler_params=pltpu.CompilerParams(vmem_limit_bytes=VMEM),
            cost_estimate=cost(micros),
        )(*ins)


def cost(micros):
    return pl.CostEstimate(flops=int(micros * 1.15e9), bytes_accessed=int(micros * 1e6), transcendentals=0)


def steps(kernels, crops, pair, cot, weights, early, late_share, other_half, meet):
    w = [("all", v) for v in weights]
    call, pairs, moved = kernels.row_call, kernels.pairs, kernels.moved
    up_sums, low_sums = kernels.sums(UP_ROWS), kernels.sums(LOW_ROWS)
    earlier = lambda *names: [("all", state[0][name]) for name in names if name in state[0]]
    homes = {}
    kept = lambda name: [("kept", homes[name])]
    mine = lambda v, crop: [("own", v[0]), ("rows", v[1][crop])]
    part = lambda *vs: [("rows", v) for v in vs]
    far = lambda *vs: [("moved", v) for v in vs]
    swap = lambda v: lax.all_to_all(v, ("row", "grp"), 0, 0)
    spread_rows = lambda v: lax.all_to_all(v, "row", 0, 0)
    state = [dict() for _ in range(crops)]
    last = {}

    def ordered(kind, op, value):
        if kind in last:
            value, _ = lax.optimization_barrier((value, last[kind]))
        result = op(value)
        last[kind] = result[0] if isinstance(result, (tuple, list)) else result
        return result

    def row_kernel(body, crop, ins, *rest):
        return ordered("kernel", lambda v: call(body, crop, [(ins[0][0], v)] + ins[1:], *rest), ins[0][1])

    def channel_kernel(body, ins, *rest):
        return ordered("kernel", lambda v: kernels.channel_call(body, (v,) + tuple(ins[1:]), *rest), ins[0])

    def pre(crop, s):
        s["normed_0"], s["both_0"] = row_kernel(k_pre, crop, mine(pair, crop) + w, [pairs(BF16), moved(crop, 2)], 2, 10)

    def post_pre(crop, s):
        homes["out"], s["out_0"], s["normed_1"], s["both_1"] = row_kernel(
            k_post_pre, crop,
            mine(pair, crop) + mine(pair, crop) + part(s["normed_0"]) + far(s["mixed_0"]) + w + (kept("out") if crop else []),
            [kernels.home(0, BF16), pairs(BF16), pairs(BF16), moved(crop, 2)], 3, 18, 0, 2,
        )
        s["got_out_0"] = other_half(s["out_0"], 0)

    def post_upper(crop, s):
        homes["out"], s["out_1"], s["grad_1"], s["gate_1"], s["grad_mixed_1"], s["up_1"] = row_kernel(
            k_post_upper, crop,
            mine(pair, crop) + mine(cot, crop) + part(s["out_0"], s["normed_1"]) + far(s["mixed_1"]) + w + kept("out")
            + earlier("up_1"),
            [kernels.home(1, BF16), pairs(BF16), pairs(F32), pairs(BF16), moved(crop), up_sums], 1, 23, 1,
        )
        s["got_out_1"] = other_half(s["out_1"], 1)

    def lower_upper(crop, s):
        homes["grad"], s["pair_grad_1"], s["grad_0"], s["gate_0"], s["grad_mixed_0"], s["low_1"], s["up_0"] = row_kernel(
            k_lower_upper, crop,
            mine(pair, crop) + mine(pair, crop) + mine(cot, crop)
            + part(s["out_0"], s["normed_1"], s["grad_1"], s["gate_1"], s["normed_0"])
            + far(s["back_1"], s["mixed_0"]) + w + (kept("grad") if crop else []) + earlier("low_1", "up_0"),
            [kernels.home(1, F32), pairs(F32), pairs(F32), pairs(BF16), moved(crop), low_sums, up_sums], 3, 31, 1, 2,
        )
        s["got_grad_1"] = other_half(s["pair_grad_1"], 1)

    def lower(crop, s):
        homes["grad"], s["pair_grad_0"], s["low_0"], s["late"] = row_kernel(
            k_lower, crop, mine(pair, crop) + part(s["normed_0"], s["grad_0"], s["gate_0"]) + far(s["back_0"]) + w
            + kept("grad") + earlier("low_0"),
            [kernels.home(0, F32), pairs(F32), low_sums, ("all", jax.ShapeDtypeStruct(share_shape(LOW_ROWS), BF16))], 2, 13,
        )
        s["got_grad_0"] = other_half(s["pair_grad_0"], 0)

    def product(crop, s, k):
        s[f"product_{k}"] = channel_kernel(k_product, (s[f"factors_{k}"],), moved(crop), 2, 6)

    def product_back(crop, s, k):
        s[f"grads_{k}"] = channel_kernel(k_product_back, (s[f"g_{k}"], s[f"factors_{k}"]), moved(crop, 2), 3, 12)

    transfers = dict(S=("factors", "both"), M=("mixed", "product"), G=("g", "grad_mixed"), s=("back", "grads"))
    rows_of = {"1": pre, "2": post_pre, "3": post_upper, "4": lower_upper, "5": lower}
    channels_of = {"T": product, "t": product_back}
    for step in STEPS.split():
        what, crop, k = step[0], "AB".index(step[1]), step[2:]
        s = state[crop]
        if what == "E":
            sums = {name: lax.optimization_barrier((s[name], last["kernel"]))[0] for name in ("up_0", "up_1", "low_1")}
            last["kernel"] = s["early"] = early(sums)
        elif what in "QqA":
            if what == "A":
                s["total"] = ordered("swap", spread_rows, late_share(s["share_q"], s["share_Q"]))
            else:
                moved_parts = ordered("swap", spread_rows, s["early" if what == "Q" else "late"])
                s[f"share_{what}"] = jnp.sum(moved_parts.astype(F32), axis=0)
        elif what in "HJ":
            name = "out" if what == "H" else "grad"
            homes[name] = meet(homes[name], crop, s[f"got_{name}_0"], s[f"got_{name}_1"])
            if what == "H":
                last["kernel"] = homes[name]
        elif what in rows_of:
            rows_of[what](crop, s)
        elif what in channels_of:
            channels_of[what](crop, s, k)
        else:
            new, old = transfers[what]
            s[f"{new}_{k}"] = ordered("swap", swap, s[f"{old}_{k}"])

    return state, homes


def share_shape(rows):
    n = lax.axis_size("row")
    return (n, -(-rows // (16 * n)) * 16, LANES)


def in_shares(sums):
    n, rows, _ = share_shape(sums.shape[0])
    return jnp.pad(sums, ((0, n * rows - sums.shape[0]), (0, 0))).reshape(n, rows, LANES)


def early_sums(first, swap, sums):
    early_0 = jnp.concatenate([sums["up_0"], jnp.zeros((LOW_ROWS, LANES), F32)])
    early_1 = jnp.concatenate([sums["up_1"], sums["low_1"]])
    early = jnp.where(first, early_0, early_1) + swap(jnp.where(first, early_1, early_0))
    return jnp.concatenate([in_shares(early[:UP_ROWS]), in_shares(early[UP_ROWS:])], axis=1).astype(BF16)


def late_share(first, late, early):
    late = jnp.where(first, late, 0.0) + lax.ppermute(late, "grp", [(1, 0)])
    rows = early.shape[0] - late.shape[0]
    share = jnp.concatenate([early[:rows], early[rows:] + late]).astype(BF16)
    return jnp.broadcast_to(share[None], (lax.axis_size("row"),) + share.shape)


def plain_steps(n, base, crop_length, pair_0, pair_1, cot_0, cot_1, weights):
    rows, cols = pair_0.shape[:2]
    own_rows = base + jnp.arange(rows)
    mask = (own_rows < crop_length).astype(F32)[:, None, None] * (jnp.arange(cols) < crop_length).astype(F32)[None, :, None]

    def send(*values):
        return swap_rows(jnp.stack([to_channels(v, n) for v in values], axis=1))

    w0, w1 = weights
    state_0 = pair_0.astype(F32)
    normed_0, left, right = pre(state_0, mask, w0)
    lr_0 = send(left, right)
    mixed_0 = from_channels(swap_rows(product(lr_0[:, 0], lr_0[:, 1]))).astype(F32)
    out_0, saved_0 = post(state_0, normed_0, mixed_0, w0)
    state_1 = out_0.astype(F32) + pair_1.astype(F32)
    normed_1, left, right = pre(state_1, mask, w1)
    lr_1 = send(left, right)
    mixed_1 = from_channels(swap_rows(product(lr_1[:, 0], lr_1[:, 1]))).astype(F32)
    out_1, saved_1 = post(state_1, normed_1, mixed_1, w1)
    grad_result, grad_gate, grad_mixed, upper_1 = back_upper(cot_1.astype(F32), saved_1, w1)
    gm = send(grad_mixed)
    glr = swap_rows(jnp.stack(product_back(gm[:, 0], lr_1[:, 0], lr_1[:, 1]), axis=1))
    grad_1, lower_1 = back_lower(
        state_1, normed_1, mask, grad_result, grad_gate, from_channels(glr[:, 0]), from_channels(glr[:, 1]), w1
    )
    grad_final = cot_0.astype(F32) + grad_1.astype(BF16).astype(F32)
    grad_result, grad_gate, grad_mixed, upper_0 = back_upper(grad_final, saved_0, w0)
    gm = send(grad_mixed)
    glr = swap_rows(jnp.stack(product_back(gm[:, 0], lr_0[:, 0], lr_0[:, 1]), axis=1))
    grad_0, lower_0 = back_lower(
        state_0, normed_0, mask, grad_result, grad_gate, from_channels(glr[:, 0]), from_channels(glr[:, 1]), w0
    )
    return out_0, out_1, grad_0, grad_1, {**upper_0, **lower_0}, {**upper_1, **lower_1}


ORDER = ("gain_in", "bias_in", "proj", "gate", "out", "gain_out", "bias_out", "gain_tr", "bias_tr", "up", "down")


def per_device(pair_in, crop_lengths, gain_in, bias_in, proj, gate, out, gain_out, bias_out, gain_tr, bias_tr, up, down, pair_cot):
    own_weights = dict(
        gain_in=gain_in[0], bias_in=bias_in[0], proj=proj[0], gate=gate[0], out=out[0], gain_out=gain_out[0],
        bias_out=bias_out[0], gain_tr=gain_tr[0], bias_tr=bias_tr[0], up=up[0], down=down[0],
    )
    groups, count = lax.axis_size("grp"), lax.axis_size("row")
    crops, rows, cols, channels = pair_in.shape[1:]
    group = lax.axis_index("grp")
    first = group == 0
    base = lax.axis_index("row") * rows
    swap = lambda v: lax.ppermute(v, "grp", [(0, 1), (1, 0)])
    pick = lambda v, i: lax.dynamic_index_in_dim(v, i, 0, keepdims=False)
    n = groups * count
    my_rows = rows // 2
    sizes = channels == LANES and out.shape[1] == LANES and up.shape[2] == 4 * LANES and crops == 2 and groups == 2
    if sizes and rows % 2 == 0 and my_rows % BLOCK_ROWS == 0 and cols % LANES == 0 and channels % n == 0 and n % 8 == 0 and (my_rows * (channels // n)) % 16 == 0:
        before_last = (cols // LANES - 1) * LANES
        swapped = crop_lengths[0] <= before_last
        which = [jnp.where(swapped, 1, 0), jnp.where(swapped, 0, 1)]
        lengths = [crop_lengths[crop] for crop in which]
        place = jnp.stack(lengths + [base + group * my_rows, group] + which).astype(jnp.int32)
        def shared(value):
            got, source = [], value
            for crop in which:
                got.append(swap(lax.dynamic_slice(source, (crop, (1 - group) * my_rows, 0, 0), (1, my_rows, cols, channels))[0]))
                source, _ = lax.optimization_barrier((value, got[-1]))
            return value, got

        def meet(home, crop, got_0, got_1):
            half = jnp.where(first, got_0, got_1)[None]
            return lax.dynamic_update_slice(home, half, (which[crop], (1 - group) * my_rows, 0, 0))

        def run(used):
            other_half = lambda value, section: lax.ppermute(value, "grp", [(1 - section, section)])
            pair, own = shared(pair_in[0]), pack_weights(own_weights)
            kernels = Kernels(place, used, n, my_rows, cols, channels, BLOCK_ROWS)
            state, homes = steps(
                kernels, crops, pair, shared(pair_cot[0]), own + tuple(swap(v) for v in own), functools.partial(early_sums, first, swap),
                functools.partial(late_share, first), other_half, meet,
            )
            total, _ = lax.optimization_barrier((state[-1]["total"], homes["grad"]))
            spec = pl.BlockSpec(memory_space=pltpu.VMEM)
            order = ("proj", "gate", "gain_in", "bias_in", "out", "gain_out", "bias_out", "gain_tr", "bias_tr", "up", "down")
            arrays = dict(
                gain_in=gain_in, bias_in=bias_in, proj=proj, gate=gate, out=out, gain_out=gain_out, bias_out=bias_out, gain_tr=gain_tr,
                bias_tr=bias_tr, up=up, down=down,
            )
            results = pl.pallas_call(
                k_results,
                out_shape=[jax.ShapeDtypeStruct(arrays[name].shape, F32) for name in order],
                in_specs=[spec],
                out_specs=[spec] * len(order),
                scratch_shapes=[pltpu.VMEM((s[0] * s[1], LANES), F32) for s in (share_shape(UP_ROWS), share_shape(LOW_ROWS))],
                compiler_params=pltpu.CompilerParams(vmem_limit_bytes=VMEM),
            )(total)
            results = dict(zip(order, results))
            return (homes["out"][None], homes["grad"][None]) + tuple(results[name] for name in ORDER)

        chunks = cols // LANES
        if chunks == 1:
            return run((1, 1))
        return lax.cond(lengths[1] <= before_last, lambda: run((chunks, chunks - 1)), lambda: run((chunks, chunks)))

    other_weights = {k: swap(v) for k, v in own_weights.items()}
    weights = [
        {k: jnp.where(first, own_weights[k], other_weights[k]) for k in ORDER},
        {k: jnp.where(first, other_weights[k], own_weights[k]) for k in ORDER},
    ]

    def both(value):
        own, got = pick(value, group), swap(pick(value, 1 - group))
        return jnp.where(first, own, got), jnp.where(first, got, own)

    def home(value_0, value_1):
        own, got = jnp.where(first, value_0, value_1), swap(jnp.where(first, value_1, value_0))
        return jnp.stack([jnp.where(first, own, got), jnp.where(first, got, own)])[None]

    out_0, out_1, grad_0, grad_1, grads_0, grads_1 = plain_steps(
        count, base, pick(crop_lengths, group), *both(pair_in[0]), *both(pair_cot[0]), weights
    )
    pair_out, pair_grad = home(out_0, out_1), home(grad_0, grad_1)
    mine = {k: jnp.where(first, grads_0[k], grads_1[k]) + swap(jnp.where(first, grads_1[k], grads_0[k])) for k in ORDER}
    summed = lax.psum(mine, "row")
    return (pair_out, pair_grad) + tuple(summed[k][None] for k in ORDER)


def solution(mesh):
    pair = P("grp", None, "row", None, None)
    vector, matrix = P("grp", None), P("grp", None, None)
    weights = (vector, vector, matrix, matrix, matrix, vector, vector, vector, vector, matrix, matrix)
    return jax.shard_map(
        per_device,
        mesh=mesh,
        in_specs=(pair, P()) + weights + (pair,),
        out_specs=(pair, pair) + weights,
        check_vma=False,
    )
```

```python
import functools

import jax
import jax.numpy as jnp
from jax import lax
from jax.experimental import pallas as pl
from jax.experimental.pallas import tpu as pltpu
from jax.sharding import PartitionSpec as P

EPSILON = 1e-05
F32 = jnp.float32
BF16 = jnp.bfloat16


def norm_stats(values):
    mean_value = jnp.mean(values, axis=-1, keepdims=True)
    centred = values - mean_value
    inv_scale = lax.rsqrt(jnp.mean(centred * centred, axis=-1, keepdims=True) + EPSILON)
    return (centred * inv_scale, inv_scale)


def norm_back(grad_scaled, scaled, inv_scale):
    mean_grad = jnp.mean(grad_scaled, axis=-1, keepdims=True)
    mean_cross = jnp.mean(grad_scaled * scaled, axis=-1, keepdims=True)
    return inv_scale * (grad_scaled - mean_grad - scaled * mean_cross)


def dot(a, b):
    return jnp.dot(a, b, preferred_element_type=F32)


def dot_t(a, b):
    return jnp.einsum("ijf,cf->ijc", a, b, preferred_element_type=F32)


def outer(a, b):
    return jnp.einsum("ijc,ijf->cf", a, b, preferred_element_type=F32)


def to_channels(value, n):
    rows, cols, channels = value.shape
    return jnp.transpose(value, (2, 0, 1)).reshape(n, channels // n, rows, cols)


def from_channels(value):
    n, held, rows, cols = value.shape
    return jnp.transpose(value.reshape(n * held, rows, cols), (1, 2, 0))


def swap_rows(value):
    return lax.all_to_all(value, "row", 0, 0)


def pre(state, mask, w):
    scaled, _ = norm_stats(state)
    normed = (scaled * w["gain_in"] + w["bias_in"]).astype(BF16)
    projected = dot(normed, w["proj"])
    width = projected.shape[-1] // 4
    lv, lg, rv, rg = (projected[..., i * width : (i + 1) * width] for i in range(4))
    left = (jax.nn.sigmoid(lg) * lv * mask).astype(BF16)
    right = (jax.nn.sigmoid(rg) * rv * mask).astype(BF16)
    return normed, left, right


def post(state, normed, mixed, w):
    gate_logit = dot(normed, w["gate"])
    scaled_mid, inv_mid = norm_stats(mixed)
    mixed_norm = (scaled_mid * w["gain_out"] + w["bias_out"]).astype(BF16)
    update = dot(mixed_norm, w["out"])
    gate_sigma = jax.nn.sigmoid(gate_logit)
    first_state = state + gate_sigma * update
    scaled_tr, inv_tr = norm_stats(first_state)
    trans_normed = (scaled_tr * w["gain_tr"] + w["bias_tr"]).astype(BF16)
    hidden = dot(trans_normed, w["up"])
    activated = jax.nn.silu(hidden).astype(BF16)
    result = (first_state + dot(activated, w["down"])).astype(BF16)
    saved = (gate_sigma, scaled_mid, inv_mid, mixed_norm, update, scaled_tr, inv_tr, trans_normed, hidden, activated)
    return result, saved


def back_upper(grad_final, saved, w):
    gate_sigma, scaled_mid, inv_mid, mixed_norm, update, scaled_tr, inv_tr, trans_normed, hidden, activated = saved
    grads = {}
    grad_trans = grad_final.astype(BF16)
    grads["down"] = outer(activated, grad_trans)
    grad_act = dot_t(grad_trans, w["down"])
    sigma = jax.nn.sigmoid(hidden)
    grad_hidden = (grad_act * sigma * (1.0 + hidden * (1.0 - sigma))).astype(BF16)
    grads["up"] = outer(trans_normed, grad_hidden)
    grad_tnorm = dot_t(grad_hidden, w["up"])
    grads["gain_tr"] = jnp.sum(grad_tnorm * scaled_tr, axis=(0, 1))
    grads["bias_tr"] = jnp.sum(grad_tnorm, axis=(0, 1))
    grad_result = grad_final + norm_back(grad_tnorm * w["gain_tr"], scaled_tr, inv_tr)
    grad_update = (grad_result * gate_sigma).astype(BF16)
    grad_gate = (grad_result * update * gate_sigma * (1.0 - gate_sigma)).astype(BF16)
    grads["out"] = outer(mixed_norm, grad_update)
    grad_norm_mid = dot_t(grad_update, w["out"])
    grads["gain_out"] = jnp.sum(grad_norm_mid * scaled_mid, axis=(0, 1))
    grads["bias_out"] = jnp.sum(grad_norm_mid, axis=(0, 1))
    grad_mixed = norm_back(grad_norm_mid * w["gain_out"], scaled_mid, inv_mid).astype(BF16)
    return grad_result, grad_gate, grad_mixed, grads


def back_lower(state, normed, mask, grad_result, grad_gate, grad_left, grad_right, w):
    scaled_in, inv_in = norm_stats(state)
    projected = dot(normed, w["proj"])
    width = projected.shape[-1] // 4
    lv, lg, rv, rg = (projected[..., i * width : (i + 1) * width] for i in range(4))
    ls = jax.nn.sigmoid(lg)
    rs = jax.nn.sigmoid(rg)
    gl = grad_left.astype(F32) * mask
    gr = grad_right.astype(F32) * mask
    grad_proj = jnp.concatenate(
        [gl * ls, gl * lv * ls * (1.0 - ls), gr * rs, gr * rv * rs * (1.0 - rs)], axis=-1
    ).astype(BF16)
    grads = {"proj": outer(normed, grad_proj), "gate": outer(normed, grad_gate)}
    grad_normed = dot_t(grad_proj, w["proj"]) + dot_t(grad_gate, w["gate"])
    grads["gain_in"] = jnp.sum(grad_normed * scaled_in, axis=(0, 1))
    grads["bias_in"] = jnp.sum(grad_normed, axis=(0, 1))
    return grad_result + norm_back(grad_normed * w["gain_in"], scaled_in, inv_in), grads


def product(left, right):
    n, held, rows, cols = left.shape
    mixed = jnp.einsum("atik,btjk->taibj", left, right, preferred_element_type=F32)
    return jnp.transpose(mixed.reshape(held, n, rows, n * rows), (1, 0, 2, 3)).astype(BF16)


def product_back(grad_mixed, left, right):
    n, held, rows, cols = left.shape
    split = grad_mixed.reshape(n, held, rows, n, rows)
    grad_left = jnp.einsum("atibj,btjk->atik", split, right, preferred_element_type=F32)
    grad_right = jnp.einsum("atibj,atik->btjk", split, left, preferred_element_type=F32)
    return grad_left.astype(BF16), grad_right.astype(BF16)


BLOCK_ROWS = 12
LANES = 128
VMEM = 63 << 20


def sig(x):
    return 0.5 * jnp.tanh(0.5 * x) + 0.5


def mm(a, b, ca=1, cb=0):
    return lax.dot_general(a, b, (((ca,), (cb,)), ((), ())), preferred_element_type=F32)


def col_stats(values):
    centred = values - jnp.mean(values, axis=0, keepdims=True)
    inv_scale = lax.rsqrt(jnp.mean(centred * centred, axis=0, keepdims=True) + EPSILON)
    return centred * inv_scale, inv_scale


def col_back(grad_scaled, scaled, inv_scale):
    mean_grad = jnp.mean(grad_scaled, axis=0, keepdims=True)
    mean_cross = jnp.mean(grad_scaled * scaled, axis=0, keepdims=True)
    return inv_scale * (grad_scaled - mean_grad - scaled * mean_cross)


def fold(values):
    return jnp.sum(values.reshape(values.shape[0] // 8, 8, values.shape[1]), axis=0)


class Step:
    def __init__(self, place, n, rows, held, block_rows, crop, last, used, chunks):
        self.last = last
        self.live = pl.program_id(0) < used if used < chunks else None
        self.n, self.rows, self.held, self.block = n, rows, held, block_rows
        self.row = pl.program_id(1) * block_rows
        self.length, self.base, self.group = place[crop], place[2], place[3]
        column = pl.program_id(0) * LANES + lax.broadcasted_iota(jnp.int32, (1, LANES), 1)
        self.columns = (column < self.length).astype(F32)

    def mask(self, r):
        return self.columns * jnp.where(self.base + self.row + r < self.length, 1.0, 0.0)

    def flat(self, ref):
        return ref[...].reshape(self.block * LANES, ref.shape[-1])

    def pick(self, pair, section):
        own, got = (self.flat(ref).astype(F32) for ref in pair)
        return jnp.where(jnp.full(own.shape, self.group) == section, own, got)

    def put(self, ref, value):
        ref[...] = value.reshape(self.block, LANES, value.shape[-1]).astype(ref.dtype)

    def lanes(self, r):
        return slice(r * LANES, (r + 1) * LANES)

    def spans(self, r):
        return [pl.ds((self.row + r) * self.held + t, self.n, stride=self.rows * self.held) for t in range(self.held)]

    def load(self, scratch, r):
        return jnp.concatenate([scratch[span, :] for span in self.spans(r)], axis=0)

    def store(self, scratch, r, value):
        for t, span in enumerate(self.spans(r)):
            scratch[span, :] = value[t * self.n : (t + 1) * self.n, :]


def unpack(ref, scratch, first=0):
    n, size = ref.shape[0], scratch.shape[0] // (ref.shape[0] + 1)

    def body(d, carry):
        scratch[pl.ds(pl.multiple_of(d * size, 8), size), :] = ref[d, first : first + size, :].astype(F32)
        return carry

    lax.fori_loop(0, n, body, 0)


def pack(scratch, ref, first=0):
    n, size = ref.shape[0], scratch.shape[0] // (ref.shape[0] + 1)

    def body(d, carry):
        ref[d, first : first + size, :] = scratch[pl.ds(pl.multiple_of(d * size, 8), size), :].astype(ref.dtype)
        return carry

    lax.fori_loop(0, n, body, 0)


def fetch(st, ref, scratch, first=0):
    if st.live is None:
        return unpack(ref, scratch, first)

    @pl.when(st.live)
    def _():
        unpack(ref, scratch, first)

    @pl.when(jnp.logical_not(st.live))
    def _():
        scratch[...] = jnp.zeros(scratch.shape, scratch.dtype)


def deliver(st, scratch, ref, first=0):
    if st.live is None:
        return pack(scratch, ref, first)
    pl.when(st.live)(lambda: pack(scratch, ref, first))


def at_first(action):
    pl.when(pl.program_id(1) == 0)(action)


def at_last(action):
    pl.when(pl.program_id(1) == pl.num_programs(1) - 1)(action)


def clear(accs, olds, cols=()):
    @pl.when((pl.program_id(0) == 0) & (pl.program_id(1) == 0))
    def _():
        for k, ref in enumerate(accs):
            ref[...] = olds[k][...] if olds else jnp.zeros(ref.shape, ref.dtype)
        for ref in cols:
            ref[...] = jnp.zeros(ref.shape, ref.dtype)


def add_blocks(ref, first, value):
    for q in range(value.shape[1] // LANES):
        ref[first + q * LANES : first + (q + 1) * LANES, :] += value[:, q * LANES : (q + 1) * LANES]


def close(st, ref, cols=None):
    @pl.when((pl.program_id(0) == pl.num_programs(0) - 1) & (pl.program_id(1) == pl.num_programs(1) - 1))
    def _():
        for k in range(2 if cols is not None else 0):
            row = UP_VEC + 16 + 8 * k
            ref[row : row + 1, :] += jnp.sum(jnp.transpose(cols[k]), axis=0, keepdims=True)
        for q in range(4 if st.last else 0):
            block = slice(q * LANES, (q + 1) * LANES)
            ref[block, :] = jnp.transpose(ref[block, :])


def pre_part(st, state, w, normed_ref, left_scr, right_scr):
    scaled, _ = norm_stats(state)
    normed = (scaled * w.vec[0:1, :] + w.vec[1:2, :]).astype(BF16)
    st.put(normed_ref, normed)
    projected = mm(w.proj_t[...], normed, 1, 1)
    for r in range(st.block):
        lv, lg, rv, rg = (projected[q * LANES : (q + 1) * LANES, st.lanes(r)] for q in range(4))
        mask = st.mask(r)
        st.store(left_scr, r, sig(lg) * lv * mask)
        st.store(right_scr, r, sig(rg) * rv * mask)


def post_part(st, state, normed, mixed_scr, w):
    mids = [col_stats(st.load(mixed_scr, r)) for r in range(st.block)]
    gain, bias = w.col[0], w.col[1]
    mixed_norm = jnp.concatenate([(scaled * gain + bias).astype(BF16) for scaled, _ in mids], axis=1)
    update = mm(mixed_norm, w.out[...], 0, 0)
    gate = sig(mm(normed, w.gate[...]))
    first_state = state + gate * update
    scaled_tr, inv_tr = norm_stats(first_state)
    trans = (scaled_tr * w.vec[2:3, :] + w.vec[3:4, :]).astype(BF16)
    hidden = mm(trans, w.up[...])
    sigma = sig(hidden)
    activated = (hidden * sigma).astype(BF16)
    return mids, mixed_norm, update, gate, first_state, scaled_tr, inv_tr, trans, hidden, sigma, activated


def upper_part(st, grad_final, kept, w, acc, cols, grad_ref, gate_ref, mixed_scr):
    mids, mixed_norm, update, gate, first_state, scaled_tr, inv_tr, trans, hidden, sigma, activated = kept
    low = grad_final.astype(BF16)
    add_blocks(acc, 0, mm(low, activated, 0, 0))
    grad_hidden = (mm(low, w.down[...], 1, 1) * (sigma * (1.0 + hidden * (1.0 - sigma)))).astype(BF16)
    add_blocks(acc, 4 * LANES, mm(trans, grad_hidden, 0, 0))
    grad_tnorm = mm(grad_hidden, w.up[...], 1, 1)
    acc[UP_VEC : UP_VEC + 8, :] += fold(grad_tnorm * scaled_tr)
    acc[UP_VEC + 8 : UP_VEC + 16, :] += fold(grad_tnorm)
    grad_result = grad_final + norm_back(grad_tnorm * w.vec[2:3, :], scaled_tr, inv_tr)
    st.put(grad_ref, grad_result)
    scaled_grad = grad_result * gate
    grad_update = scaled_grad.astype(BF16)
    st.put(gate_ref, scaled_grad * update * (1.0 - gate))
    add_blocks(acc, 8 * LANES, mm(mixed_norm, grad_update))
    grad_norm = mm(w.out[...], grad_update, 1, 1)
    for r, (scaled, inv_scale) in enumerate(mids):
        grad = grad_norm[:, st.lanes(r)]
        cols[0] += grad * scaled
        cols[1] += grad
        st.store(mixed_scr, r, col_back(grad * w.col[0], scaled, inv_scale) * st.mask(r))


def lower_part(st, state, normed, grad_result, grad_gate, left_scr, right_scr, w, acc):
    projected = mm(w.proj_t[...], normed, 1, 1)
    parts = []
    for r in range(st.block):
        lv, lg, rv, rg = (projected[q * LANES : (q + 1) * LANES, st.lanes(r)] for q in range(4))
        ls, rs = sig(lg), sig(rg)
        a, b = st.load(left_scr, r) * ls, st.load(right_scr, r) * rs
        parts.append(jnp.concatenate([v.astype(BF16) for v in (a, a * lv * (1.0 - ls), b, b * rv * (1.0 - rs))], axis=0))
    grad_proj = jnp.concatenate(parts, axis=1)
    acc[: 4 * LANES, :] += mm(grad_proj, normed)
    add_blocks(acc, 4 * LANES, mm(normed, grad_gate, 0, 0))
    grad_normed = jnp.transpose(mm(w.proj[...], grad_proj)) + mm(grad_gate, w.gate[...], 1, 1)
    scaled_in, inv_in = norm_stats(state)
    acc[LOW_VEC : LOW_VEC + 8, :] += fold(grad_normed * scaled_in)
    acc[LOW_VEC + 8 : LOW_VEC + 16, :] += fold(grad_normed)
    return grad_result + norm_back(grad_normed * w.vec[0:1, :], scaled_in, inv_in)


class Weights:
    def __init__(self, group, section, refs, scratch):
        self.wide, self.down, self.vec, self.col, self.proj_t = scratch
        cut = lambda first, count: self.wide.at[:, first * LANES : (first + count) * LANES]
        self.proj, self.gate, self.out, self.up = cut(0, 4), cut(4, 1), cut(5, 1), cut(6, 4)

        @pl.when((pl.program_id(0) == 0) & (pl.program_id(1) == 0))
        def _():
            for chosen, sources in ((group == section, refs[:3]), (group != section, refs[3:])):

                @pl.when(chosen)
                def _():
                    for ref, source in zip((self.wide, self.down, self.vec), sources):
                        ref[...] = source[...]

            for k in range(2):
                self.col[k] = jnp.transpose(jnp.broadcast_to(self.vec[4 + k : 5 + k, :], (LANES, LANES)))
            for q in range(4):
                block = slice(q * LANES, (q + 1) * LANES)
                self.proj_t[block, :] = jnp.transpose(self.wide[:, block])

    @staticmethod
    def scratch():
        return [
            pltpu.VMEM((LANES, 10 * LANES), BF16), pltpu.VMEM((4 * LANES, LANES), BF16), pltpu.VMEM((8, LANES), F32),
            pltpu.VMEM((2, LANES, LANES), F32), pltpu.VMEM((4 * LANES, LANES), BF16),
        ]


def pack_weights(w):
    zero = jnp.zeros_like(w["gain_in"])
    names = ("gain_in", "bias_in", "gain_tr", "bias_tr", "gain_out", "bias_out")
    wide = jnp.concatenate([w[name] for name in ("proj", "gate", "out", "up")], axis=1)
    return wide, w["down"], jnp.stack([w[name] for name in names] + [zero, zero])


UP_VEC = 9 * LANES
UP_ROWS = UP_VEC + 32
LOW_VEC = 5 * LANES
LOW_ROWS = LOW_VEC + 16


def k_pre(cfg, place, own, got, *refs):
    st = Step(place, *cfg)
    w = Weights(st.group, 0, refs[:6], refs[-5:])
    normed, both, left, right = refs[6:-5]
    pre_part(st, st.pick((own, got), 0), w, normed, left, right)

    @at_last
    def _():
        deliver(st, left, both)
        deliver(st, right, both, both.shape[1] // 2)


def k_post_pre(cfg, place, own_0, got_0, own_1, got_1, normed_in, mixed_in, *refs):
    st = Step(place, *cfg)
    w0, w1 = Weights(st.group, 0, refs[:6], refs[-10:-5]), Weights(st.group, 1, refs[:6], refs[-5:])
    *_, home, out, normed, both, mixed, left, right = refs[6:-10]
    at_first(lambda: fetch(st, mixed_in, mixed))
    kept = post_part(st, st.pick((own_0, got_0), 0), st.flat(normed_in), mixed, w0)
    result = (kept[4] + mm(kept[-1], w0.down[...])).astype(BF16)
    st.put(home, result)
    st.put(out, result)
    pre_part(st, result.astype(F32) + st.pick((own_1, got_1), 1), w1, normed, left, right)

    @at_last
    def _():
        deliver(st, left, both)
        deliver(st, right, both, both.shape[1] // 2)


def k_post_upper(cfg, place, own, got, own_cot, got_cot, before, normed_in, mixed_in, *refs):
    st = Step(place, *cfg)
    w = Weights(st.group, 1, refs[:6], refs[-5:])
    _, *olds, home, out, grad, gate, grad_mixed, sums, mixed, cols = refs[6:-5]
    clear([sums], olds, [cols])
    at_first(lambda: fetch(st, mixed_in, mixed))
    state = st.flat(before).astype(F32) + st.pick((own, got), 1)
    kept = post_part(st, state, st.flat(normed_in), mixed, w)
    result = kept[4] + mm(kept[-1], w.down[...])
    st.put(home, result)
    st.put(out, result)
    upper_part(st, st.pick((own_cot, got_cot), 1), kept, w, sums, cols, grad, gate, mixed)
    close(st, sums, cols)
    at_last(lambda: deliver(st, mixed, grad_mixed))


def k_lower_upper(
    cfg, place, own_1, got_1, own_0, got_0, own_cot, got_cot, before, normed_1, grad_1, gate_1, normed_0, both, mixed_in, *refs
):
    st = Step(place, *cfg)
    w1, w0 = Weights(st.group, 1, refs[:6], refs[-10:-5]), Weights(st.group, 0, refs[:6], refs[-5:])
    olds = refs[7:9] if cfg[4] else ()
    home, pair_grad, grad, gate, grad_mixed, low_sums, up_sums, left, right, mixed, cols = refs[-21:-10]
    clear([low_sums, up_sums], olds, [cols])

    @at_first
    def _():
        fetch(st, both, left)
        fetch(st, both, right, both.shape[1] // 2)
        fetch(st, mixed_in, mixed)

    state = st.flat(before).astype(F32) + st.pick((own_1, got_1), 1)
    grad_state = lower_part(
        st, state, st.flat(normed_1), st.flat(grad_1), st.flat(gate_1), left, right, w1, low_sums
    )
    st.put(home, grad_state)
    st.put(pair_grad, grad_state)
    kept = post_part(st, st.pick((own_0, got_0), 0), st.flat(normed_0), mixed, w0)
    grad_final = st.pick((own_cot, got_cot), 0) + grad_state.astype(BF16).astype(F32)
    upper_part(st, grad_final, kept, w0, up_sums, cols, grad, gate, mixed)
    close(st, low_sums)
    close(st, up_sums, cols)
    at_last(lambda: deliver(st, mixed, grad_mixed))


def k_lower(cfg, place, own, got, normed, grad, gate, both, *refs):
    st = Step(place, *cfg)
    w = Weights(st.group, 0, refs[:6], refs[-5:])
    _, *olds, home, pair_grad, sums, parts, left, right = refs[6:-5]
    clear([sums], olds)

    @at_first
    def _():
        fetch(st, both, left)
        fetch(st, both, right, both.shape[1] // 2)

    state = st.pick((own, got), 0)
    grad_state = lower_part(
        st, state, st.flat(normed), st.flat(grad), st.flat(gate), left, right, w, sums
    )
    st.put(home, grad_state)
    st.put(pair_grad, grad_state)
    close(st, sums)

    @pl.when((pl.program_id(0) == pl.num_programs(0) - 1) & (pl.program_id(1) == pl.num_programs(1) - 1))
    def _():
        n, rows, _ = parts.shape
        parts[...] = jnp.zeros(parts.shape, BF16)
        for d in range(n):
            count = max(0, min(rows, LOW_ROWS - d * rows))
            if count:
                parts[d, :count, :] = sums[d * rows : d * rows + count, :].astype(BF16)


def k_results(total, proj, gate, gain_in, bias_in, out, gain_out, bias_out, gain_tr, bias_tr, up, down, early, low):
    n = total.shape[0]
    first, second = early.shape[0] // n, low.shape[0] // n
    for d in range(n):
        early[d * first : (d + 1) * first, :] = total[d, :first, :].astype(F32)
        low[d * second : (d + 1) * second, :] = total[d, first:, :].astype(F32)
    down[0] = early[: 4 * LANES, :]
    for q in range(4):
        up[0, :, q * LANES : (q + 1) * LANES] = early[(4 + q) * LANES : (5 + q) * LANES, :]
        proj[0, :, q * LANES : (q + 1) * LANES] = low[q * LANES : (q + 1) * LANES, :]
    out[0] = early[8 * LANES : UP_VEC, :]
    gate[0] = low[4 * LANES : LOW_VEC, :]
    for k, ref in enumerate((gain_tr, bias_tr, gain_out, bias_out)):
        ref[...] = jnp.sum(early[UP_VEC + 8 * k : UP_VEC + 8 * k + 8, :], axis=0, keepdims=True)
    for k, ref in enumerate((gain_in, bias_in)):
        ref[...] = jnp.sum(low[LOW_VEC + 8 * k : LOW_VEC + 8 * k + 8, :], axis=0, keepdims=True)


def spread(ref, scratch, first=0):
    n, size = ref.shape[0], (scratch.shape[1] - 8) // ref.shape[0]

    def body(d, carry):
        for c in range(scratch.shape[0]):
            value = ref[d, first : first + size, c * LANES : (c + 1) * LANES]
            scratch[c, pl.ds(pl.multiple_of(d * size, 8), size), :] = value.astype(F32)
        return carry

    lax.fori_loop(0, n, body, 0)


def gather(scratch, ref, first=0):
    n, size = ref.shape[0], (scratch.shape[1] - 8) // ref.shape[0]

    def body(d, carry):
        for c in range(scratch.shape[0]):
            value = scratch[c, pl.ds(pl.multiple_of(d * size, 8), size), :]
            ref[d, first : first + size, c * LANES : (c + 1) * LANES] = value.astype(ref.dtype)
        return carry

    lax.fori_loop(0, n, body, 0)


def channel(scratch, t, held):
    chunks, size, _ = scratch.shape
    span = pl.ds(t, (size - 8) // held, stride=held)
    return jnp.concatenate([scratch[c, span, :].astype(BF16) for c in range(chunks)], axis=1)


def put_channel(scratch, t, held, value):
    chunks, size, _ = scratch.shape
    span = pl.ds(t, (size - 8) // held, stride=held)
    for c in range(chunks):
        scratch[c, span, :] = value[:, c * LANES : (c + 1) * LANES]


def k_product(held, both, out, left, right):
    spread(both, left)
    spread(both, right, both.shape[1] // 2)

    def body(t, carry):
        others = channel(right, t, held)[: left.shape[0] * LANES]
        put_channel(left, t, held, mm(channel(left, t, held), others, 1, 1))
        return carry

    lax.fori_loop(0, held, body, 0)
    gather(left, out)


def k_product_back(held, grad_in, both, out, grad, left, right):
    spread(grad_in, grad)
    spread(both, left)
    spread(both, right, both.shape[1] // 2)

    def body(t, carry):
        low, lv, rv = channel(grad, t, held), channel(left, t, held), channel(right, t, held)
        put_channel(left, t, held, mm(low, rv[: low.shape[1]]))
        grad_right = mm(low, lv, 0, 0)
        if low.shape[1] < rv.shape[0]:
            rest = jnp.zeros((rv.shape[0] - low.shape[1], lv.shape[1]), F32)
            grad_right = jnp.concatenate([grad_right, rest])
        put_channel(right, t, held, grad_right)
        return carry

    lax.fori_loop(0, held, body, 0)
    gather(left, out)
    gather(right, out, both.shape[1] // 2)


STEPS = """\
1A SA0 1B SB0 TA0 MA0 TB0 MB0 2A SA1 2B SB1 TA1 MA1 TB1 MB1 3A GA1 3B GB1 tA1 sA1 tB1 sB1 HA HB 4A GA0 4B GB0 tA0 sA0 tB0 sB0 EB0 QB0 5A JA 5B qB0 JB AB0
"""


class Kernels:
    def __init__(self, place, used, n, rows, cols, channels, block_rows):
        self.place, self.used, self.crops = place, used, len(used)
        self.n, self.rows, self.cols, self.channels, self.block = n, rows, cols, channels, block_rows
        self.held = channels // n
        self.size = rows * self.held
        self.chunks = cols // LANES

    def row_call(self, body, crop, ins, outs, scratch, micros, cols=0, sections=1):
        rows, block = self.rows, self.block

        def spec(kind, shape):
            if kind == "own":
                return pl.BlockSpec(
                    (pl.squeezed, block, LANES, shape[-1]), lambda c, i, s: (s[4 + crop], s[3] * (rows // block) + i, c, 0)
                )
            if kind in ("home 0", "home 1"):
                first = int(kind[-1]) * (rows // block)
                return pl.BlockSpec((pl.squeezed, block, LANES, shape[-1]), lambda c, i, s: (s[4 + crop], first + i, c, 0))
            if kind == "rows":
                return pl.BlockSpec((block, LANES, shape[-1]), lambda c, i, s: (i, c, 0))
            if kind == "moved":
                final = shape[-1] // LANES - 1
                return pl.BlockSpec(shape[:-1] + (LANES,), lambda c, i, s: (0, 0, jnp.minimum(c, final)))
            if kind == "kept":
                return pl.BlockSpec(memory_space=pl.ANY)
            zeros = (0,) * len(shape)
            return pl.BlockSpec(shape, lambda c, i, s: zeros)

        aliases = {1 + k: 0 for k, (kind, _) in enumerate(ins) if kind == "kept"}
        return pl.pallas_call(
            functools.partial(
                body, (self.n, rows, self.held, block, crop, crop == self.crops - 1, self.used[crop], self.chunks)
            ),
            out_shape=tuple(v for _, v in outs),
            grid_spec=pltpu.PrefetchScalarGridSpec(
                num_scalar_prefetch=1,
                grid=(self.chunks, rows // block),
                in_specs=[spec(k, v.shape) for k, v in ins],
                out_specs=tuple(spec(k, v.shape) for k, v in outs),
                scratch_shapes=[pltpu.VMEM(((self.n + 1) * self.size, LANES), F32)] * scratch
                + [pltpu.VMEM((2, self.channels, LANES), F32)] * cols
                + Weights.scratch() * sections,
            ),
            input_output_aliases=aliases,
            compiler_params=pltpu.CompilerParams(vmem_limit_bytes=VMEM),
            cost_estimate=cost(micros),
        )(self.place, *[v for _, v in ins])

    def home(self, section, dtype):
        return (f"home {section}", jax.ShapeDtypeStruct((self.crops, 2 * self.rows, self.cols, self.channels), dtype))

    def pairs(self, dtype):
        return ("rows", jax.ShapeDtypeStruct((self.rows, self.cols, self.channels), dtype))

    def moved(self, crop, count=1):
        return ("moved", jax.ShapeDtypeStruct((self.n, count * self.size, self.used[crop] * LANES), BF16))

    def sums(self, rows):
        return ("all", jax.ShapeDtypeStruct((rows, self.channels), F32))

    def channel_call(self, body, ins, out, scratch, micros):
        spec = pl.BlockSpec(memory_space=pltpu.VMEM)
        return pl.pallas_call(
            functools.partial(body, self.held),
            out_shape=out[1],
            in_specs=[spec] * len(ins),
            out_specs=spec,
            scratch_shapes=[pltpu.VMEM((out[1].shape[2] // LANES, self.n * self.size + 8, LANES), F32)] * scratch,
            compiler_params=pltpu.CompilerParams(vmem_limit_bytes=VMEM),
            cost_estimate=cost(micros),
        )(*ins)


def cost(micros):
    return pl.CostEstimate(flops=int(micros * 1.15e9), bytes_accessed=int(micros * 1e6), transcendentals=0)


def steps(kernels, crops, pair, cot, weights, early, late_share, other_half, meet):
    w = [("all", v) for v in weights]
    call, pairs, moved = kernels.row_call, kernels.pairs, kernels.moved
    up_sums, low_sums = kernels.sums(UP_ROWS), kernels.sums(LOW_ROWS)
    earlier = lambda *names: [("all", state[0][name]) for name in names if name in state[0]]
    homes = {}
    kept = lambda name: [("kept", homes[name])]
    mine = lambda v, crop: [("own", v[0]), ("rows", v[1][crop])]
    part = lambda *vs: [("rows", v) for v in vs]
    far = lambda *vs: [("moved", v) for v in vs]
    swap = lambda v: lax.all_to_all(v, ("row", "grp"), 0, 0)
    spread_rows = lambda v: lax.all_to_all(v, "row", 0, 0)
    state = [dict() for _ in range(crops)]
    last = {}

    def ordered(kind, op, value):
        if kind in last:
            value, _ = lax.optimization_barrier((value, last[kind]))
        result = op(value)
        last[kind] = result[0] if isinstance(result, (tuple, list)) else result
        return result

    def row_kernel(body, crop, ins, *rest):
        return ordered("kernel", lambda v: call(body, crop, [(ins[0][0], v)] + ins[1:], *rest), ins[0][1])

    def channel_kernel(body, ins, *rest):
        return ordered("kernel", lambda v: kernels.channel_call(body, (v,) + tuple(ins[1:]), *rest), ins[0])

    def pre(crop, s):
        s["normed_0"], s["both_0"] = row_kernel(k_pre, crop, mine(pair, crop) + w, [pairs(BF16), moved(crop, 2)], 2, 10)

    def post_pre(crop, s):
        homes["out"], s["out_0"], s["normed_1"], s["both_1"] = row_kernel(
            k_post_pre, crop,
            mine(pair, crop) + mine(pair, crop) + part(s["normed_0"]) + far(s["mixed_0"]) + w + (kept("out") if crop else []),
            [kernels.home(0, BF16), pairs(BF16), pairs(BF16), moved(crop, 2)], 3, 18, 0, 2,
        )
        s["got_out_0"] = other_half(s["out_0"], 0)

    def post_upper(crop, s):
        homes["out"], s["out_1"], s["grad_1"], s["gate_1"], s["grad_mixed_1"], s["up_1"] = row_kernel(
            k_post_upper, crop,
            mine(pair, crop) + mine(cot, crop) + part(s["out_0"], s["normed_1"]) + far(s["mixed_1"]) + w + kept("out")
            + earlier("up_1"),
            [kernels.home(1, BF16), pairs(BF16), pairs(F32), pairs(BF16), moved(crop), up_sums], 1, 23, 1,
        )
        s["got_out_1"] = other_half(s["out_1"], 1)

    def lower_upper(crop, s):
        homes["grad"], s["pair_grad_1"], s["grad_0"], s["gate_0"], s["grad_mixed_0"], s["low_1"], s["up_0"] = row_kernel(
            k_lower_upper, crop,
            mine(pair, crop) + mine(pair, crop) + mine(cot, crop)
            + part(s["out_0"], s["normed_1"], s["grad_1"], s["gate_1"], s["normed_0"])
            + far(s["back_1"], s["mixed_0"]) + w + (kept("grad") if crop else []) + earlier("low_1", "up_0"),
            [kernels.home(1, F32), pairs(F32), pairs(F32), pairs(BF16), moved(crop), low_sums, up_sums], 3, 31, 1, 2,
        )
        s["got_grad_1"] = other_half(s["pair_grad_1"], 1)

    def lower(crop, s):
        homes["grad"], s["pair_grad_0"], s["low_0"], s["late"] = row_kernel(
            k_lower, crop, mine(pair, crop) + part(s["normed_0"], s["grad_0"], s["gate_0"]) + far(s["back_0"]) + w
            + kept("grad") + earlier("low_0"),
            [kernels.home(0, F32), pairs(F32), low_sums, ("all", jax.ShapeDtypeStruct(share_shape(LOW_ROWS), BF16))], 2, 13,
        )
        s["got_grad_0"] = other_half(s["pair_grad_0"], 0)

    def product(crop, s, k):
        s[f"product_{k}"] = channel_kernel(k_product, (s[f"factors_{k}"],), moved(crop), 2, 6)

    def product_back(crop, s, k):
        s[f"grads_{k}"] = channel_kernel(k_product_back, (s[f"g_{k}"], s[f"factors_{k}"]), moved(crop, 2), 3, 12)

    transfers = dict(S=("factors", "both"), M=("mixed", "product"), G=("g", "grad_mixed"), s=("back", "grads"))
    rows_of = {"1": pre, "2": post_pre, "3": post_upper, "4": lower_upper, "5": lower}
    channels_of = {"T": product, "t": product_back}
    for step in STEPS.split():
        what, crop, k = step[0], "AB".index(step[1]), step[2:]
        s = state[crop]
        if what == "E":
            sums = {name: lax.optimization_barrier((s[name], last["kernel"]))[0] for name in ("up_0", "up_1", "low_1")}
            last["kernel"] = s["early"] = early(sums)
        elif what in "QqA":
            if what == "A":
                s["total"] = ordered("swap", spread_rows, late_share(s["share_q"], s["share_Q"]))
            else:
                moved_parts = ordered("swap", spread_rows, s["early" if what == "Q" else "late"])
                s[f"share_{what}"] = jnp.sum(moved_parts.astype(F32), axis=0)
        elif what in "HJ":
            name = "out" if what == "H" else "grad"
            homes[name] = meet(homes[name], crop, s[f"got_{name}_0"], s[f"got_{name}_1"])
            if what == "H":
                last["kernel"] = homes[name]
        elif what in rows_of:
            rows_of[what](crop, s)
        elif what in channels_of:
            channels_of[what](crop, s, k)
        else:
            new, old = transfers[what]
            s[f"{new}_{k}"] = ordered("swap", swap, s[f"{old}_{k}"])

    return state, homes


def share_shape(rows):
    n = lax.axis_size("row")
    return (n, -(-rows // (16 * n)) * 16, LANES)


def in_shares(sums):
    n, rows, _ = share_shape(sums.shape[0])
    return jnp.pad(sums, ((0, n * rows - sums.shape[0]), (0, 0))).reshape(n, rows, LANES)


def early_sums(first, swap, sums):
    early_0 = jnp.concatenate([sums["up_0"], jnp.zeros((LOW_ROWS, LANES), F32)])
    early_1 = jnp.concatenate([sums["up_1"], sums["low_1"]])
    early = jnp.where(first, early_0, early_1) + swap(jnp.where(first, early_1, early_0))
    return jnp.concatenate([in_shares(early[:UP_ROWS]), in_shares(early[UP_ROWS:])], axis=1).astype(BF16)


def late_share(first, late, early):
    late = jnp.where(first, late, 0.0) + lax.ppermute(late, "grp", [(1, 0)])
    rows = early.shape[0] - late.shape[0]
    share = jnp.concatenate([early[:rows], early[rows:] + late]).astype(BF16)
    return jnp.broadcast_to(share[None], (lax.axis_size("row"),) + share.shape)


def plain_steps(n, base, crop_length, pair_0, pair_1, cot_0, cot_1, weights):
    rows, cols = pair_0.shape[:2]
    own_rows = base + jnp.arange(rows)
    mask = (own_rows < crop_length).astype(F32)[:, None, None] * (jnp.arange(cols) < crop_length).astype(F32)[None, :, None]

    def send(*values):
        return swap_rows(jnp.stack([to_channels(v, n) for v in values], axis=1))

    w0, w1 = weights
    state_0 = pair_0.astype(F32)
    normed_0, left, right = pre(state_0, mask, w0)
    lr_0 = send(left, right)
    mixed_0 = from_channels(swap_rows(product(lr_0[:, 0], lr_0[:, 1]))).astype(F32)
    out_0, saved_0 = post(state_0, normed_0, mixed_0, w0)
    state_1 = out_0.astype(F32) + pair_1.astype(F32)
    normed_1, left, right = pre(state_1, mask, w1)
    lr_1 = send(left, right)
    mixed_1 = from_channels(swap_rows(product(lr_1[:, 0], lr_1[:, 1]))).astype(F32)
    out_1, saved_1 = post(state_1, normed_1, mixed_1, w1)
    grad_result, grad_gate, grad_mixed, upper_1 = back_upper(cot_1.astype(F32), saved_1, w1)
    gm = send(grad_mixed)
    glr = swap_rows(jnp.stack(product_back(gm[:, 0], lr_1[:, 0], lr_1[:, 1]), axis=1))
    grad_1, lower_1 = back_lower(
        state_1, normed_1, mask, grad_result, grad_gate, from_channels(glr[:, 0]), from_channels(glr[:, 1]), w1
    )
    grad_final = cot_0.astype(F32) + grad_1.astype(BF16).astype(F32)
    grad_result, grad_gate, grad_mixed, upper_0 = back_upper(grad_final, saved_0, w0)
    gm = send(grad_mixed)
    glr = swap_rows(jnp.stack(product_back(gm[:, 0], lr_0[:, 0], lr_0[:, 1]), axis=1))
    grad_0, lower_0 = back_lower(
        state_0, normed_0, mask, grad_result, grad_gate, from_channels(glr[:, 0]), from_channels(glr[:, 1]), w0
    )
    return out_0, out_1, grad_0, grad_1, {**upper_0, **lower_0}, {**upper_1, **lower_1}


ORDER = ("gain_in", "bias_in", "proj", "gate", "out", "gain_out", "bias_out", "gain_tr", "bias_tr", "up", "down")


def per_device(pair_in, crop_lengths, gain_in, bias_in, proj, gate, out, gain_out, bias_out, gain_tr, bias_tr, up, down, pair_cot):
    own_weights = dict(
        gain_in=gain_in[0], bias_in=bias_in[0], proj=proj[0], gate=gate[0], out=out[0], gain_out=gain_out[0],
        bias_out=bias_out[0], gain_tr=gain_tr[0], bias_tr=bias_tr[0], up=up[0], down=down[0],
    )
    groups, count = lax.axis_size("grp"), lax.axis_size("row")
    crops, rows, cols, channels = pair_in.shape[1:]
    group = lax.axis_index("grp")
    first = group == 0
    base = lax.axis_index("row") * rows
    swap = lambda v: lax.ppermute(v, "grp", [(0, 1), (1, 0)])
    pick = lambda v, i: lax.dynamic_index_in_dim(v, i, 0, keepdims=False)
    n = groups * count
    my_rows = rows // 2
    sizes = channels == LANES and out.shape[1] == LANES and up.shape[2] == 4 * LANES and crops == 2 and groups == 2
    if sizes and rows % 2 == 0 and my_rows % BLOCK_ROWS == 0 and cols % LANES == 0 and channels % n == 0 and n % 8 == 0 and (my_rows * (channels // n)) % 16 == 0:
        before_last = (cols // LANES - 1) * LANES
        swapped = crop_lengths[0] <= before_last
        which = [jnp.where(swapped, 1, 0), jnp.where(swapped, 0, 1)]
        lengths = [crop_lengths[crop] for crop in which]
        place = jnp.stack(lengths + [base + group * my_rows, group] + which).astype(jnp.int32)
        def shared(value):
            got, source = [], value
            for crop in which:
                got.append(swap(lax.dynamic_slice(source, (crop, (1 - group) * my_rows, 0, 0), (1, my_rows, cols, channels))[0]))
                source, _ = lax.optimization_barrier((value, got[-1]))
            return value, got

        def meet(home, crop, got_0, got_1):
            half = jnp.where(first, got_0, got_1)[None]
            return lax.dynamic_update_slice(home, half, (which[crop], (1 - group) * my_rows, 0, 0))

        def run(used):
            other_half = lambda value, section: lax.ppermute(value, "grp", [(1 - section, section)])
            pair, own = shared(pair_in[0]), pack_weights(own_weights)
            kernels = Kernels(place, used, n, my_rows, cols, channels, BLOCK_ROWS)
            state, homes = steps(
                kernels, crops, pair, shared(pair_cot[0]), own + tuple(swap(v) for v in own), functools.partial(early_sums, first, swap),
                functools.partial(late_share, first), other_half, meet,
            )
            total, _ = lax.optimization_barrier((state[-1]["total"], homes["grad"]))
            spec = pl.BlockSpec(memory_space=pltpu.VMEM)
            order = ("proj", "gate", "gain_in", "bias_in", "out", "gain_out", "bias_out", "gain_tr", "bias_tr", "up", "down")
            arrays = dict(
                gain_in=gain_in, bias_in=bias_in, proj=proj, gate=gate, out=out, gain_out=gain_out, bias_out=bias_out, gain_tr=gain_tr,
                bias_tr=bias_tr, up=up, down=down,
            )
            results = pl.pallas_call(
                k_results,
                out_shape=[jax.ShapeDtypeStruct(arrays[name].shape, F32) for name in order],
                in_specs=[spec],
                out_specs=[spec] * len(order),
                scratch_shapes=[pltpu.VMEM((s[0] * s[1], LANES), F32) for s in (share_shape(UP_ROWS), share_shape(LOW_ROWS))],
                compiler_params=pltpu.CompilerParams(vmem_limit_bytes=VMEM),
            )(total)
            results = dict(zip(order, results))
            return (homes["out"][None], homes["grad"][None]) + tuple(results[name] for name in ORDER)

        chunks = cols // LANES
        return run((chunks, chunks))

    other_weights = {k: swap(v) for k, v in own_weights.items()}
    weights = [
        {k: jnp.where(first, own_weights[k], other_weights[k]) for k in ORDER},
        {k: jnp.where(first, other_weights[k], own_weights[k]) for k in ORDER},
    ]

    def both(value):
        own, got = pick(value, group), swap(pick(value, 1 - group))
        return jnp.where(first, own, got), jnp.where(first, got, own)

    def home(value_0, value_1):
        own, got = jnp.where(first, value_0, value_1), swap(jnp.where(first, value_1, value_0))
        return jnp.stack([jnp.where(first, own, got), jnp.where(first, got, own)])[None]

    out_0, out_1, grad_0, grad_1, grads_0, grads_1 = plain_steps(
        count, base, pick(crop_lengths, group), *both(pair_in[0]), *both(pair_cot[0]), weights
    )
    pair_out, pair_grad = home(out_0, out_1), home(grad_0, grad_1)
    mine = {k: jnp.where(first, grads_0[k], grads_1[k]) + swap(jnp.where(first, grads_1[k], grads_0[k])) for k in ORDER}
    summed = lax.psum(mine, "row")
    return (pair_out, pair_grad) + tuple(summed[k][None] for k in ORDER)


def solution(mesh):
    pair = P("grp", None, "row", None, None)
    vector, matrix = P("grp", None), P("grp", None, None)
    weights = (vector, vector, matrix, matrix, matrix, vector, vector, vector, vector, matrix, matrix)
    return jax.shard_map(
        per_device,
        mesh=mesh,
        in_specs=(pair, P()) + weights + (pair,),
        out_specs=(pair, pair) + weights,
        check_vma=False,
    )
```
